128 devices in a mesh: section: 8 (over z, core), tensor: 16 (over y, x).
Axes of the slice: x: 4, y: 4, z: 4, core: 2. Of those that a mesh axis runs over, the one named last changes fastest.
Arguments:
- attn_logits: bfloat16 [8, 64, 96, 96], P('section', 'tensor'), may hold values from -7.5 to 256
- out_weight: bfloat16 [8, 8192, 5120], P('section', 'tensor'), may hold values from -0.0625 to 0.0625
- value_weight: bfloat16 [8, 1024, 5120], P('section', 'tensor'), may hold values from -0.078125 to 0.078125
- norm_gain: float32 [8, 5120], P('section'), may hold values from 0.1 to 1.9
- norm_scale: float32 [8, 96], P('section', 'tensor'), may hold values from 0.5 to 2
- target_encoder: bfloat16 [16384, 5120], P(None, ('section', 'tensor')), may hold values from -6 to 6
- target_ids: int32 [2], replicated, may hold values from 0 to 16383
- target_token: int32 [2], replicated, may hold values from 48 to 95, as said below
- decoder: bfloat16 [8, 16384, 5120], P('section', 'tensor'), may hold values from -0.078125 to 0.078125
- source_ids: int32 [8, 96, 128], P('section'), may hold values from 0 to 16383, all different within a row
- source_values: float32 [8, 96, 128], P('section'), may hold values from 0.05 to 0.6
Outputs:
- edges: float32 [8, 96, 2, 128], P('section', 'tensor')
The draws below stay inside these ranges and needn't reach their ends.
Inputs may be any that keep to these rules, and one draw needn't show every extreme that they name: `target_token`: the targets' tokens are distinct, and the last token is always one of them.
All inputs are finite; a program needn't handle non-finite values.
Results may differ from the reference program's by a relative error of at most 0.04.
Values may be sent and summed in bfloat16 or wider, within the bound.
A program may use at most 64 MiB of HBM per device.

```python
import math
import jax
import jax.numpy as jnp
from jax import lax

D = 5120
HEADS = 64
KV = 8
HD = 128
FEAT = 16384
TARGETS = 2
ACT = 128
TOK = 96
LAYERS = 8
N_TENSOR = 16


def draw_attn_logits(key, part):
    key = jax.random.fold_in(key, 11)
    keys = jax.random.split(key, 1)
    shape = (LAYERS, HEADS, TOK, TOK)
    logits = 1.5 * jax.random.truncated_normal(keys[0], -5.0, 5.0, shape, jnp.float32)
    return logits.astype(jnp.bfloat16)


def draw_target_token(key, part):
    key = jax.random.fold_in(key, 23)
    keys = jax.random.split(key, 2)
    order = jax.random.permutation(keys[0], TOK // 2 - 1) + TOK // 2
    chosen = jnp.concatenate([jnp.full((1,), TOK - 1, jnp.int32), order[:TARGETS - 1].astype(jnp.int32)])
    return jax.random.permutation(keys[1], chosen).astype(jnp.int32)


def shard_levels(own_key, shape, cuts, smallest, largest):
    level = 1.0
    for dim, parts in cuts:
        draws = jax.random.uniform(jax.random.fold_in(jax.random.fold_in(own_key, 6), dim), (parts,), jnp.float32, smallest / len(cuts), largest / len(cuts))
        level = level * jnp.repeat(jnp.exp(draws), shape[dim] // parts).reshape((-1,) + (1,) * (len(shape) - 1 - dim))
    return level


def different_ones(key, rows, number_of, top, lift):
    ranking = jax.random.permutation(jax.random.fold_in(key, 1), number_of)
    boost = ranking
    for power in range(3):
        boost = boost * boost // number_of
    boost = boost * lift // number_of
    lots = jax.random.randint(jax.random.fold_in(key, 2), (rows, number_of), 0, 4096) + boost
    sure = jax.random.permutation(jax.random.fold_in(key, 3), rows)[jnp.arange(number_of) % rows]
    lots = jnp.where(jnp.arange(rows)[:, None] == sure[None, :], 1 << 14, lots)
    score = lots * number_of + jnp.arange(number_of)
    return lax.top_k(score.astype(jnp.int32), top)[1].astype(jnp.int32)


def gaussian(rng, dims, deviation, most, shards=(), held_as=jnp.bfloat16):
    array = deviation * jax.random.normal(rng, dims, jnp.float32)
    if shards:
        array = array * shard_levels(rng, dims, shards, -0.22, 0.18)
    return jnp.clip(array, -most, most).astype(held_as)


def setup_inputs(seed: int = 0) -> dict:
    splits = jax.random.split(jax.random.key(seed), 12)
    return {
        "attn_logits": draw_attn_logits(jax.random.fold_in(splits[11], 71), 0),
        "out_weight": gaussian(splits[1], (LAYERS, HEADS * HD, D), (HEADS * HD) ** -0.5, 0.0625, ((0, 8), (1, 16))),
        "value_weight": gaussian(splits[2], (LAYERS, KV * HD, D), D ** -0.5, 0.078125, ((0, 8), (1, 16))),
        "norm_gain": jnp.clip(1.0 + 0.18 * jax.random.normal(splits[3], (LAYERS, D), jnp.float32), 0.1, 1.9),
        "norm_scale": jnp.clip(jnp.exp(math.log(2.0) - 1.3862944 * jax.random.uniform(splits[4], (LAYERS, TOK), jnp.float32) ** shard_levels(splits[4], (LAYERS, TOK), ((0, 8), (1, 16)), -0.2, 0.2)), 0.5, 2.0),
        "target_encoder": gaussian(splits[5], (FEAT, D), 1.0, 6.0, ((1, 128),)),
        "target_ids": jax.random.randint(splits[6], (TARGETS,), 0, FEAT).astype(jnp.int32),
        "target_token": draw_target_token(jax.random.fold_in(splits[11], 71), 0),
        "decoder": gaussian(splits[8], (LAYERS, FEAT, D), D ** -0.5, 0.078125, ((0, 8), (1, 16))),
        "source_ids": different_ones(splits[9], LAYERS * TOK, FEAT, ACT, 128).reshape((LAYERS, TOK, ACT)),
        "source_values": jnp.clip(jnp.exp(math.log(0.6) - 2.4849067 * jax.random.uniform(splits[10], (LAYERS, TOK, ACT), jnp.float32) ** shard_levels(splits[10], (LAYERS, TOK, ACT), ((0, 8),), -0.2, 0.2)), 0.05, 0.6),
    }


def frozen_pattern(logits):
    scores = logits.astype(jnp.float32)
    query_pos = lax.broadcasted_iota(jnp.int32, scores.shape, scores.ndim - 2)
    key_pos = lax.broadcasted_iota(jnp.int32, scores.shape, scores.ndim - 1)
    scores = jnp.where(key_pos <= query_pos, scores, -jnp.inf)
    highest = jnp.max(scores, axis=-1, keepdims=True)
    weights = jnp.exp(scores - highest)
    return (weights / jnp.sum(weights, axis=-1, keepdims=True)).astype(jnp.bfloat16)


def pull_back(gradient, pattern, out_rows, value_rows, gain_row, scale_row):
    tok_count = gradient.shape[0]
    targets_here = gradient.shape[1]
    model_width = gradient.shape[2]
    head_grad = jnp.dot(gradient.reshape(tok_count * targets_here, model_width), out_rows.T,
                        preferred_element_type=jnp.float32).astype(jnp.bfloat16)
    head_grad = head_grad.reshape(tok_count, targets_here, HEADS, HD)
    per_head = jnp.einsum('hts,tkhc->skhc', pattern.astype(jnp.float32), head_grad.astype(jnp.float32))
    value_grad = per_head.reshape(tok_count, targets_here, KV, HEADS // KV, HD).sum(axis=3)
    value_grad = value_grad.reshape(tok_count * targets_here, KV * HD).astype(jnp.bfloat16)
    block_width = KV * HD // N_TENSOR
    mixed = jnp.zeros((tok_count * targets_here, model_width), jnp.float32)
    for block_index in range(N_TENSOR):
        lower = block_index * block_width
        partial_term = jnp.dot(value_grad[:, lower:lower + block_width], value_rows[lower:lower + block_width],
                               preferred_element_type=jnp.float32).astype(jnp.bfloat16)
        partial_term = lax.optimization_barrier(partial_term)
        mixed = mixed + partial_term.astype(jnp.float32)
    mixed = mixed.reshape(tok_count, targets_here, model_width)
    change = mixed * gain_row.astype(jnp.float32)[None, None, :] * scale_row.astype(jnp.float32)[:, None, None]
    return (gradient.astype(jnp.float32) + change).astype(jnp.bfloat16)


def reference(attn_logits, out_weight, value_weight, norm_gain, norm_scale, target_encoder, target_ids,
              target_token, decoder, source_ids, source_values):
    encoder_rows = target_encoder[target_ids.astype(jnp.int32)]
    positions = jnp.arange(TOK, dtype=jnp.int32)
    hit = positions[:, None, None] == target_token.astype(jnp.int32)[None, :, None]
    gradient = jnp.where(hit, encoder_rows[None, :, :], jnp.zeros_like(encoder_rows)[None, :, :]).astype(jnp.bfloat16)
    edge_list = []
    for layer_index in reversed(range(LAYERS)):
        source_rows = decoder[layer_index][source_ids[layer_index].astype(jnp.int32)]
        dots = jnp.einsum('tad,tkd->tka', source_rows.astype(jnp.float32), gradient.astype(jnp.float32))
        edge_list.append(dots * source_values[layer_index].astype(jnp.float32)[:, None, :])
        if layer_index > 0:
            gradient = pull_back(gradient, frozen_pattern(attn_logits[layer_index]), out_weight[layer_index],
                                 value_weight[layer_index], norm_gain[layer_index], norm_scale[layer_index])
    return jnp.stack(edge_list[::-1], axis=0)
```

```python
import jax
import jax.numpy as jnp
from jax import lax
from jax.experimental import pallas as pl
from jax.experimental.pallas import tpu as pltpu
from jax.sharding import PartitionSpec as P

MESH = pl.DeviceIdType.MESH
F32 = jnp.float32
BF16 = jnp.bfloat16

TOK = 96
N = 16
TOP = 7
HD = 128
WIDE = 640
HEADS_HERE = 4
ACT = 128
FEATS = 1024


def nt_dot(a, b):
    return lax.dot_general(a, b, (((1,), (1,)), ((), ())), preferred_element_type=F32)


def chain_kernel(
    enc_ref, scale_ref, logits_ref, gain_ref, tok_ref, ids_ref, vals_ref,
    wo_hbm, wv_hbm, dec_hbm,
    out_ref,
    wo, dec, wvs, grad, grad_send, v_send, v_recv, sc_recv, sc_rows,
    e1_recv, e2_send, e2_recv, pat, hcat, pad, acc, ed_send, ed_recv,
    local_sem, wv_ssem, wv_rsem, sc_ssem, sc_rsem, e1_ssem, e1_rsem, e2_ssem, e2_rsem,
    v_ssem, v_rsem, g_ssem, g_rsem, hop_ssem, ed_ssem, ed_rsem,
):
    s = lax.axis_index("section")
    j = lax.axis_index("tensor")
    my_k = lax.rem(j, 2)
    my_d = j // 2

    def peer(o):
        return lax.rem(j + o, N)

    def remote(src, dst, ssem, rsem, section, index):
        return pltpu.make_async_remote_copy(
            src_ref=src, dst_ref=dst, send_sem=ssem, recv_sem=rsem,
            device_id=(section, index), device_id_type=MESH,
        )

    def arrived(dst, rsem, ssem):
        remote(dst, dst, ssem, rsem, s, peer(1)).wait_recv()

    barrier = pltpu.get_barrier_semaphore()

    def greet(section, index):
        pl.semaphore_signal(barrier, inc=1, device_id=(section, index), device_id_type=MESH)

    @pl.when(s < TOP)
    def _():
        greet(TOP, j)

    @pl.when(s == TOP)
    def _():
        for q in range(TOP):
            greet(q, j)

    @pl.when(s < TOP - 1)
    def _():
        greet(s + 1, j)

    @pl.when((s >= 1) & (s < TOP))
    def _():
        greet(s - 1, j)

    @pl.loop(1, N)
    def _(o):
        greet(s, peer(o))

    wo_copy = pltpu.make_async_copy(wo_hbm, wo, local_sem.at[0])
    wo_copy.start()
    own_cols = pl.ds(pl.multiple_of(my_d * WIDE, 128), WIDE)
    own_rows = pl.ds(pl.multiple_of(j * 64, 64), 64)
    wv_copy = pltpu.make_async_copy(wv_hbm.at[:, own_cols], wvs.at[own_rows], local_sem.at[1])
    wv_copy.start()
    dec_copy = pltpu.make_async_copy(dec_hbm, dec, local_sem.at[2])
    dec_copy.start()

    pl.semaphore_wait(
        barrier,
        15
        + jnp.where(s == TOP, TOP, 1)
        + jnp.where(s < TOP - 1, 1, 0)
        + jnp.where((s >= 1) & (s < TOP), 1, 0),
    )

    @pl.when(s < TOP)
    def _():
        remote(enc_ref, e1_recv.at[s], e1_ssem, e1_rsem.at[s], TOP, j).start()

    def sc_copy(o):
        return remote(scale_ref, sc_recv.at[j], sc_ssem.at[o], sc_rsem.at[j], s, peer(o))

    def wv_peer_copy(o):
        p = peer(o)
        cols = pl.ds(pl.multiple_of((p // 2) * WIDE, 128), WIDE)
        return remote(
            wv_hbm.at[:, cols], wvs.at[own_rows], wv_ssem.at[o], wv_rsem.at[j], s, p
        )

    def start_weights():
        @pl.when(s >= 1)
        def _():
            @pl.loop(1, N)
            def _(o):
                sc_copy(o).start()
                wv_peer_copy(o).start()

    @pl.when(s < TOP)
    def _():
        start_weights()

    pad[...] = jnp.zeros_like(pad)
    hcat[...] = jnp.zeros_like(hcat)
    query = lax.broadcasted_iota(jnp.int32, (TOK, TOK), 0)
    key = lax.broadcasted_iota(jnp.int32, (TOK, TOK), 1)
    for h in range(HEADS_HERE):
        scores = jnp.where(key <= query, logits_ref[h].astype(F32), -jnp.inf)
        highest = jnp.max(scores, axis=-1, keepdims=True)
        weights = jnp.exp(scores - highest)
        pad[0:TOK, 0:TOK] = weights / jnp.sum(weights, axis=-1, keepdims=True)
        pat[:, h * HD : (h + 1) * HD] = pad[...].T[0:TOK, :].astype(BF16)

    @pl.when(s == TOP)
    def _():
        e1_recv[TOP] = enc_ref[...]
        for q in range(TOP):
            arrived(e1_recv.at[q], e1_rsem.at[q], e1_ssem)
        rows = jnp.concatenate([e1_recv[:, 0, :], e1_recv[:, 1, :]], axis=0)
        e2_send[...] = rows.astype(BF16)
        e2_recv[j] = rows.astype(BF16)

        def e2_copy(o):
            return remote(e2_send, e2_recv.at[j], e2_ssem.at[o], e2_rsem.at[j], s, peer(o))

        @pl.loop(1, N)
        def _(o):
            e2_copy(o).start()

        start_weights()

        @pl.loop(1, N)
        def _(o):
            p = peer(o)
            arrived(e2_recv.at[p], e2_rsem.at[p], e2_ssem.at[o])

        blocks = [jnp.zeros((16, 128), F32) for _ in range(5)]
        for q in range(N):
            first = min(40 * q // 128, 3)
            piece = e2_recv[q].astype(F32)
            blocks[first] = blocks[first] + piece[:, 0:128]
            blocks[first + 1] = blocks[first + 1] + piece[:, 128:256]
        top_rows = jnp.concatenate(blocks, axis=1)
        token = lax.broadcasted_iota(jnp.int32, (TOK, WIDE), 0)
        for k in range(2):
            hit = token == tok_ref[k]
            for d in range(8):
                row = jnp.broadcast_to(top_rows[k * 8 + d : k * 8 + d + 1, :], (TOK, WIDE))
                grad[2 * d + k] = jnp.where(hit, row, 0.0).astype(BF16)

        @pl.loop(1, N)
        def _(o):
            e2_copy(o).wait_send()

    def chunk_copy(o):
        return remote(grad.at[j], grad.at[j], g_ssem.at[o], g_rsem.at[j], s, peer(o))

    @pl.when(s < TOP)
    def _():
        arrived(grad.at[j], g_rsem.at[j], g_ssem.at[0])

        @pl.loop(1, N)
        def _(o):
            chunk_copy(o).start()

    wo_copy.wait()
    wv_copy.wait()

    def v_copy(k, d):
        p = 2 * d + k
        return remote(
            v_send.at[k], v_recv.at[j], v_ssem.at[p], v_rsem.at[j], s, p
        )

    def hop_copy():
        return remote(grad_send, grad.at[j], hop_ssem, g_rsem.at[j], s - 1, j)

    def wait_chunk(c):
        @pl.when((s < TOP) & (c != j))
        def _():
            arrived(grad.at[c], g_rsem.at[c], g_ssem.at[0])

    def consume():
        @pl.loop(1, N)
        def _(o):
            p = peer(o)
            arrived(v_recv.at[p], v_rsem.at[p], v_ssem.at[0])

        pieces = []
        for q in range(8):
            both = v_recv[2 * q].astype(F32) + v_recv[2 * q + 1].astype(F32)
            pieces.append((both * sc_rows[...]).astype(BF16))
        value_grad = jnp.concatenate(pieces, axis=1)
        mixed = jnp.dot(value_grad, wvs[...], preferred_element_type=F32)
        grad_send[...] = (grad[j].astype(F32) + mixed * gain_ref[:, own_cols]).astype(BF16)
        hop_copy().start()

    @pl.when(s >= 1)
    def _():
        @pl.loop(1, N)
        def _(o):
            p = peer(o)
            arrived(sc_recv.at[p], sc_rsem.at[p], sc_ssem.at[0])
            rows = pl.ds(pl.multiple_of(p * 64, 64), 64)
            arrived(wvs.at[rows], wv_rsem.at[p], wv_ssem.at[0])

        sc_recv[j] = scale_ref[...]
        for q in range(N):
            sc_rows[6 * q : 6 * q + 6, :] = sc_recv[q, 0:6, :]

        @pl.loop(0, 2)
        def _(k):
            total = jnp.zeros((TOK, HEADS_HERE * HD), F32)
            for d in range(8):
                wait_chunk(2 * d + k)
                total += nt_dot(grad[2 * d + k], wo[:, d * WIDE : (d + 1) * WIDE])
            head_grad = total.astype(BF16)
            for h in range(HEADS_HERE):
                hcat[h * HD : h * HD + TOK, :] = head_grad[:, h * HD : (h + 1) * HD]
            part = jnp.dot(pat[...], hcat[...], preferred_element_type=F32).astype(BF16)
            v_send[k] = part
            for d in range(8):
                @pl.when(2 * d + k != j)
                def _():
                    v_copy(k, d).start()

            @pl.when(my_k == k)
            def _():
                v_recv[j] = part
                consume()

    @pl.when(s == 0)
    def _():
        for c in range(N):
            wait_chunk(c)

    dec_copy.wait()
    for d in range(8):
        both = jnp.concatenate([grad[2 * d], grad[2 * d + 1]], axis=0)
        term = nt_dot(both, dec[:, d * WIDE : (d + 1) * WIDE])
        if d == 0:
            acc[...] = term
        else:
            acc[...] += term
    local_id = ids_ref[...] - j * FEATS
    lane = local_id & 127
    block = local_id >> 7
    chosen = []
    for k in range(2):
        picked = jnp.zeros((TOK, ACT), F32)
        for b in range(8):
            table = acc[k * TOK : (k + 1) * TOK, b * 128 : (b + 1) * 128]
            got = jnp.take_along_axis(table, lane, axis=1)
            picked = jnp.where(block == b, got, picked)
        chosen.append((picked * vals_ref[...]).astype(BF16))
    terms = jnp.concatenate(chosen, axis=0)
    row = lax.broadcasted_iota(jnp.int32, (256, 192), 0)
    col = lax.broadcasted_iota(jnp.int32, (256, 192), 1)
    slot = row & 7
    source = ((row >> 3) & 1) * TOK + (row >> 4) * 6 + slot
    spread = jnp.where((col == source) & (slot < 6), 1.0, 0.0).astype(BF16)
    spread_terms = jnp.dot(spread, terms, preferred_element_type=F32).astype(BF16)
    for q in range(N):
        ed_send[q] = spread_terms[16 * q : 16 * q + 16, :]

    def ed_copy(o):
        p = peer(o)
        return remote(ed_send.at[p], ed_recv.at[j], ed_ssem.at[o], ed_rsem.at[j], s, p)

    @pl.loop(1, N)
    def _(o):
        ed_copy(o).start()

    ed_recv[j] = ed_send[j]

    @pl.loop(1, N)
    def _(o):
        p = peer(o)
        arrived(ed_recv.at[p], ed_rsem.at[p], ed_ssem.at[o])

    edges = jnp.zeros((16, ACT), F32)
    for q in range(N):
        edges += ed_recv[q].astype(F32)
    out_ref[...] = edges

    @pl.loop(1, N)
    def _(o):
        ed_copy(o).wait_send()

    @pl.when(s < TOP)
    def _():
        remote(enc_ref, e1_recv.at[s], e1_ssem, e1_rsem.at[s], TOP, j).wait_send()

        @pl.loop(1, N)
        def _(o):
            chunk_copy(o).wait_send()

    @pl.when(s >= 1)
    def _():
        @pl.loop(1, N)
        def _(o):
            sc_copy(o).wait_send()
            wv_peer_copy(o).wait_send()

        for k in range(2):
            for d in range(8):
                @pl.when(2 * d + k != j)
                def _():
                    v_copy(k, d).wait_send()

        hop_copy().wait_send()


def body(
    attn_logits, out_weight, value_weight, norm_gain, norm_scale, target_encoder,
    target_ids, target_token, decoder, source_ids, source_values,
):
    j = lax.axis_index("tensor")
    picked = jnp.concatenate(
        [lax.dynamic_slice_in_dim(target_encoder, target_ids[k], 1, axis=0) for k in range(2)],
        axis=0,
    ).astype(F32)
    start = 40 * j - 128 * jnp.minimum(40 * j // 128, 3)
    enc = lax.dynamic_update_slice(jnp.zeros((8, 256), F32), picked, (0, start))
    scale = jnp.broadcast_to(jnp.pad(norm_scale[0], (0, 2))[:, None], (8, 128))

    vmem = pl.BlockSpec(memory_space=pltpu.VMEM)
    smem = pl.BlockSpec(memory_space=pltpu.SMEM)
    hbm = pl.BlockSpec(memory_space=pl.ANY)
    dma = pltpu.SemaphoreType.DMA
    out = pl.pallas_call(
        chain_kernel,
        out_shape=jax.ShapeDtypeStruct((16, ACT), F32),
        in_specs=[vmem, vmem, vmem, vmem, smem, vmem, vmem, hbm, hbm, hbm],
        out_specs=vmem,
        scratch_shapes=[
            pltpu.VMEM((512, 5120), BF16),
            pltpu.VMEM((FEATS, 5120), BF16),
            pltpu.VMEM((1024, WIDE), BF16),
            pltpu.VMEM((N, TOK, WIDE), BF16),
            pltpu.VMEM((TOK, WIDE), BF16),
            pltpu.VMEM((2, TOK, HD), BF16),
            pltpu.VMEM((N, TOK, HD), BF16),
            pltpu.VMEM((N, 8, 128), F32),
            pltpu.VMEM((TOK, 128), F32),
            pltpu.VMEM((8, 8, 256), F32),
            pltpu.VMEM((16, 256), BF16),
            pltpu.VMEM((N, 16, 256), BF16),
            pltpu.VMEM((TOK, HEADS_HERE * HD), BF16),
            pltpu.VMEM((HEADS_HERE * HD, HD), BF16),
            pltpu.VMEM((128, 128), F32),
            pltpu.VMEM((2 * TOK, FEATS), F32),
            pltpu.VMEM((N, 16, ACT), BF16),
            pltpu.VMEM((N, 16, ACT), BF16),
            dma((3,)),
            dma((N,)), dma((N,)),
            dma((N,)), dma((N,)),
            dma, dma((8,)),
            dma((N,)), dma((N,)),
            dma((N,)), dma((N,)),
            dma((N,)), dma((N,)),
            dma,
            dma((N,)), dma((N,)),
        ],
        compiler_params=pltpu.CompilerParams(
            collective_id=0, has_side_effects=True, vmem_limit_bytes=48 * 2**20
        ),
        name="chain",
    )(
        enc, scale, attn_logits[0], norm_gain, target_token, source_ids[0], source_values[0],
        out_weight[0], value_weight[0], decoder[0],
    )
    return out.reshape(2, 8, ACT)[:, :6].transpose(1, 0, 2)[None]


def solution(mesh):
    return jax.shard_map(
        body,
        mesh=mesh,
        in_specs=(
            P("section", "tensor", None, None),
            P("section", "tensor", None),
            P("section", "tensor", None),
            P("section", None),
            P("section", "tensor"),
            P(None, ("section", "tensor")),
            P(),
            P(),
            P("section", "tensor", None),
            P("section", None, None),
            P("section", None, None),
        ),
        out_specs=P("section", "tensor", None, None),
        check_vma=False,
    )
```

```python
import jax
import jax.numpy as jnp
from jax import lax
from jax.experimental import pallas as pl
from jax.experimental.pallas import tpu as pltpu
from jax.sharding import PartitionSpec as P

MESH = pl.DeviceIdType.MESH
F32 = jnp.float32
BF16 = jnp.bfloat16

TOK = 96
N = 16
TOP = 7
HD = 128
WIDE = 640
HEADS_HERE = 4
ACT = 128
FEATS = 1024


def nt_dot(a, b):
    return lax.dot_general(a, b, (((1,), (1,)), ((), ())), preferred_element_type=F32)


def chain_kernel(
    enc_hbm, scale_hbm, logits_hbm, gain_hbm, want_hbm, tok_hbm, ids_hbm, vals_hbm,
    wo_hbm, wv_hbm, dec_hbm,
    out_ref,
    table, scale_raw, logits_ref, gain_up, want_ref, tok_ref, ids_ref, vals_ref,
    enc_ref, scale_ref,
    wo, dec, wvs, wvf, joint, grad, grad_base, grad_own, v_send, v_recv, v_full, base,
    sc_recv, sc_rows, e1_recv, e2_send, e2_recv, pat, hcat, pad, acc, ed_send, ed_recv,
    local_sem, gain_ssem, gain_rsem, wv_ssem, wv_rsem, fw_ssem, fw_rsem, sc_ssem, sc_rsem,
    e1_ssem, e1_rsem, e2_ssem, e2_rsem, v_ssem, v_rsem, g_ssem, g_rsem, hop_ssem, hop_rsem,
    copy_ssem, copy_rsem, ed_ssem, ed_rsem,
):
    s = lax.axis_index("section")
    j = lax.axis_index("tensor")
    my_k = lax.rem(j, 2)
    my_d = j // 2
    row = j // 4
    col = lax.rem(j, 4)
    mine = my_k * 8 + my_d
    below = s - 1
    spreads = (s == 6) | (s == 5) | (s == 3) | (s == 1)
    joins = (s == 4) | (s == 2) | (s == 0)
    feeds_spread = (s == 7) | (s == 6) | (s == 4) | (s == 2)
    feeds_join = (s == 5) | (s == 3) | (s == 1)

    def peer(o):
        return lax.rem(j + o, N)

    def at_row(o):
        return row * 4 + lax.rem(col + o, 4)

    def at_col(o):
        return lax.rem(row + o, 4) * 4 + col

    def chunk_of(p):
        return lax.rem(p, 2) * 8 + p // 2

    def remote(src, dst, ssem, rsem, section, index):
        return pltpu.make_async_remote_copy(
            src_ref=src, dst_ref=dst, send_sem=ssem, recv_sem=rsem,
            device_id=(section, index), device_id_type=MESH,
        )

    def arrived(dst, rsem, ssem):
        remote(dst, dst, ssem, rsem, s, peer(1)).wait_recv()

    barrier = pltpu.get_barrier_semaphore()

    def greet(section, index):
        pl.semaphore_signal(barrier, inc=1, device_id=(section, index), device_id_type=MESH)

    @pl.when(s < TOP - 1)
    def _():
        greet(TOP, j)

    @pl.when(s == TOP)
    def _():
        for q in range(TOP - 1):
            greet(q, j)

    @pl.loop(1, N)
    def _(o):
        greet(s, peer(o))

    @pl.when(s < TOP)
    def _():
        @pl.loop(0, N)
        def _(p):
            greet(s + 1, p)

    @pl.when(s >= 1)
    def _():
        @pl.loop(0, N)
        def _(p):
            greet(below, p)

    small = [
        pltpu.make_async_copy(src, dst, local_sem.at[2 + i])
        for i, (src, dst) in enumerate([
            (want_hbm, want_ref), (enc_hbm, table), (scale_hbm, scale_raw),
            (logits_hbm, logits_ref), (tok_hbm, tok_ref),
            (ids_hbm, ids_ref), (vals_hbm, vals_ref),
        ])
    ]
    for copy in small:
        copy.start()
    wo_copy = pltpu.make_async_copy(wo_hbm, wo, local_sem.at[0])
    wo_copy.start()
    dec_copy = pltpu.make_async_copy(dec_hbm, dec, local_sem.at[1])
    dec_copy.start()

    small[0].wait()
    small[1].wait()
    first_lane = 40 * j - 128 * jnp.minimum((40 * j) // 128, 3)
    spot = lax.broadcasted_iota(jnp.int32, (40, 256), 1) - lax.broadcasted_iota(jnp.int32, (40, 256), 0)
    lane = lax.broadcasted_iota(jnp.int32, (40, 512), 1)

    def pick(i, found):
        part = table[:, pl.ds(pl.multiple_of(i * 512, 512), 512)].astype(F32)
        return tuple(
            found[k] + jnp.where(lane + i * 512 == want_ref[k], part, 0.0) for k in range(2)
        )

    found = lax.fori_loop(0, 32, pick, (jnp.zeros((40, 512), F32),) * 2)
    enc_ref[...] = jnp.zeros_like(enc_ref)
    for k in range(2):
        column = jnp.sum(found[k], axis=1, keepdims=True)
        enc_ref[k : k + 1, :] = jnp.sum(
            jnp.where(spot == first_lane, column, 0.0), axis=0, keepdims=True
        )
    small[2].wait()
    diagonal = lax.broadcasted_iota(jnp.int32, (8, 6), 0) == lax.broadcasted_iota(jnp.int32, (8, 6), 1)
    scale_ref[...] = jnp.broadcast_to(
        jnp.sum(jnp.where(diagonal, scale_raw[...], 0.0), axis=1, keepdims=True), (8, 128)
    )

    pl.semaphore_wait(
        barrier,
        15
        + jnp.where(s >= 1, N, 0)
        + jnp.where(s < TOP, N, 0)
        + jnp.where(s < TOP - 1, 1, 0)
        + jnp.where(s == TOP, TOP - 1, 0),
    )

    def e1_copy():
        return remote(enc_ref, e1_recv.at[s], e1_ssem, e1_rsem.at[s], TOP, j)

    @pl.when(s < TOP)
    def _():
        e1_copy().start()

    def sc_copy(o):
        return remote(scale_ref, sc_recv.at[j], sc_ssem.at[o], sc_rsem.at[j], s, peer(o))

    def gain_copy():
        return remote(gain_hbm, gain_up, gain_ssem, gain_rsem, below, j)

    def wv_copy(p):
        cols = pl.ds(pl.multiple_of((p // 2) * WIDE, 128), WIDE)
        rows = pl.ds(pl.multiple_of(j * 64, 64), 64)
        return remote(
            wv_hbm.at[:, cols], wvs.at[rows], wv_ssem.at[p], wv_rsem.at[j], below, p
        )

    def half_rows(c, h):
        return wvf.at[pl.ds(pl.multiple_of(c * 64 + 32 * h, 32), 32)]

    def full_copy(h, o):
        return remote(
            wv_hbm.at[pl.ds(32 * h, 32)], half_rows(j, h),
            wv_ssem.at[4 * h + o], fw_rsem.at[2 * j + h], below, at_col(o) if h else at_row(o),
        )

    @pl.when(s >= 1)
    def _():
        gain_copy().start()

        @pl.loop(1, N)
        def _(o):
            sc_copy(o).start()

    @pl.when(feeds_spread)
    def _():
        @pl.loop(0, N)
        def _(p):
            wv_copy(p).start()

    @pl.when(feeds_join)
    def _():
        for o in (0, 1, 3, 2):
            for h in range(2):
                full_copy(h, o).start()

    for copy in small[3:]:
        copy.wait()
    pad[...] = jnp.zeros_like(pad)
    hcat[...] = jnp.zeros_like(hcat)
    query = lax.broadcasted_iota(jnp.int32, (TOK, TOK), 0)
    key = lax.broadcasted_iota(jnp.int32, (TOK, TOK), 1)
    for h in range(HEADS_HERE):
        scores = jnp.where(key <= query, logits_ref[h].astype(F32), -jnp.inf)
        highest = jnp.max(scores, axis=-1, keepdims=True)
        weights = jnp.exp(scores - highest)
        pad[0:TOK, 0:TOK] = weights / jnp.sum(weights, axis=-1, keepdims=True)
        pat[:, h * HD : (h + 1) * HD] = pad[...].T[0:TOK, :].astype(BF16)

    def hop_copy(src):
        return remote(src, grad_base, hop_ssem, hop_rsem, below, j)

    @pl.when(s == TOP)
    def _():
        e1_recv[TOP] = enc_ref[...]
        for q in range(TOP):
            arrived(e1_recv.at[q], e1_rsem.at[q], e1_ssem)
        rows = jnp.concatenate([e1_recv[:, 0, :], e1_recv[:, 1, :]], axis=0)
        e2_send[...] = rows.astype(BF16)
        e2_recv[j] = rows.astype(BF16)

        def e2_copy(o):
            return remote(e2_send, e2_recv.at[j], e2_ssem.at[o], e2_rsem.at[j], s, peer(o))

        @pl.loop(1, N)
        def _(o):
            e2_copy(o).start()

        @pl.loop(1, N)
        def _(o):
            p = peer(o)
            arrived(e2_recv.at[p], e2_rsem.at[p], e2_ssem.at[o])

        blocks = [jnp.zeros((16, 128), F32) for _ in range(5)]
        for q in range(N):
            first = min(40 * q // 128, 3)
            piece = e2_recv[q].astype(F32)
            blocks[first] = blocks[first] + piece[:, 0:128]
            blocks[first + 1] = blocks[first + 1] + piece[:, 128:256]
        top_rows = jnp.concatenate(blocks, axis=1)
        token = lax.broadcasted_iota(jnp.int32, (TOK, WIDE), 0)
        for k in range(2):
            hit = token == tok_ref[k]
            for d in range(8):
                one = jnp.broadcast_to(top_rows[k * 8 + d : k * 8 + d + 1, :], (TOK, WIDE))
                grad[8 * k + d] = jnp.where(hit, one, 0.0).astype(BF16)
        hop_copy(grad.at[mine]).start()

        @pl.loop(1, N)
        def _(o):
            e2_copy(o).wait_send()

    forwards = []
    for o in (0, 1, 3, 2):
        forwards.append([(at_row(o), 0, at_col(q), 4 * o + q) for q in (1, 3, 2)])
        forwards.append([(at_col(o), 1, at_row(q), 16 + 4 * o + q) for q in (1, 3, 2)])

    def forward_copy(c, h, to, sem):
        return remote(half_rows(c, h), half_rows(c, h), fw_ssem.at[sem], fw_rsem.at[2 * c + h], s, to)

    @pl.when(joins)
    def _():
        for items in forwards:
            c, h = items[0][0], items[0][1]
            arrived(half_rows(c, h), fw_rsem.at[2 * c + h], fw_ssem.at[0])
            for item in items:
                forward_copy(*item).start()
        arrived(gain_up, gain_rsem, gain_ssem)

        @pl.loop(0, N)
        def _(c):
            @pl.when(c // 4 != row)
            def _():
                arrived(half_rows(c, 0), fw_rsem.at[2 * c], fw_ssem.at[0])

            @pl.when(lax.rem(c, 4) != col)
            def _():
                arrived(half_rows(c, 1), fw_rsem.at[2 * c + 1], fw_ssem.at[0])

        for items in forwards:
            for item in items:
                forward_copy(*item).wait_send()

        @pl.loop(0, 64)
        def _(i):
            part = pl.ds(pl.multiple_of(i * 16, 16), 16)
            wvf[part, :] = (wvf[part, :].astype(F32) * gain_up[...]).astype(BF16)

    wo_copy.wait()
    dec_copy.wait()

    @pl.when((s == 4) | (s == 2))
    def _():
        @pl.loop(0, 4)
        def _(i):
            part = pl.ds(pl.multiple_of(i * 256, 256), 256)
            total = jnp.zeros((256, HEADS_HERE * HD), F32)
            for d in range(8):
                cols = slice(d * WIDE, (d + 1) * WIDE)
                total += nt_dot(wvf[part, cols], wo[:, cols])
            joint[part, 0 : HEADS_HERE * HD] = total.astype(BF16)

    @pl.when(s == 0)
    def _():
        @pl.loop(0, 8)
        def _(i):
            part = pl.ds(pl.multiple_of(i * 128, 128), 128)
            total = jnp.zeros((128, FEATS), F32)
            for d in range(8):
                cols = slice(d * WIDE, (d + 1) * WIDE)
                total += nt_dot(wvf[part, cols], dec[:, cols])
            joint[part, :] = total.astype(BF16)

    @pl.when(s >= 1)
    def _():
        @pl.loop(1, N)
        def _(o):
            p = peer(o)
            arrived(sc_recv.at[p], sc_rsem.at[p], sc_ssem.at[0])

        sc_recv[j] = scale_ref[...]
        for q in range(N):
            sc_rows[6 * q : 6 * q + 6, :] = sc_recv[q, 0:6, :]

    def value_grad(k):
        @pl.loop(0, N)
        def _(p):
            arrived(v_recv.at[k, p], v_rsem.at[k * N + p], v_ssem.at[0])

        pieces = []
        for q in range(8):
            both = v_recv[k, 2 * q].astype(F32) + v_recv[k, 2 * q + 1].astype(F32)
            pieces.append(both.astype(BF16))
        return jnp.concatenate(pieces, axis=1)

    def v_copy(k, p):
        return remote(
            v_send.at[k], v_recv.at[k, j], v_ssem.at[k * N + p], v_rsem.at[k * N + j], below, p
        )

    def send_values(k, head_grad):
        for h in range(HEADS_HERE):
            hcat[h * HD : h * HD + TOK, :] = head_grad[:, h * HD : (h + 1) * HD]
        part = jnp.dot(pat[...], hcat[...], preferred_element_type=F32)
        v_send[k] = (part * sc_rows[...]).astype(BF16)
        for p in range(N):
            @pl.when(feeds_join | (k == p % 2))
            def _():
                v_copy(k, p).start()

    def half_copy(c, h, to, sem):
        part = grad.at[chunk_of(c), pl.ds(48 * h, 48)]
        return remote(part, part, g_ssem.at[sem], g_rsem.at[2 * c + h], s, to)

    def half_arrived(c, h):
        arrived(grad.at[chunk_of(c), pl.ds(48 * h, 48)], g_rsem.at[2 * c + h], g_ssem.at[0])

    own_sends, row_sends, col_sends = [], [], []
    for o in (1, 3, 2):
        own_sends.append((j, 0, at_row(o), o))
        own_sends.append((j, 1, at_col(o), 4 + o))
    for o in (1, 3, 2):
        own_sends.append((j, 0, at_col(o), 8 + o))
        own_sends.append((j, 1, at_row(o), 12 + o))
    for o in (1, 3, 2):
        row_sends.append([(at_row(o), 0, at_col(q), 16 + 4 * o + q) for q in (1, 3, 2)])
        col_sends.append([(at_col(o), 1, at_row(q), 32 + 4 * o + q) for q in (1, 3, 2)])

    own_cols = pl.ds(pl.multiple_of(my_d * WIDE, 128), WIDE)

    def make_chunk():
        mixed = jnp.dot(value_grad(my_k), wvs[...], preferred_element_type=F32)
        grad[mine] = (grad_base[...].astype(F32) + mixed * gain_up[:, own_cols]).astype(BF16)
        for item in own_sends:
            half_copy(*item).start()

        @pl.when(s == 6)
        def _():
            hop_copy(grad.at[mine]).start()

    def forward(k):
        for items in row_sends:
            c = items[0][0]

            @pl.when(lax.rem(c, 2) == k)
            def _():
                half_arrived(c, 0)
                for item in items:
                    half_copy(*item).start()

        @pl.when(my_k == k)
        def _():
            for items in col_sends:
                half_arrived(items[0][0], 1)
                for item in items:
                    half_copy(*item).start()

    def wait_chunk(k, d):
        c = 2 * d + k

        @pl.when(spreads & (c // 4 != row))
        def _():
            half_arrived(c, 0)

        @pl.when(spreads & (lax.rem(c, 4) != col))
        def _():
            half_arrived(c, 1)

    def whole_copy(k):
        part = grad.at[pl.ds(8 * k, 8)]
        return remote(part, part, copy_ssem.at[k], copy_rsem.at[k], below, j)

    @pl.when(spreads)
    def _():
        arrived(gain_up, gain_rsem, gain_ssem)

        @pl.loop(0, N)
        def _(p):
            rows = pl.ds(pl.multiple_of(p * 64, 64), 64)
            arrived(wvs.at[rows], wv_rsem.at[p], wv_ssem.at[0])

        arrived(grad_base, hop_rsem, hop_ssem)

    @pl.when(spreads)
    def _():
        make_chunk()
        forward(0)

        forward(1)


    @pl.when(spreads | (s == TOP))
    def _():
        @pl.loop(0, 2)
        def _(k):
            total = jnp.zeros((TOK, HEADS_HERE * HD), F32)
            for d in range(8):
                wait_chunk(k, d)
                total += nt_dot(grad[8 * k + d], wo[:, d * WIDE : (d + 1) * WIDE])
            send_values(k, total.astype(BF16))

            @pl.when(feeds_join)
            def _():
                whole_copy(k).start()

    @pl.when((s == 4) | (s == 2))
    def _():
        @pl.loop(0, 2)
        def _(k):
            arrived(grad.at[pl.ds(8 * k, 8)], copy_rsem.at[k], copy_ssem.at[0])
            total = jnp.zeros((TOK, HEADS_HERE * HD), F32)
            for d in range(8):
                total += nt_dot(grad[8 * k + d], wo[:, d * WIDE : (d + 1) * WIDE])
            base[...] = total
            values = value_grad(k)
            v_full[k] = values
            total = base[...] + jnp.dot(
                values, joint[:, 0 : HEADS_HERE * HD], preferred_element_type=F32
            )
            send_values(k, total.astype(BF16))

            @pl.when(my_k == k)
            def _():
                mixed = jnp.dot(values, wvf[:, own_cols], preferred_element_type=F32)
                grad_own[...] = (grad[mine].astype(F32) + mixed).astype(BF16)
                hop_copy(grad_own).start()

        @pl.loop(0, 2)
        def _(k):
            for d in range(8):
                mixed = jnp.dot(
                    v_full[k], wvf[:, d * WIDE : (d + 1) * WIDE], preferred_element_type=F32
                )
                grad[8 * k + d] = (grad[8 * k + d].astype(F32) + mixed).astype(BF16)

    @pl.when(s == 0)
    def _():
        for k in range(2):
            arrived(grad.at[pl.ds(8 * k, 8)], copy_rsem.at[k], copy_ssem.at[0])
            part = slice(k * TOK, (k + 1) * TOK)
            for d in range(8):
                term = nt_dot(grad[8 * k + d], dec[:, d * WIDE : (d + 1) * WIDE])
                if d == 0:
                    acc[part, :] = term
                else:
                    acc[part, :] += term
            acc[part, :] += jnp.dot(value_grad(k), joint[...], preferred_element_type=F32)

    @pl.when(s >= 1)
    def _():
        for d in range(8):
            both = jnp.concatenate([grad[d], grad[8 + d]], axis=0)
            term = nt_dot(both, dec[:, d * WIDE : (d + 1) * WIDE])
            if d == 0:
                acc[...] = term
            else:
                acc[...] += term

    local_id = ids_ref[...] - j * FEATS
    lane = local_id & 127
    block = local_id >> 7
    chosen = []
    for k in range(2):
        picked = jnp.zeros((TOK, ACT), F32)
        for b in range(8):
            near = acc[k * TOK : (k + 1) * TOK, b * 128 : (b + 1) * 128]
            got = jnp.take_along_axis(near, lane, axis=1)
            picked = jnp.where(block == b, got, picked)
        chosen.append((picked * vals_ref[...]).astype(BF16))
    terms = jnp.concatenate(chosen, axis=0)
    e_row = lax.broadcasted_iota(jnp.int32, (256, 192), 0)
    e_col = lax.broadcasted_iota(jnp.int32, (256, 192), 1)
    slot = e_row & 7
    source = ((e_row >> 3) & 1) * TOK + (e_row >> 4) * 6 + slot
    placing = jnp.where((e_col == source) & (slot < 6), 1.0, 0.0).astype(BF16)
    placed = jnp.dot(placing, terms, preferred_element_type=F32).astype(BF16)
    for q in range(N):
        ed_send[q] = placed[16 * q : 16 * q + 16, :]

    def ed_copy(o):
        p = peer(o)
        return remote(ed_send.at[p], ed_recv.at[j], ed_ssem.at[o], ed_rsem.at[j], s, p)

    @pl.loop(1, N)
    def _(o):
        ed_copy(o).start()

    ed_recv[j] = ed_send[j]

    @pl.loop(1, N)
    def _(o):
        p = peer(o)
        arrived(ed_recv.at[p], ed_rsem.at[p], ed_ssem.at[o])

    edges = jnp.zeros((16, ACT), F32)
    for q in range(N):
        edges += ed_recv[q].astype(F32)
    out_ref[...] = edges

    @pl.loop(1, N)
    def _(o):
        ed_copy(o).wait_send()

    @pl.when(s < TOP)
    def _():
        e1_copy().wait_send()

    @pl.when(s >= 1)
    def _():
        gain_copy().wait_send()

        @pl.loop(1, N)
        def _(o):
            sc_copy(o).wait_send()

        for k in range(2):
            for p in range(N):
                @pl.when(feeds_join | (k == p % 2))
                def _():
                    v_copy(k, p).wait_send()

    @pl.when(feeds_spread)
    def _():
        hop_copy(grad_own).wait_send()

        @pl.loop(0, N)
        def _(p):
            wv_copy(p).wait_send()

    @pl.when(feeds_join)
    def _():
        for o in range(4):
            for h in range(2):
                full_copy(h, o).wait_send()
        for k in range(2):
            whole_copy(k).wait_send()

    @pl.when(spreads)
    def _():
        for item in own_sends + sum(row_sends, []) + sum(col_sends, []):
            half_copy(*item).wait_send()


def body(
    attn_logits, out_weight, value_weight, norm_gain, norm_scale, target_encoder,
    target_ids, target_token, decoder, source_ids, source_values,
):
    vmem = pl.BlockSpec(memory_space=pltpu.VMEM)
    hbm = pl.BlockSpec(memory_space=pltpu.HBM)
    dma = pltpu.SemaphoreType.DMA
    out = pl.pallas_call(
        chain_kernel,
        out_shape=jax.ShapeDtypeStruct((16, ACT), F32),
        in_specs=[hbm] * 11,
        out_specs=vmem,
        scratch_shapes=[
            pltpu.VMEM((40, 16384), BF16),
            pltpu.VMEM((1, 6), F32),
            pltpu.VMEM((HEADS_HERE, TOK, TOK), BF16),
            pltpu.VMEM((1, 5120), F32),
            pltpu.SMEM((2,), jnp.int32),
            pltpu.SMEM((2,), jnp.int32),
            pltpu.VMEM((TOK, ACT), jnp.int32),
            pltpu.VMEM((TOK, ACT), F32),
            pltpu.VMEM((8, 256), F32),
            pltpu.VMEM((8, 128), F32),
            pltpu.VMEM((512, 5120), BF16),
            pltpu.VMEM((FEATS, 5120), BF16),
            pltpu.VMEM((1024, WIDE), BF16),
            pltpu.VMEM((1024, 5120), BF16),
            pltpu.VMEM((1024, FEATS), BF16),
            pltpu.VMEM((N, TOK, WIDE), BF16),
            pltpu.VMEM((TOK, WIDE), BF16),
            pltpu.VMEM((TOK, WIDE), BF16),
            pltpu.VMEM((2, TOK, HD), BF16),
            pltpu.VMEM((2, N, TOK, HD), BF16),
            pltpu.VMEM((2, TOK, 1024), BF16),
            pltpu.VMEM((TOK, HEADS_HERE * HD), F32),
            pltpu.VMEM((N, 8, 128), F32),
            pltpu.VMEM((TOK, 128), F32),
            pltpu.VMEM((8, 8, 256), F32),
            pltpu.VMEM((16, 256), BF16),
            pltpu.VMEM((N, 16, 256), BF16),
            pltpu.VMEM((TOK, HEADS_HERE * HD), BF16),
            pltpu.VMEM((HEADS_HERE * HD, HD), BF16),
            pltpu.VMEM((128, 128), F32),
            pltpu.VMEM((2 * TOK, FEATS), F32),
            pltpu.VMEM((N, 16, ACT), BF16),
            pltpu.VMEM((N, 16, ACT), BF16),
            dma((9,)),
            dma, dma,
            dma((N,)), dma((N,)),
            dma((2 * N,)), dma((2 * N,)),
            dma((N,)), dma((N,)),
            dma, dma((8,)),
            dma((N,)), dma((N,)),
            dma((2 * N,)), dma((2 * N,)),
            dma((3 * N,)), dma((2 * N,)),
            dma, dma,
            dma((2,)), dma((2,)),
            dma((N,)), dma((N,)),
        ],
        compiler_params=pltpu.CompilerParams(
            collective_id=0, has_side_effects=True, vmem_limit_bytes=63 * 2**20
        ),
        name="chain",
    )(
        target_encoder.T, norm_scale, attn_logits[0], norm_gain, target_ids, target_token,
        source_ids[0], source_values[0],
        out_weight[0], value_weight[0], decoder[0],
    )
    return out.reshape(2, 8, ACT)[:, :6].transpose(1, 0, 2)[None]


def solution(mesh):
    return jax.shard_map(
        body,
        mesh=mesh,
        in_specs=(
            P("section", "tensor", None, None),
            P("section", "tensor", None),
            P("section", "tensor", None),
            P("section", None),
            P("section", "tensor"),
            P(None, ("section", "tensor")),
            P(),
            P(),
            P("section", "tensor", None),
            P("section", None, None),
            P("section", None, None),
        ),
        out_specs=P("section", "tensor", None, None),
        check_vma=False,
    )
```

```python
import jax
import jax.numpy as jnp
from jax import lax
from jax.experimental import pallas as pl
from jax.experimental.pallas import tpu as pltpu
from jax.sharding import PartitionSpec as P

MESH = pl.DeviceIdType.MESH
F32 = jnp.float32
BF16 = jnp.bfloat16

TOK = 96
N = 16
TOP = 7
HD = 128
WIDE = 640
HEADS_HERE = 4
ACT = 128
FEATS = 1024
FAR_FIRST = sorted(
    [(dy, dx) for dy in range(4) for dx in range(4)],
    key=lambda at: -min(at[0], 4 - at[0]) - min(at[1], 4 - at[1]),
)


def nt_dot(a, b):
    return lax.dot_general(a, b, (((1,), (1,)), ((), ())), preferred_element_type=F32)


def chain_kernel(
    enc_hbm, scale_hbm, logits_hbm, gain_hbm, want_hbm, tok_hbm, ids_hbm, vals_hbm,
    wo_hbm, wv_hbm, dec_hbm,
    out_ref,
    table, scale_raw, logits_ref, gain_up, want_ref, tok_ref, ids_ref, vals_ref,
    enc_ref, scale_ref,
    wo, wo_t, dec, wvs, wvf, joint, grad, grad_base, grad_own, v_send, v_recv, v_full, base,
    sc_recv, sc_rows, e1_recv, e2_send, e2_recv, pat, hcat, pad, acc, ed_send, ed_recv,
    local_sem, gain_ssem, gain_rsem, wv_ssem, wv_rsem, fw_ssem, fw_rsem, sc_ssem, sc_rsem,
    e1_ssem, e1_rsem, e2_ssem, e2_rsem, v_ssem, v_rsem, g_ssem, g_rsem, hop_ssem, hop_rsem,
    copy_ssem, copy_rsem, ed_ssem, ed_rsem,
    seeds, u_rows, u_send, u_recv, mix_send, mix_recv, mix,
    wv_stage, stage_ssem, stage_rsem, pair_ssem, pair_rsem, u_ssem, u_rsem, mix_ssem, mix_rsem, seed_ssem, seed_rsem,
):
    s = lax.axis_index("section")
    j = lax.axis_index("tensor")
    my_k = lax.rem(j, 2)
    my_d = j // 2
    row = j // 4
    col = lax.rem(j, 4)
    below = s - 1
    spreads = (s == 5) | (s == 4) | (s == 3) | (s == 1)
    joins = (s == 2) | (s == 0)
    second = s == TOP - 1
    feeds_spread = (s == 6) | (s == 5) | (s == 4) | (s == 2)
    feeds_join = (s == 3) | (s == 1)

    def peer(o):
        return lax.rem(j + o, N)

    def far_first(body):
        for dy, dx in FAR_FIRST:
            body(lax.rem(row + dy, 4) * 4 + lax.rem(col + dx, 4))

    def far_first_peers(body):
        for dy, dx in FAR_FIRST[:-1]:
            body(lax.rem(row + dy, 4) * 4 + lax.rem(col + dx, 4))

    def at_row(o):
        return row * 4 + lax.rem(col + o, 4)

    def at_col(o):
        return lax.rem(row + o, 4) * 4 + col

    def remote(src, dst, ssem, rsem, section, index):
        return pltpu.make_async_remote_copy(
            src_ref=src, dst_ref=dst, send_sem=ssem, recv_sem=rsem,
            device_id=(section, index), device_id_type=MESH,
        )

    def arrived(dst, rsem, ssem):
        remote(dst, dst, ssem, rsem, s, peer(1)).wait_recv()

    barrier = pltpu.get_barrier_semaphore()

    def greet(section, index):
        pl.semaphore_signal(barrier, inc=1, device_id=(section, index), device_id_type=MESH)

    @pl.when(s < TOP - 1)
    def _():
        greet(TOP, j)

    @pl.when(s == TOP)
    def _():
        for q in range(TOP - 1):
            greet(q, j)

    @pl.loop(1, N)
    def _(o):
        greet(s, peer(o))

    @pl.when(s < TOP)
    def _():
        @pl.loop(0, N)
        def _(p):
            greet(s + 1, p)

    @pl.when(s >= 1)
    def _():
        @pl.loop(0, N)
        def _(p):
            greet(below, p)

    small = [
        pltpu.make_async_copy(src, dst, local_sem.at[2 + i])
        for i, (src, dst) in enumerate([
            (want_hbm, want_ref), (enc_hbm, table), (scale_hbm, scale_raw),
            (logits_hbm, logits_ref), (tok_hbm, tok_ref),
            (ids_hbm, ids_ref), (vals_hbm, vals_ref),
        ])
    ]
    for copy in small:
        copy.start()
    wo_copy = pltpu.make_async_copy(wo_hbm, wo, local_sem.at[0])
    wo_copy.start()
    dec_copy = pltpu.make_async_copy(dec_hbm, dec, local_sem.at[1])
    dec_copy.start()

    small[0].wait()
    small[1].wait()
    first_lane = 40 * j - 128 * jnp.minimum((40 * j) // 128, 3)
    spot = lax.broadcasted_iota(jnp.int32, (40, 256), 1) - lax.broadcasted_iota(jnp.int32, (40, 256), 0)
    lane = lax.broadcasted_iota(jnp.int32, (40, 512), 1)

    def pick(i, found):
        part = table[:, pl.ds(pl.multiple_of(i * 512, 512), 512)].astype(F32)
        return tuple(
            found[k] + jnp.where(lane + i * 512 == want_ref[k], part, 0.0) for k in range(2)
        )

    found = lax.fori_loop(0, 32, pick, (jnp.zeros((40, 512), F32),) * 2)
    enc_ref[...] = jnp.zeros_like(enc_ref)
    for k in range(2):
        column = jnp.sum(found[k], axis=1, keepdims=True)
        enc_ref[k : k + 1, :] = jnp.sum(
            jnp.where(spot == first_lane, column, 0.0), axis=0, keepdims=True
        )
    small[2].wait()
    diagonal = lax.broadcasted_iota(jnp.int32, (8, 6), 0) == lax.broadcasted_iota(jnp.int32, (8, 6), 1)
    scale_ref[...] = jnp.broadcast_to(
        jnp.sum(jnp.where(diagonal, scale_raw[...], 0.0), axis=1, keepdims=True), (8, 128)
    )

    pl.semaphore_wait(
        barrier,
        15
        + jnp.where(s >= 1, N, 0)
        + jnp.where(s < TOP, N, 0)
        + jnp.where(s < TOP - 1, 1, 0)
        + jnp.where(s == TOP, TOP - 1, 0),
    )

    def e1_copy():
        return remote(enc_ref, e1_recv.at[s], e1_ssem, e1_rsem.at[s], TOP, j)

    @pl.when(s < TOP)
    def _():
        e1_copy().start()

    def sc_copy(o):
        return remote(scale_ref, sc_recv.at[j], sc_ssem.at[o], sc_rsem.at[j], s, peer(o))

    def gain_copy():
        return remote(gain_hbm, gain_up, gain_ssem, gain_rsem, below, j)

    def stage_copy():
        return remote(wv_hbm, wv_stage, stage_ssem, stage_rsem, below, j)

    own_rows = pl.ds(pl.multiple_of(j * 64, 64), 64)

    def columns_of(p):
        return wv_stage.at[:, pl.ds(pl.multiple_of((p // 2) * WIDE, 128), WIDE)]

    def wv_copy(o):
        p = peer(o)
        return remote(columns_of(p), wvs.at[own_rows], wv_ssem.at[o], wv_rsem.at[j], s, p)

    own_columns = pltpu.make_async_copy(columns_of(j), wvs.at[own_rows], local_sem.at[11])

    def half_rows(c, h):
        return wvf.at[pl.ds(pl.multiple_of(c * 64 + 32 * h, 32), 32)]

    def full_copy(h, o):
        return remote(
            wv_hbm.at[pl.ds(32 * h, 32)], half_rows(j, h),
            wv_ssem.at[4 * h + o], fw_rsem.at[2 * j + h], below, at_col(o) if h else at_row(o),
        )

    def pair_rows(h, k):
        return wvf.at[pl.ds(pl.multiple_of(k * 64 + 32 * h, 32), 32)]

    def pair_copy(h):
        return remote(
            wv_hbm.at[pl.ds(32 * h, 32)], pair_rows(h, my_k),
            pair_ssem.at[h], pair_rsem.at[h], s, j + 1 - 2 * my_k,
        )

    own_wv = pltpu.make_async_copy(
        wv_hbm, wvf.at[pl.ds(pl.multiple_of(my_k * 64, 64), 64)], local_sem.at[9]
    )
    own_gain = pltpu.make_async_copy(gain_hbm, gain_up, local_sem.at[10])

    @pl.when(s == TOP)
    def _():
        own_wv.start()
        own_gain.start()

    @pl.when((s >= 1) & (s < TOP))
    def _():
        gain_copy().start()

    @pl.when(s >= 1)
    def _():
        @pl.loop(1, N)
        def _(o):
            sc_copy(o).start()

    @pl.when(s == TOP)
    def _():
        pair_copy(0).start()

    @pl.when(feeds_spread)
    def _():
        stage_copy().start()

    @pl.when(feeds_join)
    def _():
        for o in (2, 1, 3, 0):
            for h in range(2):
                full_copy(h, o).start()

    for copy in small[3:]:
        copy.wait()
    pad[...] = jnp.zeros_like(pad)
    hcat[...] = jnp.zeros_like(hcat)
    query = lax.broadcasted_iota(jnp.int32, (TOK, TOK), 0)
    key = lax.broadcasted_iota(jnp.int32, (TOK, TOK), 1)
    for h in range(HEADS_HERE):
        scores = jnp.where(key <= query, logits_ref[h].astype(F32), -jnp.inf)
        highest = jnp.max(scores, axis=-1, keepdims=True)
        weights = jnp.exp(scores - highest)
        pad[0:TOK, 0:TOK] = weights / jnp.sum(weights, axis=-1, keepdims=True)
        pat[:, h * HD : (h + 1) * HD] = pad[...].T[0:TOK, :].astype(BF16)

    @pl.when(spreads)
    def _():
        arrived(wv_stage, stage_rsem, stage_ssem)
        own_columns.start()

        @pl.loop(1, N)
        def _(o):
            wv_copy(o).start()

    def u_copy(h, o):
        part = u_recv.at[j, :, pl.ds(1280 * h, 1280)]
        return remote(
            u_send.at[:, pl.ds(1280 * h, 1280)], part,
            u_ssem.at[4 * h + o], u_rsem.at[2 * j + h], below, at_col(o) if h else at_row(o),
        )

    def mix_copy(p):
        return remote(mix_send, mix_recv.at[j], mix_ssem.at[p], mix_rsem.at[j], below, p)

    def spread_scales():
        @pl.loop(1, N)
        def _(o):
            p = peer(o)
            arrived(sc_recv.at[p], sc_rsem.at[p], sc_ssem.at[0])

        sc_recv[j] = scale_ref[...]
        for q in range(N):
            sc_rows[6 * q : 6 * q + 6, :] = sc_recv[q, 0:6, :]

    def seed_copy():
        return remote(seeds, u_recv.at[N], seed_ssem, seed_rsem, below, j)

    def hop_copy(src):
        return remote(src, grad_base, hop_ssem, hop_rsem, below, j)

    @pl.when(s == TOP)
    def _():
        e1_recv[TOP] = enc_ref[...]
        for q in range(TOP):
            arrived(e1_recv.at[q], e1_rsem.at[q], e1_ssem)
        rows = jnp.concatenate([e1_recv[:, 0, :], e1_recv[:, 1, :]], axis=0)
        e2_send[...] = rows.astype(BF16)
        e2_recv[j] = rows.astype(BF16)

        def e2_copy(o):
            return remote(e2_send, e2_recv.at[j], e2_ssem.at[o], e2_rsem.at[j], s, o)

        far_first_peers(lambda p: e2_copy(p).start())

        pair_copy(1).start()
        spread_scales()
        lane = lax.broadcasted_iota(jnp.int32, (TOK, HEADS_HERE * HD), 1)
        place = lax.broadcasted_iota(jnp.int32, (TOK, HD), 1) - 16 * lax.rem(j, 8)
        slab = jnp.zeros((TOK, HD), F32)
        for k in range(2):
            for h in range(HEADS_HERE):
                hit = lane == h * HD + tok_ref[k]
                chosen = jnp.sum(jnp.where(hit, pat[...].astype(F32), 0.0), axis=1, keepdims=True)
                spot = 4 * k + h
                slab = slab + jnp.where((place == spot) | (place == spot + 8), chosen, 0.0)
        mix_send[...] = (slab * sc_rows[...]).astype(BF16)

        @pl.loop(1, N)
        def _(o):
            p = peer(o)
            arrived(e2_recv.at[p], e2_rsem.at[p], e2_ssem.at[o])

        blocks = [jnp.zeros((16, 128), F32) for _ in range(5)]
        for q in range(N):
            first = min(40 * q // 128, 3)
            piece = e2_recv[q].astype(F32)
            blocks[first] = blocks[first] + piece[:, 0:128]
            blocks[first + 1] = blocks[first + 1] + piece[:, 128:256]
        top_rows = jnp.concatenate(blocks, axis=1)
        seeds[...] = jnp.zeros_like(seeds)
        for d in range(4):
            cols = slice(d * WIDE, (d + 1) * WIDE)
            for k in range(2):
                low = top_rows[k * 8 + d : k * 8 + d + 1, :]
                high = top_rows[k * 8 + d + 4 : k * 8 + d + 5, :]
                seeds[k : k + 1, cols] = low.astype(BF16)
                seeds[8 + k : 9 + k, cols] = high.astype(BF16)
        seed_copy().start()
        wo_copy.wait()
        half = 2560
        low = nt_dot(seeds[...], wo[:, 0:half])
        high = nt_dot(seeds[...], wo[:, half:])
        rows = low[0:2] + high[8:10]
        parts = [
            rows[k : k + 1, h * HD : (h + 1) * HD] for k in range(2) for h in range(HEADS_HERE)
        ]
        head_rows = jnp.concatenate(parts, axis=0).astype(BF16)
        own_wv.wait()
        own_gain.wait()
        for h in range(2):
            arrived(pair_rows(h, 1 - my_k), pair_rsem.at[h], pair_ssem.at[h])
        for h in range(2):
            cols = slice(h * half, (h + 1) * half)
            mixed = jnp.dot(head_rows, wvf[0:128, cols], preferred_element_type=F32)
            u_rows[8 * h : 8 * h + 8, :] = mixed * gain_up[:, cols]
        u_send[...] = u_rows[...].astype(BF16)
        for o in (2, 1, 3, 0):
            for h in range(2):
                u_copy(h, o).start()

        @pl.loop(0, N)
        def _(p):
            mix_copy(p).start()

        token = lax.broadcasted_iota(jnp.int32, (TOK, WIDE), 0)
        for k in range(2):
            hit = token == tok_ref[k]
            for d in range(8):
                one = jnp.broadcast_to(top_rows[k * 8 + d : k * 8 + d + 1, :], (TOK, WIDE))
                grad[2 * d + k] = jnp.where(hit, one, 0.0).astype(BF16)

        @pl.loop(1, N)
        def _(o):
            e2_copy(peer(o)).wait_send()

    @pl.when((s >= 1) & (s < TOP))
    def _():
        spread_scales()

    forwards = []
    for o in (0, 1, 3, 2):
        forwards.append([(at_row(o), 0, at_col(q), 4 * o + q) for q in (2, 1, 3)])
        forwards.append([(at_col(o), 1, at_row(q), 16 + 4 * o + q) for q in (2, 1, 3)])

    def forward_copy(c, h, to, sem):
        return remote(half_rows(c, h), half_rows(c, h), fw_ssem.at[sem], fw_rsem.at[2 * c + h], s, to)

    @pl.when(joins)
    def _():
        for items in forwards:
            c, h = items[0][0], items[0][1]
            arrived(half_rows(c, h), fw_rsem.at[2 * c + h], fw_ssem.at[0])
            for item in items:
                forward_copy(*item).start()
        arrived(gain_up, gain_rsem, gain_ssem)

        @pl.loop(0, N)
        def _(c):
            @pl.when(c // 4 != row)
            def _():
                arrived(half_rows(c, 0), fw_rsem.at[2 * c], fw_ssem.at[0])

            @pl.when(lax.rem(c, 4) != col)
            def _():
                arrived(half_rows(c, 1), fw_rsem.at[2 * c + 1], fw_ssem.at[0])

        for items in forwards:
            for item in items:
                forward_copy(*item).wait_send()

        @pl.loop(0, 64)
        def _(i):
            part = pl.ds(pl.multiple_of(i * 16, 16), 16)
            wvf[part, :] = (wvf[part, :].astype(F32) * gain_up[...]).astype(BF16)

    @pl.when(s < TOP)
    def _():
        wo_copy.wait()

    dec_copy.wait()

    @pl.when(spreads)
    def _():
        @pl.loop(0, 40)
        def _(i):
            part = pl.ds(pl.multiple_of(i * 128, 128), 128)
            wo_t[part, :] = wo[:, part].T

    @pl.when(s == 2)
    def _():
        @pl.loop(0, 4)
        def _(i):
            part = pl.ds(pl.multiple_of(i * 256, 256), 256)
            total = jnp.zeros((256, HEADS_HERE * HD), F32)
            for d in range(8):
                cols = slice(d * WIDE, (d + 1) * WIDE)
                total += nt_dot(wvf[part, cols], wo[:, cols])
            joint[part, 0 : HEADS_HERE * HD] = total.astype(BF16)

    @pl.when(s == 0)
    def _():
        @pl.loop(0, 8)
        def _(i):
            part = pl.ds(pl.multiple_of(i * 128, 128), 128)
            total = jnp.zeros((128, FEATS), F32)
            for d in range(8):
                cols = slice(d * WIDE, (d + 1) * WIDE)
                total += nt_dot(wvf[part, cols], dec[:, cols])
            joint[part, :] = total.astype(BF16)

    def wait_values():
        @pl.loop(0, N)
        def _(p):
            @pl.when(spreads)
            def _():
                arrived(v_recv.at[p, 0], v_rsem.at[p], v_ssem.at[0])

            @pl.when(joins)
            def _():
                arrived(v_recv.at[p], v_rsem.at[p], v_ssem.at[0])

    def value_grad(k):
        pieces = []
        for q in range(8):
            both = v_recv[2 * q, k].astype(F32) + v_recv[2 * q + 1, k].astype(F32)
            pieces.append(both.astype(BF16))
        return jnp.concatenate(pieces, axis=1)

    def v_copy_both(p):
        return remote(v_send, v_recv.at[j], v_ssem.at[p], v_rsem.at[j], below, p)

    def v_copy_one(p):
        return remote(v_send.at[lax.rem(p, 2)], v_recv.at[j, 0], v_ssem.at[p], v_rsem.at[j], below, p)

    def send_values(head_grad):
        for k in range(2):
            for h in range(HEADS_HERE):
                hcat[h * HD : h * HD + TOK, k * HD : (k + 1) * HD] = head_grad[
                    k * TOK : (k + 1) * TOK, h * HD : (h + 1) * HD
                ]
        part = jnp.dot(pat[...], hcat[...], preferred_element_type=F32)
        for k in range(2):
            v_send[k] = (part[:, k * HD : (k + 1) * HD] * sc_rows[...]).astype(BF16)

        @pl.when(feeds_join)
        def _():
            far_first(lambda p: v_copy_both(p).start())

        @pl.when(feeds_spread)
        def _():
            far_first(lambda p: v_copy_one(p).start())

    def half_copy(c, h, to, sem):
        part = grad.at[c, pl.ds(48 * h, 48)]
        return remote(part, part, g_ssem.at[sem], g_rsem.at[2 * c + h], s, to)

    def half_arrived(c, h):
        arrived(grad.at[c, pl.ds(48 * h, 48)], g_rsem.at[2 * c + h], g_ssem.at[0])

    own_sends, row_sends, col_sends = [], [], []
    for o in (2, 1, 3):
        own_sends.append((j, 0, at_row(o), o))
        own_sends.append((j, 1, at_col(o), 4 + o))
    for o in (2, 1, 3):
        own_sends.append((j, 0, at_col(o), 8 + o))
        own_sends.append((j, 1, at_row(o), 12 + o))
    for o in (1, 3, 2):
        row_sends.append([(at_row(o), 0, at_col(q), 16 + 4 * o + q) for q in (2, 1, 3)])
        col_sends.append([(at_col(o), 1, at_row(q), 32 + 4 * o + q) for q in (2, 1, 3)])

    own_cols = pl.ds(pl.multiple_of(my_d * WIDE, 128), WIDE)

    def make_chunk():
        wait_values()
        mixed = jnp.dot(value_grad(0), wvs[...], preferred_element_type=F32)
        grad[j] = (grad_base[...].astype(F32) + mixed * gain_up[:, own_cols]).astype(BF16)
        for item in own_sends:
            half_copy(*item).start()

        @pl.when(feeds_spread)
        def _():
            hop_copy(grad.at[j]).start()

    def forward(k):
        for items in row_sends:
            c = items[0][0]

            @pl.when(lax.rem(c, 2) == k)
            def _():
                half_arrived(c, 0)
                for item in items:
                    half_copy(*item).start()

        @pl.when(my_k == k)
        def _():
            for items in col_sends:
                half_arrived(items[0][0], 1)
                for item in items:
                    half_copy(*item).start()

    def wait_chunk(c):
        @pl.when(c // 4 != row)
        def _():
            half_arrived(c, 0)

        @pl.when(c % 4 != col)
        def _():
            half_arrived(c, 1)

    def whole_copy(d):
        part = grad.at[pl.ds(2 * d, 2)]
        return remote(part, part, copy_ssem.at[d], copy_rsem.at[d], below, j)

    def whole_arrived(d):
        arrived(grad.at[pl.ds(2 * d, 2)], copy_rsem.at[d], copy_ssem.at[0])

    def head_grad_of(at_chunk, dot):
        total = jnp.zeros((2 * TOK, HEADS_HERE * HD), F32)
        for d in range(8):
            at_chunk(d)
            both = grad[2 * d : 2 * d + 2].reshape(2 * TOK, WIDE)
            total += dot(both, slice(d * WIDE, (d + 1) * WIDE))
        return total

    @pl.when(spreads)
    def _():
        arrived(gain_up, gain_rsem, gain_ssem)
        own_columns.wait()

        @pl.loop(1, N)
        def _(o):
            p = peer(o)
            rows = pl.ds(pl.multiple_of(p * 64, 64), 64)
            arrived(wvs.at[rows], wv_rsem.at[p], wv_ssem.at[0])

        arrived(grad_base, hop_rsem, hop_ssem)

    @pl.when(spreads)
    def _():
        make_chunk()
        forward(0)
        forward(1)

        def take_chunks(d):
            wait_chunk(2 * d)
            wait_chunk(2 * d + 1)

            @pl.when(feeds_join)
            def _():
                whole_copy(d).start()

        send_values(head_grad_of(
            take_chunks,
            lambda both, part: jnp.dot(both, wo_t[part, :], preferred_element_type=F32),
        ).astype(BF16))

    u_forwards = []
    for o in (0, 1, 3, 2):
        u_forwards.append([(at_row(o), 0, at_col(q), 8 + 4 * o + q) for q in (2, 1, 3)])
        u_forwards.append([(at_col(o), 1, at_row(q), 24 + 4 * o + q) for q in (2, 1, 3)])

    def u_half(c, h):
        return u_recv.at[c, :, pl.ds(1280 * h, 1280)]

    def u_forward(c, h, to, sem):
        return remote(u_half(c, h), u_half(c, h), u_ssem.at[sem], u_rsem.at[2 * c + h], s, to)

    @pl.when(second)
    def _():
        for items in u_forwards:
            c, h = items[0][0], items[0][1]
            arrived(u_half(c, h), u_rsem.at[2 * c + h], u_ssem.at[0])
            for item in items:
                u_forward(*item).start()

        @pl.loop(0, N)
        def _(p):
            arrived(mix_recv.at[p], mix_rsem.at[p], mix_ssem.at[0])

        arrived(u_recv.at[N], seed_rsem, seed_ssem)
        kind = lax.broadcasted_iota(jnp.int32, (TOK, HD), 1) & 15
        for t in range(2):
            tile = jnp.zeros((TOK, HD), F32)
            for q in range(8):
                tile = tile + mix_recv[8 * t + q].astype(F32)
            for h in range(2):
                for k in range(2):
                    keep = (kind >> 2) == 2 * h + k
                    mix[h, k * TOK : (k + 1) * TOK, t * HD : (t + 1) * HD] = jnp.where(
                        keep, tile, 0.0
                    ).astype(BF16)

        @pl.loop(0, N)
        def _(c):
            @pl.when(c // 4 != row)
            def _():
                arrived(u_half(c, 0), u_rsem.at[2 * c], u_ssem.at[0])

            @pl.when(lax.rem(c, 4) != col)
            def _():
                arrived(u_half(c, 1), u_rsem.at[2 * c + 1], u_ssem.at[0])

        half = 2560
        flat = u_recv[...].reshape(16 * (N + 1), half)
        low = nt_dot(flat, wo[:, 0:half])
        high = nt_dot(flat, wo[:, half:])
        total = jnp.dot(mix[0], low[0:256].astype(BF16), preferred_element_type=F32)
        total += jnp.dot(mix[1], high[0:256].astype(BF16), preferred_element_type=F32)
        token = lax.broadcasted_iota(jnp.int32, (TOK, HEADS_HERE * HD), 0)
        parts = []
        for k in range(2):
            one = low[256 + k : 257 + k] + high[264 + k : 265 + k]
            parts.append(
                total[k * TOK : (k + 1) * TOK] + jnp.where(token == tok_ref[k], one, 0.0)
            )
        send_values(jnp.concatenate(parts, axis=0).astype(BF16))
        token = lax.broadcasted_iota(jnp.int32, (TOK, WIDE), 0)
        for d in range(8):
            h, cols = d // 4, slice((d % 4) * WIDE, (d % 4 + 1) * WIDE)
            head_rows = u_recv[0:N, :, cols].reshape(16 * N, WIDE)
            mixed = jnp.dot(mix[h], head_rows, preferred_element_type=F32)
            for k in range(2):
                one = u_recv[N, 8 * h + k : 8 * h + k + 1, cols].astype(F32)
                grad[2 * d + k] = (
                    mixed[k * TOK : (k + 1) * TOK] + jnp.where(token == tok_ref[k], one, 0.0)
                ).astype(BF16)
        hop_copy(grad.at[j]).start()

    @pl.when(s == 2)
    def _():
        base[...] = head_grad_of(whole_arrived, lambda both, part: nt_dot(both, wo[:, part]))
        wait_values()
        for k in range(2):
            v_full[k * TOK : (k + 1) * TOK, :] = value_grad(k)
        total = base[...] + jnp.dot(
            v_full[...], joint[:, 0 : HEADS_HERE * HD], preferred_element_type=F32
        )
        send_values(total.astype(BF16))
        mixed = jnp.dot(
            v_full[pl.ds(pl.multiple_of(my_k * TOK, TOK), TOK), :], wvf[:, own_cols],
            preferred_element_type=F32,
        )
        grad_own[...] = (grad[j].astype(F32) + mixed).astype(BF16)
        hop_copy(grad_own).start()
        for d in range(8):
            mixed = jnp.dot(
                v_full[...], wvf[:, d * WIDE : (d + 1) * WIDE], preferred_element_type=F32
            )
            for k in range(2):
                grad[2 * d + k] = (
                    grad[2 * d + k].astype(F32) + mixed[k * TOK : (k + 1) * TOK]
                ).astype(BF16)

    @pl.when(s == 0)
    def _():
        for d in range(8):
            whole_arrived(d)

    for d in range(8):
        both = grad[2 * d : 2 * d + 2].reshape(2 * TOK, WIDE)
        term = nt_dot(both, dec[:, d * WIDE : (d + 1) * WIDE])
        if d == 0:
            acc[...] = term
        else:
            acc[...] += term

    @pl.when(s == 0)
    def _():
        wait_values()
        for k in range(2):
            v_full[k * TOK : (k + 1) * TOK, :] = value_grad(k)
        acc[...] += jnp.dot(v_full[...], joint[...], preferred_element_type=F32)

    local_id = ids_ref[...] - j * FEATS
    lane = local_id & 127
    block = local_id >> 7
    chosen = []
    for k in range(2):
        picked = jnp.zeros((TOK, ACT), F32)
        for b in range(8):
            near = acc[k * TOK : (k + 1) * TOK, b * 128 : (b + 1) * 128]
            got = jnp.take_along_axis(near, lane, axis=1)
            picked = jnp.where(block == b, got, picked)
        chosen.append((picked * vals_ref[...]).astype(BF16))
    terms = jnp.concatenate(chosen, axis=0)
    e_row = lax.broadcasted_iota(jnp.int32, (256, 192), 0)
    e_col = lax.broadcasted_iota(jnp.int32, (256, 192), 1)
    slot = e_row & 7
    source = ((e_row >> 3) & 1) * TOK + (e_row >> 4) * 6 + slot
    placing = jnp.where((e_col == source) & (slot < 6), 1.0, 0.0).astype(BF16)
    placed = jnp.dot(placing, terms, preferred_element_type=F32).astype(BF16)
    for q in range(N):
        ed_send[q] = placed[16 * q : 16 * q + 16, :]

    def ed_copy(p):
        return remote(ed_send.at[p], ed_recv.at[j], ed_ssem.at[p], ed_rsem.at[j], s, p)

    far_first_peers(lambda p: ed_copy(p).start())

    ed_recv[j] = ed_send[j]

    @pl.loop(1, N)
    def _(o):
        p = peer(o)
        arrived(ed_recv.at[p], ed_rsem.at[p], ed_ssem.at[0])

    edges = jnp.zeros((16, ACT), F32)
    for q in range(N):
        edges += ed_recv[q].astype(F32)
    for k in range(2):
        for t in range(6):
            out_ref[t, k : k + 1, :] = edges[8 * k + t : 8 * k + t + 1, :]

    @pl.loop(1, N)
    def _(o):
        ed_copy(peer(o)).wait_send()

    @pl.when(s < TOP)
    def _():
        e1_copy().wait_send()

    @pl.when(s >= 1)
    def _():
        @pl.loop(1, N)
        def _(o):
            sc_copy(o).wait_send()

    @pl.when(s == TOP)
    def _():
        pair_copy(0).wait_send()
        pair_copy(1).wait_send()
        seed_copy().wait_send()
        for o in range(4):
            for h in range(2):
                u_copy(h, o).wait_send()

        @pl.loop(0, N)
        def _(p):
            mix_copy(p).wait_send()

    @pl.when(second)
    def _():
        for items in u_forwards:
            for item in items:
                u_forward(*item).wait_send()

    @pl.when((s >= 1) & (s < TOP))
    def _():
        gain_copy().wait_send()

        for p in range(N):
            @pl.when(feeds_join)
            def _():
                v_copy_both(p).wait_send()

            @pl.when(feeds_spread)
            def _():
                v_copy_one(p).wait_send()

    @pl.when(feeds_spread)
    def _():
        hop_copy(grad_own).wait_send()
        stage_copy().wait_send()

    @pl.when(feeds_join)
    def _():
        for o in range(4):
            for h in range(2):
                full_copy(h, o).wait_send()
        for d in range(8):
            whole_copy(d).wait_send()

    @pl.when(spreads)
    def _():
        @pl.loop(1, N)
        def _(o):
            wv_copy(o).wait_send()

        for item in own_sends + sum(row_sends, []) + sum(col_sends, []):
            half_copy(*item).wait_send()


def body(
    attn_logits, out_weight, value_weight, norm_gain, norm_scale, target_encoder,
    target_ids, target_token, decoder, source_ids, source_values,
):
    vmem = pl.BlockSpec(memory_space=pltpu.VMEM)
    hbm = pl.BlockSpec(memory_space=pltpu.HBM)
    dma = pltpu.SemaphoreType.DMA
    out = pl.pallas_call(
        chain_kernel,
        out_shape=jax.ShapeDtypeStruct((6, 2, ACT), F32),
        in_specs=[hbm] * 11,
        out_specs=vmem,
        scratch_shapes=[
            pltpu.VMEM((40, 16384), BF16),
            pltpu.VMEM((1, 6), F32),
            pltpu.VMEM((HEADS_HERE, TOK, TOK), BF16),
            pltpu.VMEM((1, 5120), F32),
            pltpu.SMEM((2,), jnp.int32),
            pltpu.SMEM((2,), jnp.int32),
            pltpu.VMEM((TOK, ACT), jnp.int32),
            pltpu.VMEM((TOK, ACT), F32),
            pltpu.VMEM((8, 256), F32),
            pltpu.VMEM((8, 128), F32),
            pltpu.VMEM((512, 5120), BF16),
            pltpu.VMEM((5120, 512), BF16),
            pltpu.VMEM((FEATS, 5120), BF16),
            pltpu.VMEM((1024, WIDE), BF16),
            pltpu.VMEM((1024, 5120), BF16),
            pltpu.VMEM((1024, FEATS), BF16),
            pltpu.VMEM((N, TOK, WIDE), BF16),
            pltpu.VMEM((TOK, WIDE), BF16),
            pltpu.VMEM((TOK, WIDE), BF16),
            pltpu.VMEM((2, TOK, HD), BF16),
            pltpu.VMEM((N, 2, TOK, HD), BF16),
            pltpu.VMEM((2 * TOK, 1024), BF16),
            pltpu.VMEM((2 * TOK, HEADS_HERE * HD), F32),
            pltpu.VMEM((N, 8, 128), F32),
            pltpu.VMEM((TOK, 128), F32),
            pltpu.VMEM((8, 8, 256), F32),
            pltpu.VMEM((16, 256), BF16),
            pltpu.VMEM((N, 16, 256), BF16),
            pltpu.VMEM((TOK, HEADS_HERE * HD), BF16),
            pltpu.VMEM((HEADS_HERE * HD, 2 * HD), BF16),
            pltpu.VMEM((128, 128), F32),
            pltpu.VMEM((2 * TOK, FEATS), F32),
            pltpu.VMEM((N, 16, ACT), BF16),
            pltpu.VMEM((N, 16, ACT), BF16),
            dma((12,)),
            dma, dma,
            dma((N,)), dma((N,)),
            dma((2 * N,)), dma((2 * N,)),
            dma((N,)), dma((N,)),
            dma, dma((8,)),
            dma((N,)), dma((N,)),
            dma((N,)), dma((N,)),
            dma((3 * N,)), dma((2 * N,)),
            dma, dma,
            dma((8,)), dma((8,)),
            dma((N,)), dma((N,)),
            pltpu.VMEM((16, 2560), BF16),
            pltpu.VMEM((16, 2560), F32),
            pltpu.VMEM((16, 2560), BF16),
            pltpu.VMEM((N + 1, 16, 2560), BF16),
            pltpu.VMEM((TOK, HD), BF16),
            pltpu.VMEM((N, TOK, HD), BF16),
            pltpu.VMEM((2, 2 * TOK, 2 * HD), BF16),
            pltpu.VMEM((64, 5120), BF16),
            dma, dma,
            dma((2,)), dma((2,)),
            dma((40,)), dma((2 * N,)),
            dma((N,)), dma((N,)),
            dma, dma,
        ],
        compiler_params=pltpu.CompilerParams(
            collective_id=0, has_side_effects=True, vmem_limit_bytes=63 * 2**20
        ),
        name="chain",
    )(
        target_encoder.T, norm_scale, attn_logits[0], norm_gain, target_ids, target_token,
        source_ids[0], source_values[0],
        out_weight[0], value_weight[0], decoder[0],
    )
    return out[None]


def solution(mesh):
    return jax.shard_map(
        body,
        mesh=mesh,
        in_specs=(
            P("section", "tensor", None, None),
            P("section", "tensor", None),
            P("section", "tensor", None),
            P("section", None),
            P("section", "tensor"),
            P(None, ("section", "tensor")),
            P(),
            P(),
            P("section", "tensor", None),
            P("section", None, None),
            P("section", None, None),
        ),
        out_specs=P("section", "tensor", None, None),
        check_vma=False,
    )
```

```python
import jax
import jax.numpy as jnp
from jax import lax
from jax.experimental import pallas as pl
from jax.experimental.pallas import tpu as pltpu
from jax.sharding import PartitionSpec as P

MESH = pl.DeviceIdType.MESH
F32 = jnp.float32
BF16 = jnp.bfloat16

TOK = 96
N = 16
TOP = 7
HD = 128
WIDE = 640
HEADS_HERE = 4
ACT = 128
FEATS = 1024
FAR_FIRST = sorted(
    [(dy, dx) for dy in range(4) for dx in range(4)],
    key=lambda at: -min(at[0], 4 - at[0]) - min(at[1], 4 - at[1]),
)


def nt_dot(a, b):
    return lax.dot_general(a, b, (((1,), (1,)), ((), ())), preferred_element_type=F32)


def chain_kernel(
    enc_hbm, scale_hbm, logits_hbm, gain_hbm, want_hbm, tok_hbm, ids_hbm, vals_hbm,
    wo_hbm, wv_hbm, dec_hbm,
    out_ref,
    table, scale_raw, logits_ref, gain_up, want_ref, tok_ref, ids_ref, vals_ref,
    enc_ref, scale_ref,
    wo, wo_t, dec, wvs, wvf, joint, grad, grad_base, grad_own, v_send, v_recv, v_full, base,
    sc_recv, sc_rows, e1_recv, e2_send, e2_recv, pat, hcat, pad, acc, ed_send, ed_recv,
    local_sem, gain_ssem, gain_rsem, wv_ssem, wv_rsem, fw_ssem, fw_rsem, sc_ssem, sc_rsem,
    e1_ssem, e1_rsem, e2_ssem, e2_rsem, v_ssem, v_rsem, g_ssem, g_rsem, hop_ssem, hop_rsem,
    copy_ssem, copy_rsem, ed_ssem, ed_rsem,
    seeds, u_rows, u_send, u_recv, mix_send, mix_recv, mix,
    wv_stage, stage_ssem, stage_rsem, pair_ssem, pair_rsem, u_ssem, u_rsem, mix_ssem, mix_rsem, seed_ssem, seed_rsem,
):
    s = lax.axis_index("section")
    j = lax.axis_index("tensor")
    my_k = lax.rem(j, 2)
    my_d = j // 2
    row = j // 4
    col = lax.rem(j, 4)
    below = s - 1
    spreads = (s == 5) | (s == 3) | (s == 1)
    joins = (s == 4) | (s == 2) | (s == 0)
    second = s == TOP - 1
    feeds_spread = (s == 6) | (s == 4) | (s == 2)
    feeds_join = (s == 5) | (s == 3) | (s == 1)

    def peer(o):
        return lax.rem(j + o, N)

    def far_first(body):
        for dy, dx in FAR_FIRST:
            body(lax.rem(row + dy, 4) * 4 + lax.rem(col + dx, 4))

    def far_first_peers(body):
        for dy, dx in FAR_FIRST[:-1]:
            body(lax.rem(row + dy, 4) * 4 + lax.rem(col + dx, 4))

    def at_row(o):
        return row * 4 + lax.rem(col + o, 4)

    def at_col(o):
        return lax.rem(row + o, 4) * 4 + col

    def remote(src, dst, ssem, rsem, section, index):
        return pltpu.make_async_remote_copy(
            src_ref=src, dst_ref=dst, send_sem=ssem, recv_sem=rsem,
            device_id=(section, index), device_id_type=MESH,
        )

    def arrived(dst, rsem, ssem):
        remote(dst, dst, ssem, rsem, s, peer(1)).wait_recv()

    barrier = pltpu.get_barrier_semaphore()

    def greet(section, index):
        pl.semaphore_signal(barrier, inc=1, device_id=(section, index), device_id_type=MESH)

    @pl.when(s < TOP - 1)
    def _():
        greet(TOP, j)

    @pl.when(s == TOP)
    def _():
        for q in range(TOP - 1):
            greet(q, j)

    @pl.loop(1, N)
    def _(o):
        greet(s, peer(o))

    @pl.when(s < TOP)
    def _():
        @pl.loop(0, N)
        def _(p):
            greet(s + 1, p)

    @pl.when(s >= 1)
    def _():
        @pl.loop(0, N)
        def _(p):
            greet(below, p)

    small = [
        pltpu.make_async_copy(src, dst, local_sem.at[2 + i])
        for i, (src, dst) in enumerate([
            (want_hbm, want_ref), (enc_hbm, table), (scale_hbm, scale_raw),
            (logits_hbm, logits_ref), (tok_hbm, tok_ref),
            (ids_hbm, ids_ref), (vals_hbm, vals_ref),
        ])
    ]
    for copy in small:
        copy.start()
    wo_copy = pltpu.make_async_copy(wo_hbm, wo, local_sem.at[0])
    wo_copy.start()
    dec_copy = pltpu.make_async_copy(dec_hbm, dec, local_sem.at[1])
    dec_copy.start()

    small[0].wait()
    small[1].wait()
    first_lane = 40 * j - 128 * jnp.minimum((40 * j) // 128, 3)
    spot = lax.broadcasted_iota(jnp.int32, (40, 256), 1) - lax.broadcasted_iota(jnp.int32, (40, 256), 0)
    lane = lax.broadcasted_iota(jnp.int32, (40, 512), 1)

    def pick(i, found):
        part = table[:, pl.ds(pl.multiple_of(i * 512, 512), 512)].astype(F32)
        return tuple(
            found[k] + jnp.where(lane + i * 512 == want_ref[k], part, 0.0) for k in range(2)
        )

    found = lax.fori_loop(0, 32, pick, (jnp.zeros((40, 512), F32),) * 2)
    enc_ref[...] = jnp.zeros_like(enc_ref)
    for k in range(2):
        column = jnp.sum(found[k], axis=1, keepdims=True)
        enc_ref[k : k + 1, :] = jnp.sum(
            jnp.where(spot == first_lane, column, 0.0), axis=0, keepdims=True
        )
    small[2].wait()
    diagonal = lax.broadcasted_iota(jnp.int32, (8, 6), 0) == lax.broadcasted_iota(jnp.int32, (8, 6), 1)
    scale_ref[...] = jnp.broadcast_to(
        jnp.sum(jnp.where(diagonal, scale_raw[...], 0.0), axis=1, keepdims=True), (8, 128)
    )

    pl.semaphore_wait(
        barrier,
        15
        + jnp.where(s >= 1, N, 0)
        + jnp.where(s < TOP, N, 0)
        + jnp.where(s < TOP - 1, 1, 0)
        + jnp.where(s == TOP, TOP - 1, 0),
    )

    def e1_copy():
        return remote(enc_ref, e1_recv.at[s], e1_ssem, e1_rsem.at[s], TOP, j)

    @pl.when(s < TOP)
    def _():
        e1_copy().start()

    def sc_copy(o):
        return remote(scale_ref, sc_recv.at[j], sc_ssem.at[o], sc_rsem.at[j], s, peer(o))

    def gain_copy():
        return remote(gain_hbm, gain_up, gain_ssem, gain_rsem, below, j)

    def stage_copy():
        return remote(wv_hbm, wv_stage, stage_ssem, stage_rsem, below, j)

    own_rows = pl.ds(pl.multiple_of(j * 64, 64), 64)

    def columns_of(p):
        return wv_stage.at[:, pl.ds(pl.multiple_of((p // 2) * WIDE, 128), WIDE)]

    def wv_copy(o):
        p = peer(o)
        return remote(columns_of(p), wvs.at[own_rows], wv_ssem.at[o], wv_rsem.at[j], s, p)

    own_columns = pltpu.make_async_copy(columns_of(j), wvs.at[own_rows], local_sem.at[11])

    def half_rows(c, h):
        return wvf.at[pl.ds(pl.multiple_of(c * 64 + 32 * h, 32), 32)]

    def quarter_rows(c, h, q):
        return wvf.at[pl.ds(pl.multiple_of(c * 64 + 32 * h + 16 * q, 16), 16)]

    def first_ring(h, o):
        return at_col(o) if h else at_row(o)

    def second_ring(h, o):
        return at_row(o) if h else at_col(o)

    def on_rings(h, o1, o2):
        if h:
            return lax.rem(row + o1, 4) * 4 + lax.rem(col + o2, 4)
        return lax.rem(row + o2, 4) * 4 + lax.rem(col + o1, 4)

    def full_copy(h, o):
        return remote(
            wv_hbm.at[pl.ds(32 * h, 32)], half_rows(j, h),
            wv_ssem.at[4 * h + o], fw_rsem.at[4 * j + 2 * h], below, first_ring(h, o),
        )

    def pair_rows(h, k):
        return wvf.at[pl.ds(pl.multiple_of(k * 64 + 32 * h, 32), 32)]

    def pair_copy(h):
        return remote(
            wv_hbm.at[pl.ds(32 * h, 32)], pair_rows(h, my_k),
            pair_ssem.at[h], pair_rsem.at[h], s, j + 1 - 2 * my_k,
        )

    own_wv = pltpu.make_async_copy(
        wv_hbm, wvf.at[pl.ds(pl.multiple_of(my_k * 64, 64), 64)], local_sem.at[9]
    )
    own_gain = pltpu.make_async_copy(gain_hbm, gain_up, local_sem.at[10])

    @pl.when(s == TOP)
    def _():
        own_wv.start()
        own_gain.start()

    @pl.when((s >= 1) & (s < TOP))
    def _():
        gain_copy().start()

    @pl.when(s >= 1)
    def _():
        @pl.loop(1, N)
        def _(o):
            sc_copy(o).start()

    @pl.when(s == TOP)
    def _():
        pair_copy(0).start()

    @pl.when(feeds_spread)
    def _():
        stage_copy().start()

    @pl.when(feeds_join)
    def _():
        for o in (1, 3, 0):
            for h in range(2):
                full_copy(h, o).start()

    for copy in small[3:]:
        copy.wait()
    pad[...] = jnp.zeros_like(pad)
    hcat[...] = jnp.zeros_like(hcat)
    query = lax.broadcasted_iota(jnp.int32, (TOK, TOK), 0)
    key = lax.broadcasted_iota(jnp.int32, (TOK, TOK), 1)
    for h in range(HEADS_HERE):
        scores = jnp.where(key <= query, logits_ref[h].astype(F32), -jnp.inf)
        highest = jnp.max(scores, axis=-1, keepdims=True)
        weights = jnp.exp(scores - highest)
        pad[0:TOK, 0:TOK] = weights / jnp.sum(weights, axis=-1, keepdims=True)
        pat[:, h * HD : (h + 1) * HD] = pad[...].T[0:TOK, :].astype(BF16)

    @pl.when(spreads)
    def _():
        arrived(wv_stage, stage_rsem, stage_ssem)
        own_columns.start()

        @pl.loop(1, N)
        def _(o):
            wv_copy(o).start()

    def u_copy(h, o):
        part = u_recv.at[j, :, pl.ds(1280 * h, 1280)]
        return remote(
            u_send.at[:, pl.ds(1280 * h, 1280)], part,
            u_ssem.at[4 * h + o], u_rsem.at[2 * j + h], below, at_col(o) if h else at_row(o),
        )

    def mix_copy(p):
        return remote(mix_send, mix_recv.at[j], mix_ssem.at[p], mix_rsem.at[j], below, p)

    def spread_scales():
        @pl.loop(1, N)
        def _(o):
            p = peer(o)
            arrived(sc_recv.at[p], sc_rsem.at[p], sc_ssem.at[0])

        sc_recv[j] = scale_ref[...]
        for q in range(N):
            sc_rows[6 * q : 6 * q + 6, :] = sc_recv[q, 0:6, :]

    def seed_copy():
        return remote(seeds, u_recv.at[N], seed_ssem, seed_rsem, below, j)

    def hop_copy(src):
        return remote(src, grad_base, hop_ssem, hop_rsem, below, j)

    @pl.when(s == TOP)
    def _():
        e1_recv[TOP] = enc_ref[...]
        for q in range(TOP):
            arrived(e1_recv.at[q], e1_rsem.at[q], e1_ssem)
        rows = jnp.concatenate([e1_recv[:, 0, :], e1_recv[:, 1, :]], axis=0)
        e2_send[...] = rows.astype(BF16)
        e2_recv[j] = rows.astype(BF16)

        def e2_copy(o):
            return remote(e2_send, e2_recv.at[j], e2_ssem.at[o], e2_rsem.at[j], s, o)

        far_first_peers(lambda p: e2_copy(p).start())

        pair_copy(1).start()
        spread_scales()
        lane = lax.broadcasted_iota(jnp.int32, (TOK, HEADS_HERE * HD), 1)
        place = lax.broadcasted_iota(jnp.int32, (TOK, HD), 1) - 16 * lax.rem(j, 8)
        slab = jnp.zeros((TOK, HD), F32)
        for k in range(2):
            for h in range(HEADS_HERE):
                hit = lane == h * HD + tok_ref[k]
                chosen = jnp.sum(jnp.where(hit, pat[...].astype(F32), 0.0), axis=1, keepdims=True)
                spot = 4 * k + h
                slab = slab + jnp.where((place == spot) | (place == spot + 8), chosen, 0.0)
        mix_send[...] = (slab * sc_rows[...]).astype(BF16)
        far_first(lambda p: mix_copy(p).start())

        @pl.loop(1, N)
        def _(o):
            p = peer(o)
            arrived(e2_recv.at[p], e2_rsem.at[p], e2_ssem.at[o])

        blocks = [jnp.zeros((16, 128), F32) for _ in range(5)]
        for q in range(N):
            first = min(40 * q // 128, 3)
            piece = e2_recv[q].astype(F32)
            blocks[first] = blocks[first] + piece[:, 0:128]
            blocks[first + 1] = blocks[first + 1] + piece[:, 128:256]
        top_rows = jnp.concatenate(blocks, axis=1)
        seeds[...] = jnp.zeros_like(seeds)
        for d in range(4):
            cols = slice(d * WIDE, (d + 1) * WIDE)
            for k in range(2):
                low = top_rows[k * 8 + d : k * 8 + d + 1, :]
                high = top_rows[k * 8 + d + 4 : k * 8 + d + 5, :]
                seeds[k : k + 1, cols] = low.astype(BF16)
                seeds[8 + k : 9 + k, cols] = high.astype(BF16)
        seed_copy().start()
        wo_copy.wait()
        half = 2560
        low = nt_dot(seeds[...], wo[:, 0:half])
        high = nt_dot(seeds[...], wo[:, half:])
        rows = low[0:2] + high[8:10]
        parts = [
            rows[k : k + 1, h * HD : (h + 1) * HD] for k in range(2) for h in range(HEADS_HERE)
        ]
        head_rows = jnp.concatenate(parts, axis=0).astype(BF16)
        own_wv.wait()
        own_gain.wait()
        for h in range(2):
            arrived(pair_rows(h, 1 - my_k), pair_rsem.at[h], pair_ssem.at[h])
        for h in range(2):
            cols = slice(h * half, (h + 1) * half)
            mixed = jnp.dot(head_rows, wvf[0:128, cols], preferred_element_type=F32)
            u_rows[8 * h : 8 * h + 8, :] = mixed * gain_up[:, cols]
        u_send[...] = u_rows[...].astype(BF16)
        for o in (2, 1, 3, 0):
            for h in range(2):
                u_copy(h, o).start()

        token = lax.broadcasted_iota(jnp.int32, (TOK, WIDE), 0)
        for k in range(2):
            hit = token == tok_ref[k]
            for d in range(8):
                one = jnp.broadcast_to(top_rows[k * 8 + d : k * 8 + d + 1, :], (TOK, WIDE))
                grad[2 * d + k] = jnp.where(hit, one, 0.0).astype(BF16)

        @pl.loop(1, N)
        def _(o):
            e2_copy(peer(o)).wait_send()

    @pl.when((s >= 1) & (s < TOP))
    def _():
        spread_scales()

    @pl.when(s < TOP)
    def _():
        wo_copy.wait()

    dec_copy.wait()

    def transpose_weights():
        @pl.loop(0, 40)
        def _(i):
            part = pl.ds(pl.multiple_of(i * 128, 128), 128)
            wo_t[part, :] = wo[:, part].T

    sent = []

    def pass_half(c, h, to):
        sem = fw_ssem.at[len(sent)]
        copy = remote(half_rows(c, h), half_rows(c, h), sem, fw_rsem.at[4 * c + 2 * h], s, to)
        copy.start()
        sent.append(copy)

    def pass_quarter(c, h, q, to):
        sem = fw_ssem.at[len(sent)]
        part = quarter_rows(c, h, q)
        copy = remote(part, part, sem, fw_rsem.at[4 * c + 2 * h + q], s, to)
        copy.start()
        sent.append(copy)

    def half_here(c, h):
        arrived(half_rows(c, h), fw_rsem.at[4 * c + 2 * h], fw_ssem.at[0])

    def quarters_here(c, h):
        for q in range(2):
            arrived(quarter_rows(c, h, q), fw_rsem.at[4 * c + 2 * h + q], fw_ssem.at[0])

    @pl.when(joins)
    def _():
        for o in (0, 1, 3):
            for h in range(2):
                c = on_rings(h, o, 0)
                half_here(c, h)
                if o == 3:
                    pass_quarter(c, h, 0, first_ring(h, 1))
                if o == 1:
                    pass_quarter(c, h, 1, first_ring(h, 3))
                pass_half(c, h, second_ring(h, 1))
                pass_half(c, h, second_ring(h, 3))
        for h in range(2):
            c = on_rings(h, 2, 0)
            quarters_here(c, h)
            pass_half(c, h, second_ring(h, 1))
            pass_half(c, h, second_ring(h, 3))
        arrived(gain_up, gain_rsem, gain_ssem)
        for step, o in enumerate((0, 1, 3, 2)):
            @pl.when(s >= 2)
            def _():
                @pl.loop(10 * step, 10 * step + 10)
                def _(i):
                    part = pl.ds(pl.multiple_of(i * 128, 128), 128)
                    scaled = wo[:, part].astype(F32) * gain_up[:, part]
                    wo_t[part, :] = scaled.T.astype(BF16)

            for h in range(2):
                c = on_rings(h, o, 3)
                half_here(c, h)
                pass_quarter(c, h, 0, second_ring(h, 1))
                c = on_rings(h, o, 1)
                half_here(c, h)
                pass_quarter(c, h, 1, second_ring(h, 3))
        for o in (0, 1, 3, 2):
            for h in range(2):
                quarters_here(on_rings(h, o, 2), h)
        for copy in sent:
            copy.wait_send()

        @pl.when(s == 0)
        def _():
            @pl.loop(0, 64)
            def _(i):
                part = pl.ds(pl.multiple_of(i * 16, 16), 16)
                wvf[part, :] = (wvf[part, :].astype(F32) * gain_up[...]).astype(BF16)

    @pl.when(spreads)
    def _():
        transpose_weights()

    @pl.when((s == 4) | (s == 2))
    def _():
        @pl.loop(0, 2)
        def _(i):
            part = pl.ds(pl.multiple_of(i * 512, 512), 512)
            total = jnp.zeros((512, HEADS_HERE * HD), F32)
            for d in range(8):
                cols = slice(d * WIDE, (d + 1) * WIDE)
                total += jnp.dot(wvf[part, cols], wo_t[cols, :], preferred_element_type=F32)
            joint[part, 0 : HEADS_HERE * HD] = total.astype(BF16)

    @pl.when(s == 0)
    def _():
        @pl.loop(0, 8)
        def _(i):
            part = pl.ds(pl.multiple_of(i * 128, 128), 128)
            total = jnp.zeros((128, FEATS), F32)
            for d in range(8):
                cols = slice(d * WIDE, (d + 1) * WIDE)
                total += nt_dot(wvf[part, cols], dec[:, cols])
            joint[part, :] = total.astype(BF16)

    def wait_values():
        @pl.loop(0, N)
        def _(p):
            @pl.when(spreads)
            def _():
                arrived(v_recv.at[p, 0], v_rsem.at[p], v_ssem.at[0])

            @pl.when(joins)
            def _():
                arrived(v_recv.at[p], v_rsem.at[p], v_ssem.at[0])

    def value_grad(k):
        pieces = []
        for q in range(8):
            both = v_recv[2 * q, k].astype(F32) + v_recv[2 * q + 1, k].astype(F32)
            pieces.append(both.astype(BF16))
        return jnp.concatenate(pieces, axis=1)

    def v_copy_both(p):
        return remote(v_send, v_recv.at[j], v_ssem.at[p], v_rsem.at[j], below, p)

    def v_copy_one(p):
        return remote(v_send.at[lax.rem(p, 2)], v_recv.at[j, 0], v_ssem.at[p], v_rsem.at[j], below, p)

    def send_values(head_grad):
        for k in range(2):
            for h in range(HEADS_HERE):
                hcat[h * HD : h * HD + TOK, k * HD : (k + 1) * HD] = head_grad[
                    k * TOK : (k + 1) * TOK, h * HD : (h + 1) * HD
                ]
        part = jnp.dot(pat[...], hcat[...], preferred_element_type=F32)
        for k in range(2):
            v_send[k] = (part[:, k * HD : (k + 1) * HD] * sc_rows[...]).astype(BF16)

        @pl.when(feeds_join)
        def _():
            far_first(lambda p: v_copy_both(p).start())

        @pl.when(feeds_spread)
        def _():
            far_first(lambda p: v_copy_one(p).start())

    def half_copy(c, h, to, sem):
        part = grad.at[c, pl.ds(48 * h, 48)]
        return remote(part, part, g_ssem.at[sem], g_rsem.at[2 * c + h], s, to)

    def half_arrived(c, h):
        arrived(grad.at[c, pl.ds(48 * h, 48)], g_rsem.at[2 * c + h], g_ssem.at[0])

    own_sends, row_sends, col_sends = [], [], []
    for o in (2, 1, 3):
        own_sends.append((j, 0, at_row(o), o))
        own_sends.append((j, 1, at_col(o), 4 + o))
    for o in (2, 1, 3):
        own_sends.append((j, 0, at_col(o), 8 + o))
        own_sends.append((j, 1, at_row(o), 12 + o))
    for o in (1, 3, 2):
        row_sends.append([(at_row(o), 0, at_col(q), 16 + 4 * o + q) for q in (2, 1, 3)])
        col_sends.append([(at_col(o), 1, at_row(q), 32 + 4 * o + q) for q in (2, 1, 3)])

    own_cols = pl.ds(pl.multiple_of(my_d * WIDE, 128), WIDE)

    def make_chunk():
        wait_values()
        mixed = jnp.dot(value_grad(0), wvs[...], preferred_element_type=F32)
        grad[j] = (grad_base[...].astype(F32) + mixed * gain_up[:, own_cols]).astype(BF16)
        for item in own_sends:
            half_copy(*item).start()

    def forward(k):
        for items in row_sends:
            c = items[0][0]

            @pl.when(lax.rem(c, 2) == k)
            def _():
                half_arrived(c, 0)
                for item in items:
                    half_copy(*item).start()

        @pl.when(my_k == k)
        def _():
            for items in col_sends:
                half_arrived(items[0][0], 1)
                for item in items:
                    half_copy(*item).start()

    def wait_chunk(c):
        @pl.when(c // 4 != row)
        def _():
            half_arrived(c, 0)

        @pl.when(c % 4 != col)
        def _():
            half_arrived(c, 1)

    def whole_copy(d):
        part = grad.at[pl.ds(2 * d, 2)]
        return remote(part, part, copy_ssem.at[d], copy_rsem.at[d], below, j)

    def whole_arrived(d):
        arrived(grad.at[pl.ds(2 * d, 2)], copy_rsem.at[d], copy_ssem.at[0])

    def head_grad_of(at_chunk, dot):
        total = jnp.zeros((2 * TOK, HEADS_HERE * HD), F32)
        for d in range(8):
            at_chunk(d)
            both = grad[2 * d : 2 * d + 2].reshape(2 * TOK, WIDE)
            total += dot(both, slice(d * WIDE, (d + 1) * WIDE))
        return total

    @pl.when(spreads)
    def _():
        arrived(gain_up, gain_rsem, gain_ssem)
        own_columns.wait()

        @pl.loop(1, N)
        def _(o):
            p = peer(o)
            rows = pl.ds(pl.multiple_of(p * 64, 64), 64)
            arrived(wvs.at[rows], wv_rsem.at[p], wv_ssem.at[0])

        arrived(grad_base, hop_rsem, hop_ssem)

    @pl.when(spreads)
    def _():
        make_chunk()
        forward(0)
        forward(1)

        def take_chunks(d):
            wait_chunk(2 * d)
            wait_chunk(2 * d + 1)
            whole_copy(d).start()

        send_values(head_grad_of(
            take_chunks,
            lambda both, part: jnp.dot(both, wo_t[part, :], preferred_element_type=F32),
        ).astype(BF16))

    u_forwards = []
    for o in (0, 1, 3, 2):
        u_forwards.append([(at_row(o), 0, at_col(q), 8 + 4 * o + q) for q in (2, 1, 3)])
        u_forwards.append([(at_col(o), 1, at_row(q), 24 + 4 * o + q) for q in (2, 1, 3)])

    def u_half(c, h):
        return u_recv.at[c, :, pl.ds(1280 * h, 1280)]

    def u_forward(c, h, to, sem):
        return remote(u_half(c, h), u_half(c, h), u_ssem.at[sem], u_rsem.at[2 * c + h], s, to)

    @pl.when(second)
    def _():
        transpose_weights()
        for items in u_forwards:
            c, h = items[0][0], items[0][1]
            arrived(u_half(c, h), u_rsem.at[2 * c + h], u_ssem.at[0])
            for item in items:
                u_forward(*item).start()

        @pl.loop(0, N)
        def _(p):
            arrived(mix_recv.at[p], mix_rsem.at[p], mix_ssem.at[0])

        arrived(u_recv.at[N], seed_rsem, seed_ssem)
        kind = lax.broadcasted_iota(jnp.int32, (TOK, HD), 1) & 15
        for t in range(2):
            tile = jnp.zeros((TOK, HD), F32)
            for q in range(8):
                tile = tile + mix_recv[8 * t + q].astype(F32)
            for h in range(2):
                for k in range(2):
                    keep = (kind >> 2) == 2 * h + k
                    mix[h, k * TOK : (k + 1) * TOK, t * HD : (t + 1) * HD] = jnp.where(
                        keep, tile, 0.0
                    ).astype(BF16)

        @pl.loop(0, N)
        def _(c):
            @pl.when(c // 4 != row)
            def _():
                arrived(u_half(c, 0), u_rsem.at[2 * c], u_ssem.at[0])

            @pl.when(lax.rem(c, 4) != col)
            def _():
                arrived(u_half(c, 1), u_rsem.at[2 * c + 1], u_ssem.at[0])

        half = 2560
        flat = u_recv[...].reshape(16 * (N + 1), half)
        low = jnp.dot(flat, wo_t[0:half, :], preferred_element_type=F32)
        high = jnp.dot(flat, wo_t[half:, :], preferred_element_type=F32)
        total = jnp.dot(mix[0], low[0:256].astype(BF16), preferred_element_type=F32)
        total += jnp.dot(mix[1], high[0:256].astype(BF16), preferred_element_type=F32)
        token = lax.broadcasted_iota(jnp.int32, (TOK, HEADS_HERE * HD), 0)
        parts = []
        for k in range(2):
            one = low[256 + k : 257 + k] + high[264 + k : 265 + k]
            parts.append(
                total[k * TOK : (k + 1) * TOK] + jnp.where(token == tok_ref[k], one, 0.0)
            )
        send_values(jnp.concatenate(parts, axis=0).astype(BF16))
        token = lax.broadcasted_iota(jnp.int32, (TOK, WIDE), 0)
        for d in range(8):
            h, cols = d // 4, slice((d % 4) * WIDE, (d % 4 + 1) * WIDE)
            head_rows = u_recv[0:N, :, cols].reshape(16 * N, WIDE)
            mixed = jnp.dot(mix[h], head_rows, preferred_element_type=F32)
            for k in range(2):
                one = u_recv[N, 8 * h + k : 8 * h + k + 1, cols].astype(F32)
                grad[2 * d + k] = (
                    mixed[k * TOK : (k + 1) * TOK] + jnp.where(token == tok_ref[k], one, 0.0)
                ).astype(BF16)
        hop_copy(grad.at[j]).start()

    @pl.when((s == 4) | (s == 2))
    def _():
        base[...] = head_grad_of(whole_arrived, lambda both, part: nt_dot(both, wo[:, part]))
        wait_values()
        for k in range(2):
            v_full[k * TOK : (k + 1) * TOK, :] = value_grad(k)
        mixed = jnp.dot(
            v_full[pl.ds(pl.multiple_of(my_k * TOK, TOK), TOK), :], wvf[:, own_cols],
            preferred_element_type=F32,
        )
        grad_own[...] = (grad[j].astype(F32) + mixed * gain_up[:, own_cols]).astype(BF16)
        hop_copy(grad_own).start()
        total = base[...] + jnp.dot(
            v_full[...], joint[:, 0 : HEADS_HERE * HD], preferred_element_type=F32
        )
        send_values(total.astype(BF16))
        for d in range(8):
            mixed = jnp.dot(
                v_full[...], wvf[:, d * WIDE : (d + 1) * WIDE], preferred_element_type=F32
            )
            mixed = mixed * gain_up[:, d * WIDE : (d + 1) * WIDE]
            for k in range(2):
                grad[2 * d + k] = (
                    grad[2 * d + k].astype(F32) + mixed[k * TOK : (k + 1) * TOK]
                ).astype(BF16)

    @pl.when(s == 0)
    def _():
        for d in range(8):
            whole_arrived(d)

    for d in range(8):
        both = grad[2 * d : 2 * d + 2].reshape(2 * TOK, WIDE)
        term = nt_dot(both, dec[:, d * WIDE : (d + 1) * WIDE])
        if d == 0:
            acc[...] = term
        else:
            acc[...] += term

    @pl.when(s == 0)
    def _():
        wait_values()
        for k in range(2):
            v_full[k * TOK : (k + 1) * TOK, :] = value_grad(k)
        acc[...] += jnp.dot(v_full[...], joint[...], preferred_element_type=F32)

    local_id = ids_ref[...] - j * FEATS
    lane = local_id & 127
    block = local_id >> 7
    chosen = []
    for k in range(2):
        picked = jnp.zeros((TOK, ACT), F32)
        for b in range(8):
            near = acc[k * TOK : (k + 1) * TOK, b * 128 : (b + 1) * 128]
            got = jnp.take_along_axis(near, lane, axis=1)
            picked = jnp.where(block == b, got, picked)
        chosen.append((picked * vals_ref[...]).astype(BF16))
    terms = jnp.concatenate(chosen, axis=0)
    e_row = lax.broadcasted_iota(jnp.int32, (256, 192), 0)
    e_col = lax.broadcasted_iota(jnp.int32, (256, 192), 1)
    slot = e_row & 7
    source = ((e_row >> 3) & 1) * TOK + (e_row >> 4) * 6 + slot
    placing = jnp.where((e_col == source) & (slot < 6), 1.0, 0.0).astype(BF16)
    placed = jnp.dot(placing, terms, preferred_element_type=F32).astype(BF16)
    for q in range(N):
        ed_send[q] = placed[16 * q : 16 * q + 16, :]

    def ed_copy(p):
        return remote(ed_send.at[p], ed_recv.at[j], ed_ssem.at[p], ed_rsem.at[j], s, p)

    far_first_peers(lambda p: ed_copy(p).start())

    ed_recv[j] = ed_send[j]

    @pl.loop(1, N)
    def _(o):
        p = peer(o)
        arrived(ed_recv.at[p], ed_rsem.at[p], ed_ssem.at[0])

    edges = jnp.zeros((16, ACT), F32)
    for q in range(N):
        edges += ed_recv[q].astype(F32)
    for k in range(2):
        for t in range(6):
            out_ref[t, k : k + 1, :] = edges[8 * k + t : 8 * k + t + 1, :]

    @pl.loop(1, N)
    def _(o):
        ed_copy(peer(o)).wait_send()

    @pl.when(s < TOP)
    def _():
        e1_copy().wait_send()

    @pl.when(s >= 1)
    def _():
        @pl.loop(1, N)
        def _(o):
            sc_copy(o).wait_send()

    @pl.when(s == TOP)
    def _():
        pair_copy(0).wait_send()
        pair_copy(1).wait_send()
        seed_copy().wait_send()
        for o in range(4):
            for h in range(2):
                u_copy(h, o).wait_send()

        @pl.loop(0, N)
        def _(p):
            mix_copy(p).wait_send()

    @pl.when(second)
    def _():
        for items in u_forwards:
            for item in items:
                u_forward(*item).wait_send()

    @pl.when((s >= 1) & (s < TOP))
    def _():
        gain_copy().wait_send()

        for p in range(N):
            @pl.when(feeds_join)
            def _():
                v_copy_both(p).wait_send()

            @pl.when(feeds_spread)
            def _():
                v_copy_one(p).wait_send()

    @pl.when(feeds_spread)
    def _():
        hop_copy(grad_own).wait_send()
        stage_copy().wait_send()

    @pl.when(feeds_join)
    def _():
        for o in (0, 1, 3):
            for h in range(2):
                full_copy(h, o).wait_send()
        for d in range(8):
            whole_copy(d).wait_send()

    @pl.when(spreads)
    def _():
        @pl.loop(1, N)
        def _(o):
            wv_copy(o).wait_send()

        for item in own_sends + sum(row_sends, []) + sum(col_sends, []):
            half_copy(*item).wait_send()


def body(
    attn_logits, out_weight, value_weight, norm_gain, norm_scale, target_encoder,
    target_ids, target_token, decoder, source_ids, source_values,
):
    vmem = pl.BlockSpec(memory_space=pltpu.VMEM)
    hbm = pl.BlockSpec(memory_space=pltpu.HBM)
    dma = pltpu.SemaphoreType.DMA
    out = pl.pallas_call(
        chain_kernel,
        out_shape=jax.ShapeDtypeStruct((6, 2, ACT), F32),
        in_specs=[hbm] * 11,
        out_specs=vmem,
        scratch_shapes=[
            pltpu.VMEM((40, 16384), BF16),
            pltpu.VMEM((1, 6), F32),
            pltpu.VMEM((HEADS_HERE, TOK, TOK), BF16),
            pltpu.VMEM((1, 5120), F32),
            pltpu.SMEM((2,), jnp.int32),
            pltpu.SMEM((2,), jnp.int32),
            pltpu.VMEM((TOK, ACT), jnp.int32),
            pltpu.VMEM((TOK, ACT), F32),
            pltpu.VMEM((8, 256), F32),
            pltpu.VMEM((8, 128), F32),
            pltpu.VMEM((512, 5120), BF16),
            pltpu.VMEM((5120, 512), BF16),
            pltpu.VMEM((FEATS, 5120), BF16),
            pltpu.VMEM((1024, WIDE), BF16),
            pltpu.VMEM((1024, 5120), BF16),
            pltpu.VMEM((1024, FEATS), BF16),
            pltpu.VMEM((N, TOK, WIDE), BF16),
            pltpu.VMEM((TOK, WIDE), BF16),
            pltpu.VMEM((TOK, WIDE), BF16),
            pltpu.VMEM((2, TOK, HD), BF16),
            pltpu.VMEM((N, 2, TOK, HD), BF16),
            pltpu.VMEM((2 * TOK, 1024), BF16),
            pltpu.VMEM((2 * TOK, HEADS_HERE * HD), F32),
            pltpu.VMEM((N, 8, 128), F32),
            pltpu.VMEM((TOK, 128), F32),
            pltpu.VMEM((8, 8, 256), F32),
            pltpu.VMEM((16, 256), BF16),
            pltpu.VMEM((N, 16, 256), BF16),
            pltpu.VMEM((TOK, HEADS_HERE * HD), BF16),
            pltpu.VMEM((HEADS_HERE * HD, 2 * HD), BF16),
            pltpu.VMEM((128, 128), F32),
            pltpu.VMEM((2 * TOK, FEATS), F32),
            pltpu.VMEM((N, 16, ACT), BF16),
            pltpu.VMEM((N, 16, ACT), BF16),
            dma((12,)),
            dma, dma,
            dma((N,)), dma((N,)),
            dma((3 * N,)), dma((4 * N,)),
            dma((N,)), dma((N,)),
            dma, dma((8,)),
            dma((N,)), dma((N,)),
            dma((N,)), dma((N,)),
            dma((3 * N,)), dma((2 * N,)),
            dma, dma,
            dma((8,)), dma((8,)),
            dma((N,)), dma((N,)),
            pltpu.VMEM((16, 2560), BF16),
            pltpu.VMEM((16, 2560), F32),
            pltpu.VMEM((16, 2560), BF16),
            pltpu.VMEM((N + 1, 16, 2560), BF16),
            pltpu.VMEM((TOK, HD), BF16),
            pltpu.VMEM((N, TOK, HD), BF16),
            pltpu.VMEM((2, 2 * TOK, 2 * HD), BF16),
            pltpu.VMEM((64, 5120), BF16),
            dma, dma,
            dma((2,)), dma((2,)),
            dma((40,)), dma((2 * N,)),
            dma((N,)), dma((N,)),
            dma, dma,
        ],
        compiler_params=pltpu.CompilerParams(
            collective_id=0, has_side_effects=True, vmem_limit_bytes=63 * 2**20
        ),
        name="chain",
    )(
        target_encoder.T, norm_scale, attn_logits[0], norm_gain, target_ids, target_token,
        source_ids[0], source_values[0],
        out_weight[0], value_weight[0], decoder[0],
    )
    return out[None]


def solution(mesh):
    return jax.shard_map(
        body,
        mesh=mesh,
        in_specs=(
            P("section", "tensor", None, None),
            P("section", "tensor", None),
            P("section", "tensor", None),
            P("section", None),
            P("section", "tensor"),
            P(None, ("section", "tensor")),
            P(),
            P(),
            P("section", "tensor", None),
            P("section", None, None),
            P("section", None, None),
        ),
        out_specs=P("section", "tensor", None, None),
        check_vma=False,
    )
```

```python
import jax
import jax.numpy as jnp
from jax import lax
from jax.experimental import pallas as pl
from jax.experimental.pallas import tpu as pltpu
from jax.sharding import PartitionSpec as P

MESH = pl.DeviceIdType.MESH
F32 = jnp.float32
BF16 = jnp.bfloat16

TOK = 96
N = 16
TOP = 7
HD = 128
WIDE = 640
HEADS_HERE = 4
ACT = 128
FEATS = 1024
FAR_FIRST = sorted(
    [(dy, dx) for dy in range(4) for dx in range(4)],
    key=lambda at: -min(at[0], 4 - at[0]) - min(at[1], 4 - at[1]),
)


def nt_dot(a, b):
    return lax.dot_general(a, b, (((1,), (1,)), ((), ())), preferred_element_type=F32)


def chain_kernel(
    enc_hbm, scale_hbm, logits_hbm, gain_hbm, want_hbm, tok_hbm, ids_hbm, vals_hbm,
    wo_hbm, wv_hbm, dec_hbm,
    out_ref,
    table, scale_raw, logits_ref, gain_up, want_ref, tok_ref, ids_ref, vals_ref,
    enc_ref, scale_ref,
    wo, wo_t, dec, wvs, wvf, joint, grad, grad_base, grad_own, v_send, v_recv, v_full, base,
    sc_recv, sc_rows, e1_recv, e2_send, e2_recv, pat, hcat, pad, acc, ed_send, ed_recv,
    local_sem, gain_ssem, gain_rsem, wv_ssem, wv_rsem, fw_ssem, fw_rsem, sc_ssem, sc_rsem,
    e1_ssem, e1_rsem, e2_ssem, e2_rsem, v_ssem, v_rsem, g_ssem, g_rsem, hop_ssem, hop_rsem,
    copy_ssem, copy_rsem, ed_ssem, ed_rsem,
    seeds, u_rows, u_send, u_recv, mix_send, mix_recv, mix,
    wv_stage, stage_ssem, stage_rsem, pair_ssem, pair_rsem, u_ssem, u_rsem, mix_ssem, mix_rsem, seed_ssem, seed_rsem,
):
    s = lax.axis_index("section")
    j = lax.axis_index("tensor")
    my_k = lax.rem(j, 2)
    my_d = j // 2
    row = j // 4
    col = lax.rem(j, 4)
    below = s - 1
    spreads = (s == 5) | (s == 3) | (s == 1)
    joins = (s == 4) | (s == 2) | (s == 0)
    second_index = TOP - 1
    second = s == second_index
    feeds_spread = (s == 4) | (s == 2)
    feeds_join = (s == 5) | (s == 3) | (s == 1)

    def peer(o):
        return lax.rem(j + o, N)

    def far_first(body):
        for dy, dx in FAR_FIRST:
            body(lax.rem(row + dy, 4) * 4 + lax.rem(col + dx, 4))

    def far_first_peers(body):
        for dy, dx in FAR_FIRST[:-1]:
            body(lax.rem(row + dy, 4) * 4 + lax.rem(col + dx, 4))

    def at_row(o):
        return row * 4 + lax.rem(col + o, 4)

    def at_col(o):
        return lax.rem(row + o, 4) * 4 + col

    def remote(src, dst, ssem, rsem, section, index):
        return pltpu.make_async_remote_copy(
            src_ref=src, dst_ref=dst, send_sem=ssem, recv_sem=rsem,
            device_id=(section, index), device_id_type=MESH,
        )

    def arrived(dst, rsem, ssem):
        remote(dst, dst, ssem, rsem, s, peer(1)).wait_recv()

    barrier = pltpu.get_barrier_semaphore()

    def greet(section, index):
        pl.semaphore_signal(barrier, inc=1, device_id=(section, index), device_id_type=MESH)

    @pl.when(s < TOP - 1)
    def _():
        greet(TOP, j)

    @pl.when(s == TOP)
    def _():
        for q in range(TOP - 1):
            greet(q, j)

    @pl.loop(1, N)
    def _(o):
        greet(s, peer(o))

    @pl.when(s < TOP)
    def _():
        @pl.loop(0, N)
        def _(p):
            greet(s + 1, p)

    @pl.when(s >= 1)
    def _():
        @pl.loop(0, N)
        def _(p):
            greet(below, p)

    small = [
        pltpu.make_async_copy(src, dst, local_sem.at[2 + i])
        for i, (src, dst) in enumerate([
            (want_hbm, want_ref), (enc_hbm, table), (scale_hbm, scale_raw),
            (logits_hbm, logits_ref), (tok_hbm, tok_ref),
            (ids_hbm, ids_ref), (vals_hbm, vals_ref),
        ])
    ]
    for copy in small:
        copy.start()
    wo_copy = pltpu.make_async_copy(wo_hbm, wo, local_sem.at[0])
    wo_copy.start()
    dec_copy = pltpu.make_async_copy(dec_hbm, dec, local_sem.at[1])
    dec_copy.start()

    small[0].wait()
    small[1].wait()
    first_lane = 40 * j - 128 * jnp.minimum((40 * j) // 128, 3)
    spot = lax.broadcasted_iota(jnp.int32, (40, 256), 1) - lax.broadcasted_iota(jnp.int32, (40, 256), 0)
    lane = lax.broadcasted_iota(jnp.int32, (40, 512), 1)

    def pick(i, found):
        part = table[:, pl.ds(pl.multiple_of(i * 512, 512), 512)].astype(F32)
        return tuple(
            found[k] + jnp.where(lane + i * 512 == want_ref[k], part, 0.0) for k in range(2)
        )

    found = lax.fori_loop(0, 32, pick, (jnp.zeros((40, 512), F32),) * 2)
    enc_ref[...] = jnp.zeros_like(enc_ref)
    for k in range(2):
        column = jnp.sum(found[k], axis=1, keepdims=True)
        enc_ref[k : k + 1, :] = jnp.sum(
            jnp.where(spot == first_lane, column, 0.0), axis=0, keepdims=True
        )
    small[2].wait()
    diagonal = lax.broadcasted_iota(jnp.int32, (8, 6), 0) == lax.broadcasted_iota(jnp.int32, (8, 6), 1)
    scale_ref[...] = jnp.broadcast_to(
        jnp.sum(jnp.where(diagonal, scale_raw[...], 0.0), axis=1, keepdims=True), (8, 128)
    )

    pl.semaphore_wait(
        barrier,
        15
        + jnp.where(s >= 1, N, 0)
        + jnp.where(s < TOP, N, 0)
        + jnp.where(s < TOP - 1, 1, 0)
        + jnp.where(s == TOP, TOP - 1, 0),
    )

    def e1_copy():
        return remote(enc_ref, e1_recv.at[s], e1_ssem, e1_rsem.at[s], TOP, j)

    @pl.when(s < TOP)
    def _():
        e1_copy().start()

    def sc_copy(o):
        return remote(scale_ref, sc_recv.at[j], sc_ssem.at[o], sc_rsem.at[j], s, peer(o))

    def gain_copy():
        return remote(gain_hbm, gain_up, gain_ssem, gain_rsem, below, j)

    def stage_copy():
        return remote(wv_hbm, wv_stage, stage_ssem, stage_rsem, below, j)

    own_rows = pl.ds(pl.multiple_of(j * 64, 64), 64)

    def columns_of(p):
        return wv_stage.at[:, pl.ds(pl.multiple_of((p // 2) * WIDE, 128), WIDE)]

    def wv_copy(o):
        p = peer(o)
        return remote(columns_of(p), wvs.at[own_rows], wv_ssem.at[o], wv_rsem.at[j], s, p)

    def column_copy(h, o):
        p = peer(o)
        cols = pl.ds(pl.multiple_of((p // 2) * WIDE, 128), WIDE)
        return remote(
            wv_hbm.at[pl.ds(32 * h, 32), cols], half_columns(h, j),
            wv_ssem.at[N * h + o], wv_rsem.at[N * h + j], s, p,
        )

    def half_columns(h, p):
        return wvs.at[pl.ds(pl.multiple_of(p * 64 + 32 * h, 32), 32)]

    straight_columns = pltpu.make_async_copy(
        wv_hbm.at[:, pl.ds(pl.multiple_of(my_d * WIDE, 128), WIDE)], wvs.at[own_rows], local_sem.at[11]
    )
    own_columns = pltpu.make_async_copy(columns_of(j), wvs.at[own_rows], local_sem.at[11])

    def half_rows(c, h):
        return wvf.at[pl.ds(pl.multiple_of(c * 64 + 32 * h, 32), 32)]

    def quarter_rows(c, h, q):
        return wvf.at[pl.ds(pl.multiple_of(c * 64 + 32 * h + 16 * q, 16), 16)]

    def first_ring(h, o):
        return at_col(o) if h else at_row(o)

    def second_ring(h, o):
        return at_row(o) if h else at_col(o)

    def on_rings(h, o1, o2):
        if h:
            return lax.rem(row + o1, 4) * 4 + lax.rem(col + o2, 4)
        return lax.rem(row + o2, 4) * 4 + lax.rem(col + o1, 4)

    def full_copy(h, o):
        return remote(
            wv_hbm.at[pl.ds(32 * h, 32)], half_rows(j, h),
            wv_ssem.at[4 * h + o], fw_rsem.at[4 * j + 2 * h], below, first_ring(h, o),
        )

    def pair_rows(h, k):
        return wvf.at[pl.ds(pl.multiple_of(k * 64 + 32 * h, 32), 32)]

    def pair_copy(h):
        return remote(
            wv_hbm.at[pl.ds(32 * h, 32)], pair_rows(h, my_k),
            pair_ssem.at[h], pair_rsem.at[h], s, j + 1 - 2 * my_k,
        )

    own_wv = pltpu.make_async_copy(
        wv_hbm, wvf.at[pl.ds(pl.multiple_of(my_k * 64, 64), 64)], local_sem.at[9]
    )
    own_gain = pltpu.make_async_copy(gain_hbm, gain_up, local_sem.at[10])

    @pl.when(s == TOP)
    def _():
        own_wv.start()

    @pl.when(s >= second_index)
    def _():
        own_gain.start()

    @pl.when((s >= 1) & (s < second_index))
    def _():
        gain_copy().start()

    @pl.when(s >= 1)
    def _():
        @pl.loop(1, N)
        def _(o):
            sc_copy(o).start()

    @pl.when(s == TOP)
    def _():
        pair_copy(0).start()

    @pl.when(feeds_spread)
    def _():
        stage_copy().start()

    @pl.when(feeds_join)
    def _():
        for o in (1, 3, 0):
            for h in range(2):
                full_copy(h, o).start()

    for copy in small[3:]:
        copy.wait()
    pad[...] = jnp.zeros_like(pad)
    hcat[...] = jnp.zeros_like(hcat)
    query = lax.broadcasted_iota(jnp.int32, (TOK, TOK), 0)
    key = lax.broadcasted_iota(jnp.int32, (TOK, TOK), 1)
    for h in range(HEADS_HERE):
        scores = jnp.where(key <= query, logits_ref[h].astype(F32), -jnp.inf)
        highest = jnp.max(scores, axis=-1, keepdims=True)
        weights = jnp.exp(scores - highest)
        pad[0:TOK, 0:TOK] = weights / jnp.sum(weights, axis=-1, keepdims=True)
        pat[:, h * HD : (h + 1) * HD] = pad[...].T[0:TOK, :].astype(BF16)

    @pl.when((s == 3) | (s == 1))
    def _():
        arrived(wv_stage, stage_rsem, stage_ssem)
        own_columns.start()

        @pl.loop(1, N)
        def _(o):
            wv_copy(o).start()

    def u_copy(h, o):
        part = u_recv.at[j, :, pl.ds(1280 * h, 1280)]
        return remote(
            u_send.at[:, pl.ds(1280 * h, 1280)], part,
            u_ssem.at[4 * h + o], u_rsem.at[2 * j + h], below, at_col(o) if h else at_row(o),
        )

    def mix_copy(p):
        return remote(mix_send, mix_recv.at[j], mix_ssem.at[p], mix_rsem.at[j], below, p)

    def spread_scales():
        @pl.loop(1, N)
        def _(o):
            p = peer(o)
            arrived(sc_recv.at[p], sc_rsem.at[p], sc_ssem.at[0])

        sc_recv[j] = scale_ref[...]
        for q in range(N):
            sc_rows[6 * q : 6 * q + 6, :] = sc_recv[q, 0:6, :]

    def seed_copy():
        return remote(seeds, u_recv.at[N], seed_ssem, seed_rsem, below, j)

    def hop_copy(src):
        return remote(src, grad_base, hop_ssem, hop_rsem, below, j)

    def last_copy():
        return remote(grad_own, grad.at[j], hop_ssem, hop_rsem, below, j)

    @pl.when(s == TOP)
    def _():
        e1_recv[TOP] = enc_ref[...]
        for q in range(TOP):
            arrived(e1_recv.at[q], e1_rsem.at[q], e1_ssem)
        rows = jnp.concatenate([e1_recv[:, 0, :], e1_recv[:, 1, :]], axis=0)
        e2_send[...] = rows.astype(BF16)
        e2_recv[j] = rows.astype(BF16)

        def e2_copy(o):
            return remote(e2_send, e2_recv.at[j], e2_ssem.at[o], e2_rsem.at[j], s, o)

        far_first_peers(lambda p: e2_copy(p).start())

        pair_copy(1).start()
        spread_scales()
        lane = lax.broadcasted_iota(jnp.int32, (TOK, HEADS_HERE * HD), 1)
        place = lax.broadcasted_iota(jnp.int32, (TOK, HD), 1) - 16 * lax.rem(j, 8)
        slab = jnp.zeros((TOK, HD), F32)
        for k in range(2):
            for h in range(HEADS_HERE):
                hit = lane == h * HD + tok_ref[k]
                chosen = jnp.sum(jnp.where(hit, pat[...].astype(F32), 0.0), axis=1, keepdims=True)
                spot = 4 * k + h
                slab = slab + jnp.where((place == spot) | (place == spot + 8), chosen, 0.0)
        mix_send[...] = (slab * sc_rows[...]).astype(BF16)
        far_first(lambda p: mix_copy(p).start())

        @pl.loop(1, N)
        def _(o):
            p = peer(o)
            arrived(e2_recv.at[p], e2_rsem.at[p], e2_ssem.at[o])

        blocks = [jnp.zeros((16, 128), F32) for _ in range(5)]
        for q in range(N):
            first = min(40 * q // 128, 3)
            piece = e2_recv[q].astype(F32)
            blocks[first] = blocks[first] + piece[:, 0:128]
            blocks[first + 1] = blocks[first + 1] + piece[:, 128:256]
        top_rows = jnp.concatenate(blocks, axis=1)
        seeds[...] = jnp.zeros_like(seeds)
        for d in range(4):
            cols = slice(d * WIDE, (d + 1) * WIDE)
            for k in range(2):
                low = top_rows[k * 8 + d : k * 8 + d + 1, :]
                high = top_rows[k * 8 + d + 4 : k * 8 + d + 5, :]
                seeds[k : k + 1, cols] = low.astype(BF16)
                seeds[8 + k : 9 + k, cols] = high.astype(BF16)
        seed_copy().start()
        wo_copy.wait()
        half = 2560
        low = nt_dot(seeds[...], wo[:, 0:half])
        high = nt_dot(seeds[...], wo[:, half:])
        rows = low[0:2] + high[8:10]
        parts = [
            rows[k : k + 1, h * HD : (h + 1) * HD] for k in range(2) for h in range(HEADS_HERE)
        ]
        head_rows = jnp.concatenate(parts, axis=0).astype(BF16)
        own_wv.wait()
        own_gain.wait()
        for h in range(2):
            arrived(pair_rows(h, 1 - my_k), pair_rsem.at[h], pair_ssem.at[h])
        for h in range(2):
            cols = slice(h * half, (h + 1) * half)
            mixed = jnp.dot(head_rows, wvf[0:128, cols], preferred_element_type=F32)
            u_rows[8 * h : 8 * h + 8, :] = mixed * gain_up[:, cols]
        u_send[...] = u_rows[...].astype(BF16)
        for o in (2, 1, 3, 0):
            for h in range(2):
                u_copy(h, o).start()

        token = lax.broadcasted_iota(jnp.int32, (TOK, WIDE), 0)
        for k in range(2):
            hit = token == tok_ref[k]
            for d in range(8):
                one = jnp.broadcast_to(top_rows[k * 8 + d : k * 8 + d + 1, :], (TOK, WIDE))
                grad[2 * d + k] = jnp.where(hit, one, 0.0).astype(BF16)

        @pl.loop(1, N)
        def _(o):
            e2_copy(peer(o)).wait_send()

    @pl.when((s >= 1) & (s < TOP))
    def _():
        spread_scales()

    @pl.when(s < TOP)
    def _():
        wo_copy.wait()

    dec_copy.wait()

    def transpose_weights():
        @pl.loop(0, 40)
        def _(i):
            part = pl.ds(pl.multiple_of(i * 128, 128), 128)
            wo_t[part, :] = wo[:, part].T

    sent = []

    def pass_half(c, h, to):
        sem = fw_ssem.at[len(sent)]
        copy = remote(half_rows(c, h), half_rows(c, h), sem, fw_rsem.at[4 * c + 2 * h], s, to)
        copy.start()
        sent.append(copy)

    def pass_quarter(c, h, q, to):
        sem = fw_ssem.at[len(sent)]
        part = quarter_rows(c, h, q)
        copy = remote(part, part, sem, fw_rsem.at[4 * c + 2 * h + q], s, to)
        copy.start()
        sent.append(copy)

    def half_here(c, h):
        arrived(half_rows(c, h), fw_rsem.at[4 * c + 2 * h], fw_ssem.at[0])

    def quarters_here(c, h):
        for q in range(2):
            arrived(quarter_rows(c, h, q), fw_rsem.at[4 * c + 2 * h + q], fw_ssem.at[0])

    @pl.when(joins)
    def _():
        for o in (0, 1, 3):
            for h in range(2):
                c = on_rings(h, o, 0)
                half_here(c, h)
                if o == 3:
                    pass_quarter(c, h, 0, first_ring(h, 1))
                if o == 1:
                    pass_quarter(c, h, 1, first_ring(h, 3))
                pass_half(c, h, second_ring(h, 1))
                pass_half(c, h, second_ring(h, 3))
        for h in range(2):
            c = on_rings(h, 2, 0)
            quarters_here(c, h)
            pass_half(c, h, second_ring(h, 1))
            pass_half(c, h, second_ring(h, 3))
        arrived(gain_up, gain_rsem, gain_ssem)
        for step, o in enumerate((0, 1, 3, 2)):
            @pl.when(s >= 2)
            def _():
                @pl.loop(10 * step, 10 * step + 10)
                def _(i):
                    part = pl.ds(pl.multiple_of(i * 128, 128), 128)
                    scaled = wo[:, part].astype(F32) * gain_up[:, part]
                    wo_t[part, :] = scaled.T.astype(BF16)

            for h in range(2):
                c = on_rings(h, o, 3)
                half_here(c, h)
                pass_quarter(c, h, 0, second_ring(h, 1))
                c = on_rings(h, o, 1)
                half_here(c, h)
                pass_quarter(c, h, 1, second_ring(h, 3))
        for o in (0, 1, 3, 2):
            for h in range(2):
                quarters_here(on_rings(h, o, 2), h)
        for copy in sent:
            copy.wait_send()

        @pl.when(s == 0)
        def _():
            @pl.loop(0, 64)
            def _(i):
                part = pl.ds(pl.multiple_of(i * 16, 16), 16)
                wvf[part, :] = (wvf[part, :].astype(F32) * gain_up[...]).astype(BF16)

    @pl.when(spreads)
    def _():
        transpose_weights()

    @pl.when((s == 4) | (s == 2))
    def _():
        @pl.loop(0, 2)
        def _(i):
            part = pl.ds(pl.multiple_of(i * 512, 512), 512)
            total = jnp.zeros((512, HEADS_HERE * HD), F32)
            for d in range(8):
                cols = slice(d * WIDE, (d + 1) * WIDE)
                total += jnp.dot(wvf[part, cols], wo_t[cols, :], preferred_element_type=F32)
            joint[part, 0 : HEADS_HERE * HD] = total.astype(BF16)

    @pl.when(s == 0)
    def _():
        @pl.loop(0, 8)
        def _(i):
            part = pl.ds(pl.multiple_of(i * 128, 128), 128)
            total = jnp.zeros((128, FEATS), F32)
            for d in range(8):
                cols = slice(d * WIDE, (d + 1) * WIDE)
                total += nt_dot(wvf[part, cols], dec[:, cols])
            joint[part, :] = total.astype(BF16)

    def wait_values():
        @pl.loop(0, N)
        def _(p):
            @pl.when(spreads | (second & (p != j)))
            def _():
                arrived(v_recv.at[p, 0], v_rsem.at[p], v_ssem.at[0])

            @pl.when(joins)
            def _():
                arrived(v_recv.at[p], v_rsem.at[p], v_ssem.at[0])

    def value_grad(k):
        pieces = []
        for q in range(8):
            both = v_recv[2 * q, k].astype(F32) + v_recv[2 * q + 1, k].astype(F32)
            pieces.append(both.astype(BF16))
        return jnp.concatenate(pieces, axis=1)

    def v_copy_both(p):
        return remote(v_send, v_recv.at[j], v_ssem.at[p], v_rsem.at[j], below, p)

    def v_copy_one(p):
        return remote(v_send.at[lax.rem(p, 2)], v_recv.at[j, 0], v_ssem.at[p], v_rsem.at[j], below, p)

    def v_copy_here(p):
        return remote(
            v_send.at[lax.rem(p, 2)], v_recv.at[j, 0], v_ssem.at[p], v_rsem.at[j], s, p
        )

    def send_values(head_grad):
        for k in range(2):
            for h in range(HEADS_HERE):
                hcat[h * HD : h * HD + TOK, k * HD : (k + 1) * HD] = head_grad[
                    k * TOK : (k + 1) * TOK, h * HD : (h + 1) * HD
                ]
        part = jnp.dot(pat[...], hcat[...], preferred_element_type=F32)
        for k in range(2):
            v_send[k] = (part[:, k * HD : (k + 1) * HD] * sc_rows[...]).astype(BF16)

        @pl.when(feeds_join)
        def _():
            far_first(lambda p: v_copy_both(p).start())

        @pl.when(feeds_spread)
        def _():
            far_first(lambda p: v_copy_one(p).start())

        @pl.when(second)
        def _():
            far_first_peers(lambda p: v_copy_here(p).start())
            v_recv[j, 0] = v_send[my_k]

    def half_copy(c, h, to, sem):
        part = grad.at[c, pl.ds(48 * h, 48)]
        return remote(part, part, g_ssem.at[sem], g_rsem.at[2 * c + h], s, to)

    def half_arrived(c, h):
        arrived(grad.at[c, pl.ds(48 * h, 48)], g_rsem.at[2 * c + h], g_ssem.at[0])

    own_sends, row_sends, col_sends = [], [], []
    for o in (2, 1, 3):
        own_sends.append((j, 0, at_row(o), o))
        own_sends.append((j, 1, at_col(o), 4 + o))
    for o in (2, 1, 3):
        own_sends.append((j, 0, at_col(o), 8 + o))
        own_sends.append((j, 1, at_row(o), 12 + o))
    for o in (1, 3, 2):
        row_sends.append([(at_row(o), 0, at_col(q), 16 + 4 * o + q) for q in (2, 1, 3)])
        col_sends.append([(at_col(o), 1, at_row(q), 32 + 4 * o + q) for q in (2, 1, 3)])

    own_cols = pl.ds(pl.multiple_of(my_d * WIDE, 128), WIDE)

    def next_chunk(chunk):
        wait_values()
        mixed = jnp.dot(value_grad(0), wvs[...], preferred_element_type=F32)
        return (chunk[...].astype(F32) + mixed * gain_up[:, own_cols]).astype(BF16)

    def make_chunk():
        @pl.when(s == 5)
        def _():
            arrived(grad.at[j], hop_rsem, hop_ssem)

        @pl.when(s < 5)
        def _():
            grad[j] = next_chunk(grad_base)

        for item in own_sends:
            half_copy(*item).start()

    def forward(k):
        for items in row_sends:
            c = items[0][0]

            @pl.when(lax.rem(c, 2) == k)
            def _():
                half_arrived(c, 0)
                for item in items:
                    half_copy(*item).start()

        @pl.when(my_k == k)
        def _():
            for items in col_sends:
                half_arrived(items[0][0], 1)
                for item in items:
                    half_copy(*item).start()

    def wait_chunk(c):
        @pl.when(c // 4 != row)
        def _():
            half_arrived(c, 0)

        @pl.when(c % 4 != col)
        def _():
            half_arrived(c, 1)

    def whole_copy(d):
        part = grad.at[pl.ds(2 * d, 2)]
        return remote(part, part, copy_ssem.at[d], copy_rsem.at[d], below, j)

    def whole_arrived(d):
        arrived(grad.at[pl.ds(2 * d, 2)], copy_rsem.at[d], copy_ssem.at[0])

    def head_grad_of(at_chunk, dot):
        total = jnp.zeros((2 * TOK, HEADS_HERE * HD), F32)
        for d in range(8):
            at_chunk(d)
            both = grad[2 * d : 2 * d + 2].reshape(2 * TOK, WIDE)
            total += dot(both, slice(d * WIDE, (d + 1) * WIDE))
        return total

    @pl.when((s == 3) | (s == 1))
    def _():
        arrived(gain_up, gain_rsem, gain_ssem)
        own_columns.wait()

        @pl.loop(1, N)
        def _(o):
            p = peer(o)
            rows = pl.ds(pl.multiple_of(p * 64, 64), 64)
            arrived(wvs.at[rows], wv_rsem.at[p], wv_ssem.at[0])

        arrived(grad_base, hop_rsem, hop_ssem)

    @pl.when(spreads)
    def _():
        make_chunk()
        forward(0)
        forward(1)

        def take_chunks(d):
            wait_chunk(2 * d)
            wait_chunk(2 * d + 1)
            whole_copy(d).start()

        send_values(head_grad_of(
            take_chunks,
            lambda both, part: jnp.dot(both, wo_t[part, :], preferred_element_type=F32),
        ).astype(BF16))

    u_forwards = []
    for o in (0, 1, 3, 2):
        u_forwards.append([(at_row(o), 0, at_col(q), 8 + 4 * o + q) for q in (2, 1, 3)])
        u_forwards.append([(at_col(o), 1, at_row(q), 24 + 4 * o + q) for q in (2, 1, 3)])

    def u_half(c, h):
        return u_recv.at[c, :, pl.ds(1280 * h, 1280)]

    def u_forward(c, h, to, sem):
        return remote(u_half(c, h), u_half(c, h), u_ssem.at[sem], u_rsem.at[2 * c + h], s, to)

    @pl.when(second)
    def _():
        straight_columns.start()
        transpose_weights()
        arrived(u_recv.at[N], seed_rsem, seed_ssem)

        @pl.loop(1, N)
        def _(o):
            column_copy(0, o).start()

        for items in u_forwards:
            c, h = items[0][0], items[0][1]
            arrived(u_half(c, h), u_rsem.at[2 * c + h], u_ssem.at[0])
            for item in items:
                u_forward(*item).start()

        @pl.loop(1, N)
        def _(o):
            column_copy(1, o).start()

        @pl.loop(0, N)
        def _(p):
            arrived(mix_recv.at[p], mix_rsem.at[p], mix_ssem.at[0])

        kind = lax.broadcasted_iota(jnp.int32, (TOK, HD), 1) & 15
        for t in range(2):
            tile = jnp.zeros((TOK, HD), F32)
            for q in range(8):
                tile = tile + mix_recv[8 * t + q].astype(F32)
            for h in range(2):
                for k in range(2):
                    keep = (kind >> 2) == 2 * h + k
                    mix[h, k * TOK : (k + 1) * TOK, t * HD : (t + 1) * HD] = jnp.where(
                        keep, tile, 0.0
                    ).astype(BF16)

        @pl.loop(0, N)
        def _(c):
            @pl.when(c // 4 != row)
            def _():
                arrived(u_half(c, 0), u_rsem.at[2 * c], u_ssem.at[0])

            @pl.when(lax.rem(c, 4) != col)
            def _():
                arrived(u_half(c, 1), u_rsem.at[2 * c + 1], u_ssem.at[0])

        half = 2560
        flat = u_recv[...].reshape(16 * (N + 1), half)
        low = jnp.dot(flat, wo_t[0:half, :], preferred_element_type=F32)
        high = jnp.dot(flat, wo_t[half:, :], preferred_element_type=F32)
        total = jnp.dot(mix[0], low[0:256].astype(BF16), preferred_element_type=F32)
        total += jnp.dot(mix[1], high[0:256].astype(BF16), preferred_element_type=F32)
        token = lax.broadcasted_iota(jnp.int32, (TOK, HEADS_HERE * HD), 0)
        parts = []
        for k in range(2):
            one = low[256 + k : 257 + k] + high[264 + k : 265 + k]
            parts.append(
                total[k * TOK : (k + 1) * TOK] + jnp.where(token == tok_ref[k], one, 0.0)
            )
        send_values(jnp.concatenate(parts, axis=0).astype(BF16))
        token = lax.broadcasted_iota(jnp.int32, (TOK, WIDE), 0)
        for d in range(8):
            h, cols = d // 4, slice((d % 4) * WIDE, (d % 4 + 1) * WIDE)
            head_rows = u_recv[0:N, :, cols].reshape(16 * N, WIDE)
            mixed = jnp.dot(mix[h], head_rows, preferred_element_type=F32)
            for k in range(2):
                one = u_recv[N, 8 * h + k : 8 * h + k + 1, cols].astype(F32)
                grad[2 * d + k] = (
                    mixed[k * TOK : (k + 1) * TOK] + jnp.where(token == tok_ref[k], one, 0.0)
                ).astype(BF16)
        own_gain.wait()
        straight_columns.wait()

        @pl.loop(1, N)
        def _(o):
            p = peer(o)
            for h in range(2):
                arrived(half_columns(h, p), wv_rsem.at[N * h + p], wv_ssem.at[0])

        grad_own[...] = next_chunk(grad.at[j])
        last_copy().start()

    @pl.when((s == 4) | (s == 2))
    def _():
        base[...] = head_grad_of(whole_arrived, lambda both, part: nt_dot(both, wo[:, part]))
        wait_values()
        for k in range(2):
            v_full[k * TOK : (k + 1) * TOK, :] = value_grad(k)
        mixed = jnp.dot(
            v_full[pl.ds(pl.multiple_of(my_k * TOK, TOK), TOK), :], wvf[:, own_cols],
            preferred_element_type=F32,
        )
        grad_own[...] = (grad[j].astype(F32) + mixed * gain_up[:, own_cols]).astype(BF16)
        hop_copy(grad_own).start()
        total = base[...] + jnp.dot(
            v_full[...], joint[:, 0 : HEADS_HERE * HD], preferred_element_type=F32
        )
        send_values(total.astype(BF16))
        for d in range(8):
            mixed = jnp.dot(
                v_full[...], wvf[:, d * WIDE : (d + 1) * WIDE], preferred_element_type=F32
            )
            mixed = mixed * gain_up[:, d * WIDE : (d + 1) * WIDE]
            for k in range(2):
                grad[2 * d + k] = (
                    grad[2 * d + k].astype(F32) + mixed[k * TOK : (k + 1) * TOK]
                ).astype(BF16)

    @pl.when(s == 0)
    def _():
        for d in range(8):
            whole_arrived(d)

    for d in range(8):
        both = grad[2 * d : 2 * d + 2].reshape(2 * TOK, WIDE)
        term = nt_dot(both, dec[:, d * WIDE : (d + 1) * WIDE])
        if d == 0:
            acc[...] = term
        else:
            acc[...] += term

    @pl.when(s == 0)
    def _():
        wait_values()
        for k in range(2):
            v_full[k * TOK : (k + 1) * TOK, :] = value_grad(k)
        acc[...] += jnp.dot(v_full[...], joint[...], preferred_element_type=F32)

    local_id = ids_ref[...] - j * FEATS
    lane = local_id & 127
    block = local_id >> 7
    chosen = []
    for k in range(2):
        picked = jnp.zeros((TOK, ACT), F32)
        for b in range(8):
            near = acc[k * TOK : (k + 1) * TOK, b * 128 : (b + 1) * 128]
            got = jnp.take_along_axis(near, lane, axis=1)
            picked = jnp.where(block == b, got, picked)
        chosen.append((picked * vals_ref[...]).astype(BF16))
    terms = jnp.concatenate(chosen, axis=0)
    e_row = lax.broadcasted_iota(jnp.int32, (256, 192), 0)
    e_col = lax.broadcasted_iota(jnp.int32, (256, 192), 1)
    slot = e_row & 7
    source = ((e_row >> 3) & 1) * TOK + (e_row >> 4) * 6 + slot
    placing = jnp.where((e_col == source) & (slot < 6), 1.0, 0.0).astype(BF16)
    placed = jnp.dot(placing, terms, preferred_element_type=F32).astype(BF16)
    for q in range(N):
        ed_send[q] = placed[16 * q : 16 * q + 16, :]

    def ed_copy(p):
        return remote(ed_send.at[p], ed_recv.at[j], ed_ssem.at[p], ed_rsem.at[j], s, p)

    far_first_peers(lambda p: ed_copy(p).start())

    ed_recv[j] = ed_send[j]

    @pl.loop(1, N)
    def _(o):
        p = peer(o)
        arrived(ed_recv.at[p], ed_rsem.at[p], ed_ssem.at[0])

    edges = jnp.zeros((16, ACT), F32)
    for q in range(N):
        edges += ed_recv[q].astype(F32)
    for k in range(2):
        for t in range(6):
            out_ref[t, k : k + 1, :] = edges[8 * k + t : 8 * k + t + 1, :]

    @pl.loop(1, N)
    def _(o):
        ed_copy(peer(o)).wait_send()

    @pl.when(s < TOP)
    def _():
        e1_copy().wait_send()

    @pl.when(s >= 1)
    def _():
        @pl.loop(1, N)
        def _(o):
            sc_copy(o).wait_send()

    @pl.when(s == TOP)
    def _():
        pair_copy(0).wait_send()
        pair_copy(1).wait_send()
        seed_copy().wait_send()
        for o in range(4):
            for h in range(2):
                u_copy(h, o).wait_send()

        @pl.loop(0, N)
        def _(p):
            mix_copy(p).wait_send()

    @pl.when(second)
    def _():
        last_copy().wait_send()
        far_first_peers(lambda p: v_copy_here(p).wait_send())

        @pl.loop(1, N)
        def _(o):
            for h in range(2):
                column_copy(h, o).wait_send()

        for items in u_forwards:
            for item in items:
                u_forward(*item).wait_send()

    @pl.when((s >= 1) & (s < second_index))
    def _():
        gain_copy().wait_send()

        for p in range(N):
            @pl.when(feeds_join)
            def _():
                v_copy_both(p).wait_send()

            @pl.when(feeds_spread)
            def _():
                v_copy_one(p).wait_send()

    @pl.when(feeds_spread)
    def _():
        hop_copy(grad_own).wait_send()
        stage_copy().wait_send()

    @pl.when(feeds_join)
    def _():
        for o in (0, 1, 3):
            for h in range(2):
                full_copy(h, o).wait_send()
        for d in range(8):
            whole_copy(d).wait_send()

    @pl.when((s == 3) | (s == 1))
    def _():
        @pl.loop(1, N)
        def _(o):
            wv_copy(o).wait_send()

    @pl.when(spreads)
    def _():
        for item in own_sends + sum(row_sends, []) + sum(col_sends, []):
            half_copy(*item).wait_send()


def body(
    attn_logits, out_weight, value_weight, norm_gain, norm_scale, target_encoder,
    target_ids, target_token, decoder, source_ids, source_values,
):
    vmem = pl.BlockSpec(memory_space=pltpu.VMEM)
    hbm = pl.BlockSpec(memory_space=pltpu.HBM)
    dma = pltpu.SemaphoreType.DMA
    out = pl.pallas_call(
        chain_kernel,
        out_shape=jax.ShapeDtypeStruct((6, 2, ACT), F32),
        in_specs=[hbm] * 11,
        out_specs=vmem,
        scratch_shapes=[
            pltpu.VMEM((40, 16384), BF16),
            pltpu.VMEM((1, 6), F32),
            pltpu.VMEM((HEADS_HERE, TOK, TOK), BF16),
            pltpu.VMEM((1, 5120), F32),
            pltpu.SMEM((2,), jnp.int32),
            pltpu.SMEM((2,), jnp.int32),
            pltpu.VMEM((TOK, ACT), jnp.int32),
            pltpu.VMEM((TOK, ACT), F32),
            pltpu.VMEM((8, 256), F32),
            pltpu.VMEM((8, 128), F32),
            pltpu.VMEM((512, 5120), BF16),
            pltpu.VMEM((5120, 512), BF16),
            pltpu.VMEM((FEATS, 5120), BF16),
            pltpu.VMEM((1024, WIDE), BF16),
            pltpu.VMEM((1024, 5120), BF16),
            pltpu.VMEM((1024, FEATS), BF16),
            pltpu.VMEM((N, TOK, WIDE), BF16),
            pltpu.VMEM((TOK, WIDE), BF16),
            pltpu.VMEM((TOK, WIDE), BF16),
            pltpu.VMEM((2, TOK, HD), BF16),
            pltpu.VMEM((N, 2, TOK, HD), BF16),
            pltpu.VMEM((2 * TOK, 1024), BF16),
            pltpu.VMEM((2 * TOK, HEADS_HERE * HD), F32),
            pltpu.VMEM((N, 8, 128), F32),
            pltpu.VMEM((TOK, 128), F32),
            pltpu.VMEM((8, 8, 256), F32),
            pltpu.VMEM((16, 256), BF16),
            pltpu.VMEM((N, 16, 256), BF16),
            pltpu.VMEM((TOK, HEADS_HERE * HD), BF16),
            pltpu.VMEM((HEADS_HERE * HD, 2 * HD), BF16),
            pltpu.VMEM((128, 128), F32),
            pltpu.VMEM((2 * TOK, FEATS), F32),
            pltpu.VMEM((N, 16, ACT), BF16),
            pltpu.VMEM((N, 16, ACT), BF16),
            dma((12,)),
            dma, dma,
            dma((2 * N,)), dma((2 * N,)),
            dma((3 * N,)), dma((4 * N,)),
            dma((N,)), dma((N,)),
            dma, dma((8,)),
            dma((N,)), dma((N,)),
            dma((N,)), dma((N,)),
            dma((3 * N,)), dma((2 * N,)),
            dma, dma,
            dma((8,)), dma((8,)),
            dma((N,)), dma((N,)),
            pltpu.VMEM((16, 2560), BF16),
            pltpu.VMEM((16, 2560), F32),
            pltpu.VMEM((16, 2560), BF16),
            pltpu.VMEM((N + 1, 16, 2560), BF16),
            pltpu.VMEM((TOK, HD), BF16),
            pltpu.VMEM((N, TOK, HD), BF16),
            pltpu.VMEM((2, 2 * TOK, 2 * HD), BF16),
            pltpu.VMEM((64, 5120), BF16),
            dma, dma,
            dma((2,)), dma((2,)),
            dma((40,)), dma((2 * N,)),
            dma((N,)), dma((N,)),
            dma, dma,
        ],
        compiler_params=pltpu.CompilerParams(
            collective_id=0, has_side_effects=True, vmem_limit_bytes=63 * 2**20
        ),
        name="chain",
    )(
        target_encoder.T, norm_scale, attn_logits[0], norm_gain, target_ids, target_token,
        source_ids[0], source_values[0],
        out_weight[0], value_weight[0], decoder[0],
    )
    return out[None]


def solution(mesh):
    return jax.shard_map(
        body,
        mesh=mesh,
        in_specs=(
            P("section", "tensor", None, None),
            P("section", "tensor", None),
            P("section", "tensor", None),
            P("section", None),
            P("section", "tensor"),
            P(None, ("section", "tensor")),
            P(),
            P(),
            P("section", "tensor", None),
            P("section", None, None),
            P("section", None, None),
        ),
        out_specs=P("section", "tensor", None, None),
        check_vma=False,
    )
```

```python
import jax
import jax.numpy as jnp
from jax import lax
from jax.experimental import pallas as pl
from jax.experimental.pallas import tpu as pltpu
from jax.sharding import PartitionSpec as P

MESH = pl.DeviceIdType.MESH
F32 = jnp.float32
BF16 = jnp.bfloat16

TOK = 96
N = 16
TOP = 7
HD = 128
WIDE = 640
HEADS_HERE = 4
ACT = 128
FEATS = 1024
FAR_FIRST = sorted(
    [(dy, dx) for dy in range(4) for dx in range(4)],
    key=lambda at: -min(at[0], 4 - at[0]) - min(at[1], 4 - at[1]),
)


def nt_dot(a, b):
    return lax.dot_general(a, b, (((1,), (1,)), ((), ())), preferred_element_type=F32)


def chain_kernel(
    enc_hbm, scale_hbm, logits_hbm, gain_hbm, want_hbm, tok_hbm, ids_hbm, vals_hbm,
    wo_hbm, wv_hbm, dec_hbm,
    out_ref,
    table, scale_raw, logits_ref, gain_up, want_ref, tok_ref, ids_ref, vals_ref,
    enc_ref, scale_ref,
    wo, wo_t, dec, wvs, wvf, joint, grad, grad_base, grad_own, v_send, v_recv, v_full, base,
    sc_recv, sc_rows, e1_recv, e2_send, e2_recv, pat, hcat, pad, acc, ed_send, ed_recv,
    local_sem, gain_ssem, gain_rsem, wv_ssem, wv_rsem, fw_ssem, fw_rsem, sc_ssem, sc_rsem,
    e1_ssem, e1_rsem, e2_ssem, e2_rsem, v_ssem, v_rsem, g_ssem, g_rsem, hop_ssem, hop_rsem,
    copy_ssem, copy_rsem, ed_ssem, ed_rsem,
    seeds, u_rows, u_send, u_recv, mix_send, mix_recv, mix,
    wv_stage, stage_ssem, stage_rsem, pair_ssem, pair_rsem, u_ssem, u_rsem, mix_ssem, mix_rsem, seed_ssem, seed_rsem,
):
    s = lax.axis_index("section")
    j = lax.axis_index("tensor")
    my_k = lax.rem(j, 2)
    my_d = j // 2
    row = j // 4
    col = lax.rem(j, 4)
    below = s - 1
    spreads = (s == 5) | (s == 3) | (s == 1)
    joins = (s == 4) | (s == 2) | (s == 0)
    second_index = TOP - 1
    second = s == second_index
    feeds_spread = (s == 4) | (s == 2)
    feeds_join = (s == 5) | (s == 3) | (s == 1)

    def peer(o):
        return lax.rem(j + o, N)

    def far_first(body):
        for dy, dx in FAR_FIRST:
            body(lax.rem(row + dy, 4) * 4 + lax.rem(col + dx, 4))

    def far_first_peers(body):
        for dy, dx in FAR_FIRST[:-1]:
            body(lax.rem(row + dy, 4) * 4 + lax.rem(col + dx, 4))

    def at_row(o):
        return row * 4 + lax.rem(col + o, 4)

    def at_col(o):
        return lax.rem(row + o, 4) * 4 + col

    def remote(src, dst, ssem, rsem, section, index):
        return pltpu.make_async_remote_copy(
            src_ref=src, dst_ref=dst, send_sem=ssem, recv_sem=rsem,
            device_id=(section, index), device_id_type=MESH,
        )

    def arrived(dst, rsem, ssem):
        remote(dst, dst, ssem, rsem, s, peer(1)).wait_recv()

    barrier = pltpu.get_barrier_semaphore()

    def greet(section, index):
        pl.semaphore_signal(barrier, inc=1, device_id=(section, index), device_id_type=MESH)

    @pl.when(s < TOP - 1)
    def _():
        greet(TOP, j)

    @pl.when(s == TOP)
    def _():
        for q in range(TOP - 1):
            greet(q, j)

    @pl.loop(1, N)
    def _(o):
        greet(s, peer(o))

    @pl.when(s < TOP)
    def _():
        @pl.loop(0, N)
        def _(p):
            greet(s + 1, p)

    @pl.when(s >= 1)
    def _():
        @pl.loop(0, N)
        def _(p):
            greet(below, p)

    small = [
        pltpu.make_async_copy(src, dst, local_sem.at[2 + i])
        for i, (src, dst) in enumerate([
            (want_hbm, want_ref), (enc_hbm, table), (scale_hbm, scale_raw),
            (logits_hbm, logits_ref), (tok_hbm, tok_ref),
            (ids_hbm, ids_ref), (vals_hbm, vals_ref),
        ])
    ]
    for copy in small:
        copy.start()
    wo_copy = pltpu.make_async_copy(wo_hbm, wo, local_sem.at[0])
    wo_copy.start()
    dec_copy = pltpu.make_async_copy(dec_hbm, dec, local_sem.at[1])
    dec_copy.start()

    small[0].wait()
    small[1].wait()
    first_lane = 40 * j - 128 * jnp.minimum((40 * j) // 128, 3)
    spot = lax.broadcasted_iota(jnp.int32, (40, 256), 1) - lax.broadcasted_iota(jnp.int32, (40, 256), 0)
    lane = lax.broadcasted_iota(jnp.int32, (40, 512), 1)

    def pick(i, found):
        part = table[:, pl.ds(pl.multiple_of(i * 512, 512), 512)].astype(F32)
        return tuple(
            found[k] + jnp.where(lane + i * 512 == want_ref[k], part, 0.0) for k in range(2)
        )

    found = lax.fori_loop(0, 32, pick, (jnp.zeros((40, 512), F32),) * 2)
    enc_ref[...] = jnp.zeros_like(enc_ref)
    for k in range(2):
        column = jnp.sum(found[k], axis=1, keepdims=True)
        enc_ref[k : k + 1, :] = jnp.sum(
            jnp.where(spot == first_lane, column, 0.0), axis=0, keepdims=True
        )
    small[2].wait()
    diagonal = lax.broadcasted_iota(jnp.int32, (8, 6), 0) == lax.broadcasted_iota(jnp.int32, (8, 6), 1)
    scale_ref[...] = jnp.broadcast_to(
        jnp.sum(jnp.where(diagonal, scale_raw[...], 0.0), axis=1, keepdims=True), (8, 128)
    )

    pl.semaphore_wait(
        barrier,
        15
        + jnp.where(s >= 1, N, 0)
        + jnp.where(s < TOP, N, 0)
        + jnp.where(s < TOP - 1, 1, 0)
        + jnp.where(s == TOP, TOP - 1, 0),
    )

    def e1_copy():
        return remote(enc_ref, e1_recv.at[s], e1_ssem, e1_rsem.at[s], TOP, j)

    @pl.when(s < TOP)
    def _():
        e1_copy().start()

    def sc_copy(o):
        return remote(scale_ref, sc_recv.at[j], sc_ssem.at[o], sc_rsem.at[j], s, peer(o))

    def gain_copy():
        return remote(gain_hbm, gain_up, gain_ssem, gain_rsem, below, j)

    def stage_copy():
        return remote(wv_hbm, wv_stage, stage_ssem, stage_rsem, below, j)

    own_rows = pl.ds(pl.multiple_of(j * 64, 64), 64)

    def columns_of(p):
        return wv_stage.at[:, pl.ds(pl.multiple_of((p // 2) * WIDE, 128), WIDE)]

    def wv_copy(o):
        p = peer(o)
        return remote(columns_of(p), wvs.at[own_rows], wv_ssem.at[o], wv_rsem.at[j], s, p)

    def column_copy(h, o):
        p = peer(o)
        cols = pl.ds(pl.multiple_of((p // 2) * WIDE, 128), WIDE)
        return remote(
            wv_hbm.at[pl.ds(32 * h, 32), cols], half_columns(h, j),
            wv_ssem.at[N * h + o], wv_rsem.at[N * h + j], s, p,
        )

    def half_columns(h, p):
        return wvs.at[pl.ds(pl.multiple_of(p * 64 + 32 * h, 32), 32)]

    straight_columns = pltpu.make_async_copy(
        wv_hbm.at[:, pl.ds(pl.multiple_of(my_d * WIDE, 128), WIDE)], wvs.at[own_rows], local_sem.at[11]
    )
    own_columns = pltpu.make_async_copy(columns_of(j), wvs.at[own_rows], local_sem.at[11])

    def half_rows(c, h):
        return wvf.at[pl.ds(pl.multiple_of(c * 64 + 32 * h, 32), 32)]

    def quarter_rows(c, h, q):
        return wvf.at[pl.ds(pl.multiple_of(c * 64 + 32 * h + 16 * q, 16), 16)]

    def first_ring(h, o):
        return at_col(o) if h else at_row(o)

    def second_ring(h, o):
        return at_row(o) if h else at_col(o)

    def on_rings(h, o1, o2):
        if h:
            return lax.rem(row + o1, 4) * 4 + lax.rem(col + o2, 4)
        return lax.rem(row + o2, 4) * 4 + lax.rem(col + o1, 4)

    def full_copy(h, o):
        return remote(
            wv_hbm.at[pl.ds(32 * h, 32)], half_rows(j, h),
            wv_ssem.at[4 * h + o], fw_rsem.at[4 * j + 2 * h], below, first_ring(h, o),
        )

    def pair_rows(h, k):
        return wvf.at[pl.ds(pl.multiple_of(k * 64 + 32 * h, 32), 32)]

    def pair_copy(h):
        return remote(
            wv_hbm.at[pl.ds(32 * h, 32)], pair_rows(h, my_k),
            pair_ssem.at[h], pair_rsem.at[h], s, j + 1 - 2 * my_k,
        )

    own_wv = pltpu.make_async_copy(
        wv_hbm, wvf.at[pl.ds(pl.multiple_of(my_k * 64, 64), 64)], local_sem.at[9]
    )
    own_gain = pltpu.make_async_copy(gain_hbm, gain_up, local_sem.at[10])

    @pl.when(s == TOP)
    def _():
        own_wv.start()

    @pl.when(s >= second_index)
    def _():
        own_gain.start()

    @pl.when((s >= 1) & (s < second_index))
    def _():
        gain_copy().start()

    @pl.when(s >= 1)
    def _():
        @pl.loop(1, N)
        def _(o):
            sc_copy(o).start()

    @pl.when(s == TOP)
    def _():
        pair_copy(0).start()

    @pl.when(feeds_spread)
    def _():
        stage_copy().start()

    @pl.when(feeds_join)
    def _():
        for o in (1, 3, 0):
            for h in range(2):
                full_copy(h, o).start()

    for copy in small[3:]:
        copy.wait()
    pad[...] = jnp.zeros_like(pad)
    hcat[...] = jnp.zeros_like(hcat)
    query = lax.broadcasted_iota(jnp.int32, (TOK, TOK), 0)
    key = lax.broadcasted_iota(jnp.int32, (TOK, TOK), 1)
    for h in range(HEADS_HERE):
        scores = jnp.where(key <= query, logits_ref[h].astype(F32), -jnp.inf)
        highest = jnp.max(scores, axis=-1, keepdims=True)
        weights = jnp.exp(scores - highest)
        pad[0:TOK, 0:TOK] = weights / jnp.sum(weights, axis=-1, keepdims=True)
        pat[:, h * HD : (h + 1) * HD] = pad[...].T[0:TOK, :].astype(BF16)

    @pl.when((s == 3) | (s == 1))
    def _():
        arrived(wv_stage, stage_rsem, stage_ssem)
        own_columns.start()

        @pl.loop(1, N)
        def _(o):
            wv_copy(o).start()

    def transpose_weights():
        @pl.loop(0, 40)
        def _(i):
            part = pl.ds(pl.multiple_of(i * 128, 128), 128)
            wo_t[part, :] = wo[:, part].T

    def u_copy(h, o):
        part = u_recv.at[j, :, pl.ds(1280 * h, 1280)]
        return remote(
            u_send.at[:, pl.ds(1280 * h, 1280)], part,
            u_ssem.at[4 * h + o], u_rsem.at[2 * j + h], below, at_col(o) if h else at_row(o),
        )

    def mix_copy(p):
        return remote(mix_send, mix_recv.at[j], mix_ssem.at[p], mix_rsem.at[j], below, p)

    def spread_scales():
        @pl.loop(1, N)
        def _(o):
            p = peer(o)
            arrived(sc_recv.at[p], sc_rsem.at[p], sc_ssem.at[0])

        sc_recv[j] = scale_ref[...]
        for q in range(N):
            sc_rows[6 * q : 6 * q + 6, :] = sc_recv[q, 0:6, :]

    def seed_copy():
        return remote(seeds, u_recv.at[N], seed_ssem, seed_rsem, below, j)

    def hop_copy(src):
        return remote(src, grad_base, hop_ssem, hop_rsem, below, j)

    def last_copy():
        return remote(grad_own, grad.at[j], hop_ssem, hop_rsem, below, j)

    @pl.when(s == TOP)
    def _():
        e1_recv[TOP] = enc_ref[...]
        for q in range(TOP):
            arrived(e1_recv.at[q], e1_rsem.at[q], e1_ssem)
        rows = jnp.concatenate([e1_recv[:, 0, :], e1_recv[:, 1, :]], axis=0)
        e2_send[...] = rows.astype(BF16)
        e2_recv[j] = rows.astype(BF16)

        def e2_copy(o):
            return remote(e2_send, e2_recv.at[j], e2_ssem.at[o], e2_rsem.at[j], s, o)

        far_first_peers(lambda p: e2_copy(p).start())

        pair_copy(1).start()
        spread_scales()
        lane = lax.broadcasted_iota(jnp.int32, (TOK, HEADS_HERE * HD), 1)
        place = lax.broadcasted_iota(jnp.int32, (TOK, HD), 1) - 16 * lax.rem(j, 8)
        slab = jnp.zeros((TOK, HD), F32)
        for k in range(2):
            for h in range(HEADS_HERE):
                hit = lane == h * HD + tok_ref[k]
                chosen = jnp.sum(jnp.where(hit, pat[...].astype(F32), 0.0), axis=1, keepdims=True)
                spot = 4 * k + h
                slab = slab + jnp.where((place == spot) | (place == spot + 8), chosen, 0.0)
        mix_send[...] = (slab * sc_rows[...]).astype(BF16)
        far_first(lambda p: mix_copy(p).start())
        wo_copy.wait()
        transpose_weights()

        @pl.loop(1, N)
        def _(o):
            p = peer(o)
            arrived(e2_recv.at[p], e2_rsem.at[p], e2_ssem.at[o])

        blocks = [jnp.zeros((16, 128), F32) for _ in range(5)]
        for q in range(N):
            first = min(40 * q // 128, 3)
            piece = e2_recv[q].astype(F32)
            blocks[first] = blocks[first] + piece[:, 0:128]
            blocks[first + 1] = blocks[first + 1] + piece[:, 128:256]
        top_rows = jnp.concatenate(blocks, axis=1)
        seeds[...] = jnp.zeros_like(seeds)
        for d in range(4):
            cols = slice(d * WIDE, (d + 1) * WIDE)
            for k in range(2):
                low = top_rows[k * 8 + d : k * 8 + d + 1, :]
                high = top_rows[k * 8 + d + 4 : k * 8 + d + 5, :]
                seeds[k : k + 1, cols] = low.astype(BF16)
                seeds[8 + k : 9 + k, cols] = high.astype(BF16)
        seed_copy().start()
        half = 2560
        low = jnp.dot(seeds[...], wo_t[0:half, :], preferred_element_type=F32)
        high = jnp.dot(seeds[...], wo_t[half:, :], preferred_element_type=F32)
        rows = low[0:2] + high[8:10]
        parts = [
            rows[k : k + 1, h * HD : (h + 1) * HD] for k in range(2) for h in range(HEADS_HERE)
        ]
        head_rows = jnp.concatenate(parts, axis=0).astype(BF16)
        own_wv.wait()
        own_gain.wait()
        for h in range(2):
            arrived(pair_rows(h, 1 - my_k), pair_rsem.at[h], pair_ssem.at[h])
        for h in range(2):
            cols = slice(h * half, (h + 1) * half)
            mixed = jnp.dot(head_rows, wvf[0:128, cols], preferred_element_type=F32)
            u_rows[8 * h : 8 * h + 8, :] = mixed * gain_up[:, cols]
        u_send[...] = u_rows[...].astype(BF16)
        for o in (2, 1, 3, 0):
            for h in range(2):
                u_copy(h, o).start()

        token = lax.broadcasted_iota(jnp.int32, (TOK, WIDE), 0)
        for k in range(2):
            hit = token == tok_ref[k]
            for d in range(8):
                one = jnp.broadcast_to(top_rows[k * 8 + d : k * 8 + d + 1, :], (TOK, WIDE))
                grad[2 * d + k] = jnp.where(hit, one, 0.0).astype(BF16)

        @pl.loop(1, N)
        def _(o):
            e2_copy(peer(o)).wait_send()

    @pl.when((s >= 1) & (s < TOP))
    def _():
        spread_scales()

    @pl.when(s < TOP)
    def _():
        wo_copy.wait()

    dec_copy.wait()


    sent = []

    def pass_half(c, h, to):
        sem = fw_ssem.at[len(sent)]
        copy = remote(half_rows(c, h), half_rows(c, h), sem, fw_rsem.at[4 * c + 2 * h], s, to)
        copy.start()
        sent.append(copy)

    def pass_quarter(c, h, q, to):
        sem = fw_ssem.at[len(sent)]
        part = quarter_rows(c, h, q)
        copy = remote(part, part, sem, fw_rsem.at[4 * c + 2 * h + q], s, to)
        copy.start()
        sent.append(copy)

    def half_here(c, h):
        arrived(half_rows(c, h), fw_rsem.at[4 * c + 2 * h], fw_ssem.at[0])

    def quarters_here(c, h):
        for q in range(2):
            arrived(quarter_rows(c, h, q), fw_rsem.at[4 * c + 2 * h + q], fw_ssem.at[0])

    @pl.when(joins)
    def _():
        for o in (0, 1, 3):
            for h in range(2):
                c = on_rings(h, o, 0)
                half_here(c, h)
                if o == 3:
                    pass_quarter(c, h, 0, first_ring(h, 1))
                if o == 1:
                    pass_quarter(c, h, 1, first_ring(h, 3))
                pass_half(c, h, second_ring(h, 1))
                pass_half(c, h, second_ring(h, 3))
        for h in range(2):
            c = on_rings(h, 2, 0)
            quarters_here(c, h)
            pass_half(c, h, second_ring(h, 1))
            pass_half(c, h, second_ring(h, 3))
        arrived(gain_up, gain_rsem, gain_ssem)
        for step, o in enumerate((0, 1, 3, 2)):
            @pl.when(s >= 2)
            def _():
                @pl.loop(10 * step, 10 * step + 10)
                def _(i):
                    part = pl.ds(pl.multiple_of(i * 128, 128), 128)
                    scaled = wo[:, part].astype(F32) * gain_up[:, part]
                    wo_t[part, :] = scaled.T.astype(BF16)

            for h in range(2):
                c = on_rings(h, o, 3)
                half_here(c, h)
                pass_quarter(c, h, 0, second_ring(h, 1))
                c = on_rings(h, o, 1)
                half_here(c, h)
                pass_quarter(c, h, 1, second_ring(h, 3))
        for o in (0, 1, 3, 2):
            for h in range(2):
                quarters_here(on_rings(h, o, 2), h)
        for copy in sent:
            copy.wait_send()

        @pl.when(s == 0)
        def _():
            @pl.loop(0, 64)
            def _(i):
                part = pl.ds(pl.multiple_of(i * 16, 16), 16)
                wvf[part, :] = (wvf[part, :].astype(F32) * gain_up[...]).astype(BF16)

    @pl.when(spreads)
    def _():
        transpose_weights()

    @pl.when((s == 4) | (s == 2))
    def _():
        @pl.loop(0, 2)
        def _(i):
            part = pl.ds(pl.multiple_of(i * 512, 512), 512)
            total = jnp.zeros((512, HEADS_HERE * HD), F32)
            for d in range(8):
                cols = slice(d * WIDE, (d + 1) * WIDE)
                total += jnp.dot(wvf[part, cols], wo_t[cols, :], preferred_element_type=F32)
            joint[part, 0 : HEADS_HERE * HD] = total.astype(BF16)

    @pl.when(s == 0)
    def _():
        @pl.loop(0, 8)
        def _(i):
            part = pl.ds(pl.multiple_of(i * 128, 128), 128)
            total = jnp.zeros((128, FEATS), F32)
            for d in range(8):
                cols = slice(d * WIDE, (d + 1) * WIDE)
                total += nt_dot(wvf[part, cols], dec[:, cols])
            joint[part, :] = total.astype(BF16)

    def wait_one_target(first):
        @pl.loop(first, N)
        def _(o):
            p = peer(o)
            arrived(v_recv.at[p, 0], v_rsem.at[p], v_ssem.at[0])

    def wait_values():
        @pl.loop(0, N)
        def _(p):
            arrived(v_recv.at[p], v_rsem.at[p], v_ssem.at[0])

    def value_grad(k):
        pieces = []
        for q in range(8):
            both = v_recv[2 * q, k].astype(F32) + v_recv[2 * q + 1, k].astype(F32)
            pieces.append(both.astype(BF16))
        return jnp.concatenate(pieces, axis=1)

    def v_copy_both(p):
        return remote(v_send, v_recv.at[j], v_ssem.at[p], v_rsem.at[j], below, p)

    def v_copy_one(p):
        return remote(v_send.at[lax.rem(p, 2)], v_recv.at[j, 0], v_ssem.at[p], v_rsem.at[j], below, p)

    def v_copy_here(p):
        return remote(
            v_send.at[lax.rem(p, 2)], v_recv.at[j, 0], v_ssem.at[p], v_rsem.at[j], s, p
        )

    def send_values(head_grad):
        for k in range(2):
            for h in range(HEADS_HERE):
                hcat[h * HD : h * HD + TOK, k * HD : (k + 1) * HD] = head_grad[
                    k * TOK : (k + 1) * TOK, h * HD : (h + 1) * HD
                ]
        part = jnp.dot(pat[...], hcat[...], preferred_element_type=F32)
        for k in range(2):
            v_send[k] = (part[:, k * HD : (k + 1) * HD] * sc_rows[...]).astype(BF16)

        @pl.when(feeds_join)
        def _():
            far_first(lambda p: v_copy_both(p).start())

        @pl.when(feeds_spread)
        def _():
            far_first(lambda p: v_copy_one(p).start())

        @pl.when(second)
        def _():
            far_first_peers(lambda p: v_copy_here(p).start())
            v_recv[j, 0] = v_send[my_k]

    def half_copy(c, h, to, sem):
        part = grad.at[c, pl.ds(48 * h, 48)]
        return remote(part, part, g_ssem.at[sem], g_rsem.at[2 * c + h], s, to)

    def half_arrived(c, h):
        arrived(grad.at[c, pl.ds(48 * h, 48)], g_rsem.at[2 * c + h], g_ssem.at[0])

    own_sends, row_sends, col_sends = [], [], []
    for o in (2, 1, 3):
        own_sends.append((j, 0, at_row(o), o))
        own_sends.append((j, 1, at_col(o), 4 + o))
    for o in (2, 1, 3):
        own_sends.append((j, 0, at_col(o), 8 + o))
        own_sends.append((j, 1, at_row(o), 12 + o))
    for o in (1, 3, 2):
        row_sends.append([(at_row(o), 0, at_col(q), 16 + 4 * o + q) for q in (2, 1, 3)])
        col_sends.append([(at_col(o), 1, at_row(q), 32 + 4 * o + q) for q in (2, 1, 3)])

    own_cols = pl.ds(pl.multiple_of(my_d * WIDE, 128), WIDE)

    def next_chunk(chunk, first):
        wait_one_target(first)
        mixed = jnp.dot(value_grad(0), wvs[...], preferred_element_type=F32)
        return (chunk[...].astype(F32) + mixed * gain_up[:, own_cols]).astype(BF16)

    def make_chunk():
        @pl.when(s == 5)
        def _():
            arrived(grad.at[j], hop_rsem, hop_ssem)

        @pl.when(s < 5)
        def _():
            grad[j] = next_chunk(grad_base, 0)

        for item in own_sends:
            half_copy(*item).start()

    def forward():
        for items in sum(zip(row_sends, col_sends), ()):
            half_arrived(*items[0][:2])
            for item in items:
                half_copy(*item).start()

    def wait_chunk(c):
        @pl.when(c // 4 != row)
        def _():
            half_arrived(c, 0)

        @pl.when(c % 4 != col)
        def _():
            half_arrived(c, 1)

    def whole_copy(d):
        part = grad.at[pl.ds(2 * d, 2)]
        return remote(part, part, copy_ssem.at[d], copy_rsem.at[d], below, j)

    def whole_arrived(d):
        arrived(grad.at[pl.ds(2 * d, 2)], copy_rsem.at[d], copy_ssem.at[0])

    def head_grad_of(at_chunk, dot):
        total = jnp.zeros((2 * TOK, HEADS_HERE * HD), F32)
        for d in range(8):
            at_chunk(d)
            both = grad[2 * d : 2 * d + 2].reshape(2 * TOK, WIDE)
            total += dot(both, slice(d * WIDE, (d + 1) * WIDE))
        return total

    @pl.when((s == 3) | (s == 1))
    def _():
        arrived(gain_up, gain_rsem, gain_ssem)
        own_columns.wait()

        @pl.loop(1, N)
        def _(o):
            p = peer(o)
            rows = pl.ds(pl.multiple_of(p * 64, 64), 64)
            arrived(wvs.at[rows], wv_rsem.at[p], wv_ssem.at[0])

        arrived(grad_base, hop_rsem, hop_ssem)

    @pl.when(spreads)
    def _():
        make_chunk()
        forward()

        def take_chunks(d):
            wait_chunk(2 * d)
            wait_chunk(2 * d + 1)
            whole_copy(d).start()

        send_values(head_grad_of(
            take_chunks,
            lambda both, part: jnp.dot(both, wo_t[part, :], preferred_element_type=F32),
        ).astype(BF16))

    u_forwards = []
    for o in (0, 1, 3, 2):
        u_forwards.append([(at_row(o), 0, at_col(q), 8 + 4 * o + q) for q in (2, 1, 3)])
        u_forwards.append([(at_col(o), 1, at_row(q), 24 + 4 * o + q) for q in (2, 1, 3)])

    def u_half(c, h):
        return u_recv.at[c, :, pl.ds(1280 * h, 1280)]

    def u_forward(c, h, to, sem):
        return remote(u_half(c, h), u_half(c, h), u_ssem.at[sem], u_rsem.at[2 * c + h], s, to)

    @pl.when(second)
    def _():
        straight_columns.start()
        transpose_weights()
        arrived(u_recv.at[N], seed_rsem, seed_ssem)

        @pl.loop(1, N)
        def _(o):
            column_copy(0, o).start()

        for items in u_forwards:
            c, h = items[0][0], items[0][1]
            arrived(u_half(c, h), u_rsem.at[2 * c + h], u_ssem.at[0])
            for item in items:
                u_forward(*item).start()

        @pl.loop(1, N)
        def _(o):
            column_copy(1, o).start()

        @pl.loop(0, N)
        def _(p):
            arrived(mix_recv.at[p], mix_rsem.at[p], mix_ssem.at[0])

        kind = lax.broadcasted_iota(jnp.int32, (TOK, HD), 1) & 15
        for t in range(2):
            tile = jnp.zeros((TOK, HD), F32)
            for q in range(8):
                tile = tile + mix_recv[8 * t + q].astype(F32)
            for h in range(2):
                for k in range(2):
                    keep = (kind >> 2) == 2 * h + k
                    mix[h, k * TOK : (k + 1) * TOK, t * HD : (t + 1) * HD] = jnp.where(
                        keep, tile, 0.0
                    ).astype(BF16)

        @pl.loop(0, N)
        def _(c):
            @pl.when(c // 4 != row)
            def _():
                arrived(u_half(c, 0), u_rsem.at[2 * c], u_ssem.at[0])

            @pl.when(lax.rem(c, 4) != col)
            def _():
                arrived(u_half(c, 1), u_rsem.at[2 * c + 1], u_ssem.at[0])

        half = 2560
        flat = u_recv[...].reshape(16 * (N + 1), half)
        low = jnp.dot(flat, wo_t[0:half, :], preferred_element_type=F32)
        high = jnp.dot(flat, wo_t[half:, :], preferred_element_type=F32)
        total = jnp.dot(mix[0], low[0:256].astype(BF16), preferred_element_type=F32)
        total += jnp.dot(mix[1], high[0:256].astype(BF16), preferred_element_type=F32)
        token = lax.broadcasted_iota(jnp.int32, (TOK, HEADS_HERE * HD), 0)
        parts = []
        for k in range(2):
            one = low[256 + k : 257 + k] + high[264 + k : 265 + k]
            parts.append(
                total[k * TOK : (k + 1) * TOK] + jnp.where(token == tok_ref[k], one, 0.0)
            )
        send_values(jnp.concatenate(parts, axis=0).astype(BF16))
        token = lax.broadcasted_iota(jnp.int32, (TOK, WIDE), 0)
        for d in range(8):
            h, cols = d // 4, slice((d % 4) * WIDE, (d % 4 + 1) * WIDE)
            head_rows = u_recv[0:N, :, cols].reshape(16 * N, WIDE)
            mixed = jnp.dot(mix[h], head_rows, preferred_element_type=F32)
            for k in range(2):
                one = u_recv[N, 8 * h + k : 8 * h + k + 1, cols].astype(F32)
                grad[2 * d + k] = (
                    mixed[k * TOK : (k + 1) * TOK] + jnp.where(token == tok_ref[k], one, 0.0)
                ).astype(BF16)
        own_gain.wait()
        straight_columns.wait()

        @pl.loop(1, N)
        def _(o):
            p = peer(o)
            for h in range(2):
                arrived(half_columns(h, p), wv_rsem.at[N * h + p], wv_ssem.at[0])

        grad_own[...] = next_chunk(grad.at[j], 1)
        last_copy().start()

    @pl.when((s == 4) | (s == 2))
    def _():
        base[...] = head_grad_of(whole_arrived, lambda both, part: nt_dot(both, wo[:, part]))
        wait_values()
        for k in range(2):
            v_full[k * TOK : (k + 1) * TOK, :] = value_grad(k)
        mixed = jnp.dot(
            v_full[pl.ds(pl.multiple_of(my_k * TOK, TOK), TOK), :], wvf[:, own_cols],
            preferred_element_type=F32,
        )
        grad_own[...] = (grad[j].astype(F32) + mixed * gain_up[:, own_cols]).astype(BF16)
        hop_copy(grad_own).start()
        total = base[...] + jnp.dot(
            v_full[...], joint[:, 0 : HEADS_HERE * HD], preferred_element_type=F32
        )
        send_values(total.astype(BF16))
        for d in range(8):
            mixed = jnp.dot(
                v_full[...], wvf[:, d * WIDE : (d + 1) * WIDE], preferred_element_type=F32
            )
            mixed = mixed * gain_up[:, d * WIDE : (d + 1) * WIDE]
            for k in range(2):
                grad[2 * d + k] = (
                    grad[2 * d + k].astype(F32) + mixed[k * TOK : (k + 1) * TOK]
                ).astype(BF16)

    @pl.when(s == 0)
    def _():
        for d in range(8):
            whole_arrived(d)

    for d in range(8):
        both = grad[2 * d : 2 * d + 2].reshape(2 * TOK, WIDE)
        term = nt_dot(both, dec[:, d * WIDE : (d + 1) * WIDE])
        if d == 0:
            acc[...] = term
        else:
            acc[...] += term

    @pl.when(s == 0)
    def _():
        wait_values()
        for k in range(2):
            v_full[k * TOK : (k + 1) * TOK, :] = value_grad(k)
        acc[...] += jnp.dot(v_full[...], joint[...], preferred_element_type=F32)

    local_id = ids_ref[...] - j * FEATS
    lane = local_id & 127
    block = local_id >> 7
    chosen = []
    for k in range(2):
        picked = jnp.zeros((TOK, ACT), F32)
        for b in range(8):
            near = acc[k * TOK : (k + 1) * TOK, b * 128 : (b + 1) * 128]
            got = jnp.take_along_axis(near, lane, axis=1)
            picked = jnp.where(block == b, got, picked)
        chosen.append((picked * vals_ref[...]).astype(BF16))
    terms = jnp.concatenate(chosen, axis=0)
    e_row = lax.broadcasted_iota(jnp.int32, (256, 192), 0)
    e_col = lax.broadcasted_iota(jnp.int32, (256, 192), 1)
    slot = e_row & 7
    source = ((e_row >> 3) & 1) * TOK + (e_row >> 4) * 6 + slot
    placing = jnp.where((e_col == source) & (slot < 6), 1.0, 0.0).astype(BF16)
    placed = jnp.dot(placing, terms, preferred_element_type=F32).astype(BF16)
    for q in range(N):
        ed_send[q] = placed[16 * q : 16 * q + 16, :]

    def ed_copy(p):
        return remote(ed_send.at[p], ed_recv.at[j], ed_ssem.at[p], ed_rsem.at[j], s, p)

    far_first_peers(lambda p: ed_copy(p).start())

    ed_recv[j] = ed_send[j]

    @pl.loop(1, N)
    def _(o):
        p = peer(o)
        arrived(ed_recv.at[p], ed_rsem.at[p], ed_ssem.at[0])

    edges = jnp.zeros((16, ACT), F32)
    for q in range(N):
        edges += ed_recv[q].astype(F32)
    for k in range(2):
        for t in range(6):
            out_ref[t, k : k + 1, :] = edges[8 * k + t : 8 * k + t + 1, :]

    @pl.loop(1, N)
    def _(o):
        ed_copy(peer(o)).wait_send()

    @pl.when(s < TOP)
    def _():
        e1_copy().wait_send()

    @pl.when(s >= 1)
    def _():
        @pl.loop(1, N)
        def _(o):
            sc_copy(o).wait_send()

    @pl.when(s == TOP)
    def _():
        pair_copy(0).wait_send()
        pair_copy(1).wait_send()
        seed_copy().wait_send()
        for o in range(4):
            for h in range(2):
                u_copy(h, o).wait_send()

        @pl.loop(0, N)
        def _(p):
            mix_copy(p).wait_send()

    @pl.when(second)
    def _():
        last_copy().wait_send()
        far_first_peers(lambda p: v_copy_here(p).wait_send())

        @pl.loop(1, N)
        def _(o):
            for h in range(2):
                column_copy(h, o).wait_send()

        for items in u_forwards:
            for item in items:
                u_forward(*item).wait_send()

    @pl.when((s >= 1) & (s < second_index))
    def _():
        gain_copy().wait_send()

        for p in range(N):
            @pl.when(feeds_join)
            def _():
                v_copy_both(p).wait_send()

            @pl.when(feeds_spread)
            def _():
                v_copy_one(p).wait_send()

    @pl.when(feeds_spread)
    def _():
        hop_copy(grad_own).wait_send()
        stage_copy().wait_send()

    @pl.when(feeds_join)
    def _():
        for o in (0, 1, 3):
            for h in range(2):
                full_copy(h, o).wait_send()
        for d in range(8):
            whole_copy(d).wait_send()

    @pl.when((s == 3) | (s == 1))
    def _():
        @pl.loop(1, N)
        def _(o):
            wv_copy(o).wait_send()

    @pl.when(spreads)
    def _():
        for item in own_sends + sum(row_sends, []) + sum(col_sends, []):
            half_copy(*item).wait_send()


def body(
    attn_logits, out_weight, value_weight, norm_gain, norm_scale, target_encoder,
    target_ids, target_token, decoder, source_ids, source_values,
):
    vmem = pl.BlockSpec(memory_space=pltpu.VMEM)
    hbm = pl.BlockSpec(memory_space=pltpu.HBM)
    dma = pltpu.SemaphoreType.DMA
    out = pl.pallas_call(
        chain_kernel,
        out_shape=jax.ShapeDtypeStruct((6, 2, ACT), F32),
        in_specs=[hbm] * 11,
        out_specs=vmem,
        scratch_shapes=[
            pltpu.VMEM((40, 16384), BF16),
            pltpu.VMEM((1, 6), F32),
            pltpu.VMEM((HEADS_HERE, TOK, TOK), BF16),
            pltpu.VMEM((1, 5120), F32),
            pltpu.SMEM((2,), jnp.int32),
            pltpu.SMEM((2,), jnp.int32),
            pltpu.VMEM((TOK, ACT), jnp.int32),
            pltpu.VMEM((TOK, ACT), F32),
            pltpu.VMEM((8, 256), F32),
            pltpu.VMEM((8, 128), F32),
            pltpu.VMEM((512, 5120), BF16),
            pltpu.VMEM((5120, 512), BF16),
            pltpu.VMEM((FEATS, 5120), BF16),
            pltpu.VMEM((1024, WIDE), BF16),
            pltpu.VMEM((1024, 5120), BF16),
            pltpu.VMEM((1024, FEATS), BF16),
            pltpu.VMEM((N, TOK, WIDE), BF16),
            pltpu.VMEM((TOK, WIDE), BF16),
            pltpu.VMEM((TOK, WIDE), BF16),
            pltpu.VMEM((2, TOK, HD), BF16),
            pltpu.VMEM((N, 2, TOK, HD), BF16),
            pltpu.VMEM((2 * TOK, 1024), BF16),
            pltpu.VMEM((2 * TOK, HEADS_HERE * HD), F32),
            pltpu.VMEM((N, 8, 128), F32),
            pltpu.VMEM((TOK, 128), F32),
            pltpu.VMEM((8, 8, 256), F32),
            pltpu.VMEM((16, 256), BF16),
            pltpu.VMEM((N, 16, 256), BF16),
            pltpu.VMEM((TOK, HEADS_HERE * HD), BF16),
            pltpu.VMEM((HEADS_HERE * HD, 2 * HD), BF16),
            pltpu.VMEM((128, 128), F32),
            pltpu.VMEM((2 * TOK, FEATS), F32),
            pltpu.VMEM((N, 16, ACT), BF16),
            pltpu.VMEM((N, 16, ACT), BF16),
            dma((12,)),
            dma, dma,
            dma((2 * N,)), dma((2 * N,)),
            dma((3 * N,)), dma((4 * N,)),
            dma((N,)), dma((N,)),
            dma, dma((8,)),
            dma((N,)), dma((N,)),
            dma((N,)), dma((N,)),
            dma((3 * N,)), dma((2 * N,)),
            dma, dma,
            dma((8,)), dma((8,)),
            dma((N,)), dma((N,)),
            pltpu.VMEM((16, 2560), BF16),
            pltpu.VMEM((16, 2560), F32),
            pltpu.VMEM((16, 2560), BF16),
            pltpu.VMEM((N + 1, 16, 2560), BF16),
            pltpu.VMEM((TOK, HD), BF16),
            pltpu.VMEM((N, TOK, HD), BF16),
            pltpu.VMEM((2, 2 * TOK, 2 * HD), BF16),
            pltpu.VMEM((64, 5120), BF16),
            dma, dma,
            dma((2,)), dma((2,)),
            dma((40,)), dma((2 * N,)),
            dma((N,)), dma((N,)),
            dma, dma,
        ],
        compiler_params=pltpu.CompilerParams(
            collective_id=0, has_side_effects=True, vmem_limit_bytes=63 * 2**20
        ),
        name="chain",
    )(
        target_encoder.T, norm_scale, attn_logits[0], norm_gain, target_ids, target_token,
        source_ids[0], source_values[0],
        out_weight[0], value_weight[0], decoder[0],
    )
    return out[None]


def solution(mesh):
    return jax.shard_map(
        body,
        mesh=mesh,
        in_specs=(
            P("section", "tensor", None, None),
            P("section", "tensor", None),
            P("section", "tensor", None),
            P("section", None),
            P("section", "tensor"),
            P(None, ("section", "tensor")),
            P(),
            P(),
            P("section", "tensor", None),
            P("section", None, None),
            P("section", None, None),
        ),
        out_specs=P("section", "tensor", None, None),
        check_vma=False,
    )
```
